32 devices in a mesh: dp: 8 (over z, y), head: 4 (over x, core).
Axes of the slice: x: 2, y: 2, z: 4, core: 2. Of those that a mesh axis runs over, the one named last changes fastest.
Arguments:
- state_in: bfloat16 [20480, 512], P(('dp', 'head')), may hold values from -12 to 12
- qkv_weight: bfloat16 [3, 512, 512], P(None, 'dp', 'head'), may hold values from -0.1875 to 0.1875
- out_weight: bfloat16 [512, 512], P('dp', 'head'), may hold values from -2 to 2
- ffn_in_weight: bfloat16 [512, 2048], P('dp', 'head'), may hold values from -0.25 to 0.25
- ffn_out_weight: bfloat16 [512, 2048], P('dp', 'head'), may hold values from -0.125 to 0.125
- ffn_in_bias: float32 [2048], replicated, may hold values from -3 to 3
- ffn_out_bias: float32 [512], replicated, may hold values from -3 to 3
- norm1_gain: float32 [512], replicated, may hold values from 0.5 to 1.5
- norm1_shift: float32 [512], replicated, may hold values from -3 to 3
- norm2_gain: float32 [512], replicated, may hold values from 0.5 to 1.5
- norm2_shift: float32 [512], replicated, may hold values from -3 to 3
- halt_weight: float32 [512], replicated, may hold values from -0.25 to 0.25
- halt_bias: float32 [1], replicated, may hold values from -3 to 3
- seg_ids: int32 [8, 2560], P('dp'), may hold values from 0 to 1, as said below
- halt_mask: int32 [20480], P(('dp', 'head')), may hold values from 0 to 1, as said below
- cotangent: bfloat16 [20480, 512], P(('dp', 'head')), may hold values from -22 to 22
Outputs:
- new_state: bfloat16 [20480, 512], P(('dp', 'head'))
- grad_state: float32 [20480, 512], P(('dp', 'head'))
- grad_qkv_weight: float32 [3, 512, 512], P(None, 'dp', 'head')
- grad_out_weight: float32 [512, 512], P('dp', 'head')
- grad_ffn_in_weight: float32 [512, 2048], P('dp', 'head')
- grad_ffn_out_weight: float32 [512, 2048], P('dp', 'head')
- grad_ffn_in_bias: float32 [2048], replicated
- grad_ffn_out_bias: float32 [512], replicated
- grad_norm1_gain: float32 [512], replicated
- grad_norm1_shift: float32 [512], replicated
- grad_norm2_gain: float32 [512], replicated
- grad_norm2_shift: float32 [512], replicated
- grad_halt_weight: float32 [512], replicated
- grad_halt_bias: float32 [1], replicated
The draws below stay inside these ranges and needn't reach their ends.
Inputs may be any that keep to these rules, and one draw needn't show every extreme that they name: `seg_ids`: row g holds the two sequences of group g in order: 0 on its first s tokens and 1 on the others, where s lies between 1024 and 1536. `halt_mask`: 1 where a token still updates its state, 0 where it has halted; the share of 1s differs between groups of 2560 tokens.
All inputs are finite; a program needn't handle non-finite values.
Results may differ from the reference program's by a relative error of at most 0.015.
The reference program's roundings to bfloat16 on the way count: a program that leaves them out, or rounds other values in their place, can miss the bound.
Values may be sent and summed in bfloat16 or wider, within the bound.
No kernel may reach another device: no remote copies, remote signals or barrier semaphores. Data moves between devices by JAX's collectives and lax.ppermute only.
A program may use at most 128 MiB of HBM per device.

```python
import math
import jax
import jax.numpy as jnp
from jax import lax

D = 512
HEADS = 8
HEAD_SIZE = 64
FF = 2048
TOK_DEV = 2560
SEQ_MIN = 1024
BLOCK = 512
STEP = 2
TOKENS = 20480
GROUPS = 8


def draw_state_in(key, part):
    key = jax.random.fold_in(key, 11)
    col_key = jax.random.fold_in(key, 0)
    entry_key = jax.random.fold_in(key, 2)
    column_scale = jnp.exp(jax.random.uniform(col_key, (D,), jnp.float32, math.log(0.3), math.log(3.0)))
    entries = jnp.clip(jax.random.normal(entry_key, (TOKENS, D), jnp.float32), -4.0, 4.0)
    return (entries * column_scale[None, :]).astype(jnp.bfloat16)


def draw_seg_ids(key, part):
    key = jax.random.fold_in(key, 12)
    split_at = jax.random.randint(key, (GROUPS, 1), SEQ_MIN, TOK_DEV - SEQ_MIN + 1)
    places = jnp.arange(TOK_DEV, dtype=jnp.int32)[None, :]
    return (places >= split_at).astype(jnp.int32)


def draw_halt_mask(key, part):
    key = jax.random.fold_in(key, 13)
    share_key, entry_key = jax.random.split(key)
    share = jax.random.randint(share_key, (GROUPS, 1), 300, 1000)
    tickets = jax.random.randint(entry_key, (GROUPS, TOK_DEV), 0, 1000)
    return (tickets < share).astype(jnp.int32).reshape(TOKENS)


def draw_cotangent(key, part):
    key = jax.random.fold_in(key, 14)
    entry_key, pair_key = jax.random.split(key)
    row_place = jnp.arange(TOKENS, dtype=jnp.float32)[:, None] / (TOKENS - 1)
    entries = jnp.clip(jax.random.normal(entry_key, (TOKENS, D), jnp.float32), -4.0, 4.0)
    rising = 0.6 * jnp.exp(row_place * math.log(3.0))
    paired = jax.random.permutation(pair_key, GROUPS)
    row_group = jnp.arange(TOKENS, dtype=jnp.int32) // TOK_DEV
    col_block = jnp.arange(D, dtype=jnp.int32) // (D // GROUPS)
    boost = jnp.where(paired[row_group][:, None] == col_block[None, :], 3.0, 1.0)
    return (entries * rising * boost).astype(jnp.bfloat16)


def level_of(stream_key, extent, pieces, least, top_value):
    gain, own = 1.0, jax.random.fold_in(stream_key, 6)
    for position, shards_of in pieces:
        heights = jnp.exp(jax.random.uniform(jax.random.fold_in(own, position), (shards_of,), jnp.float32, least / len(pieces), top_value / len(pieces)))
        gain = gain * jnp.repeat(heights, extent[position] // shards_of).reshape([-1 if axis == position else 1 for axis in range(len(extent))])
    return gain


def noise(own_key, shape, width, bound, cuts=(), held_as=jnp.bfloat16):
    factor_of = level_of(own_key, shape, cuts, -0.22, 0.18) if cuts else 1.0
    array = jax.random.normal(own_key, shape, jnp.float32) * width * factor_of
    return jnp.minimum(jnp.maximum(array, -bound), bound).astype(held_as)


def setup_inputs(seed: int = 0) -> dict:
    seeds = jax.random.split(jax.random.key(seed), 17)
    state_in = draw_state_in(jax.random.fold_in(seeds[16], 71), 0)
    qkv_weight = noise(seeds[1], (3, D, D), (2 * D) ** -0.5, 0.1875, ((1, 8), (2, 4)))
    out_weight = noise(seeds[2], (D, D), (max(4, D // 64)) ** -0.5, 2.0, ((0, 8), (1, 4)))
    ffn_in_weight = noise(seeds[3], (D, FF), D ** -0.5, 0.25, ((0, 8), (1, 4)))
    ffn_out_weight = noise(seeds[4], (D, FF), FF ** -0.5, 0.125, ((0, 8), (1, 4)))
    ffn_in_bias = noise(seeds[5], (FF,), 0.5, 3.0, (), jnp.float32)
    ffn_out_bias = noise(seeds[6], (D,), 0.5, 3.0, (), jnp.float32)
    norm1_gain = jnp.clip(1.0 + 0.1 * jax.random.normal(seeds[7], (D,), jnp.float32), 0.5, 1.5)
    norm1_shift = noise(seeds[8], (D,), 0.5, 3.0, (), jnp.float32)
    norm2_gain = jnp.clip(1.0 + 0.1 * jax.random.normal(seeds[9], (D,), jnp.float32), 0.5, 1.5)
    norm2_shift = noise(seeds[10], (D,), 0.5, 3.0, (), jnp.float32)
    halt_weight = noise(seeds[11], (D,), D ** -0.5, 0.25, (), jnp.float32)
    halt_bias = noise(seeds[12], (1,), 1.0, 3.0, (), jnp.float32)
    seg_ids = draw_seg_ids(jax.random.fold_in(seeds[16], 71), 0)
    halt_mask = draw_halt_mask(jax.random.fold_in(seeds[16], 71), 0)
    cotangent = draw_cotangent(jax.random.fold_in(seeds[16], 71), 0)
    return dict(state_in=state_in, qkv_weight=qkv_weight, out_weight=out_weight, ffn_in_weight=ffn_in_weight, ffn_out_weight=ffn_out_weight, ffn_in_bias=ffn_in_bias, ffn_out_bias=ffn_out_bias, norm1_gain=norm1_gain, norm1_shift=norm1_shift, norm2_gain=norm2_gain, norm2_shift=norm2_shift, halt_weight=halt_weight, halt_bias=halt_bias, seg_ids=seg_ids, halt_mask=halt_mask, cotangent=cotangent)


highest = lax.Precision.HIGHEST
norm_epsilon = 1e-06
masked_score = -1e+30

@jax.custom_vjp
def low(v):
    return lax.optimization_barrier(v.astype(jnp.bfloat16)).astype(jnp.float32)

@jax.custom_vjp
def low_back(v):
    return v

def low_keep(v):
    return (low(v), None)

def low_pass(kept, grad):
    return (grad,)

def back_keep(v):
    return (v, None)

def back_low(kept, grad):
    return (low(grad),)
low.defvjp(low_keep, low_pass)
low_back.defvjp(back_keep, back_low)

def signal_table(places, feature_width):
    half_width = feature_width // 2
    inverse_rates = jnp.exp(jnp.arange(half_width, dtype=jnp.float32) * (-math.log(10000.0) / (half_width - 1)))
    angles = places.astype(jnp.float32)[:, None] * inverse_rates[None, :]
    return jnp.concatenate([jnp.sin(angles), jnp.cos(angles)], axis=1)

def positions(seg_row):
    places = jnp.arange(seg_row.shape[0], dtype=jnp.int32)
    starts = jnp.concatenate([jnp.ones((1,), jnp.bool_), seg_row[1:] != seg_row[:-1]])
    first_index = lax.cummax(jnp.where(starts, places, 0), axis=0)
    return places - first_index

def layer_norm(summed, norm_gain, norm_shift):
    center = summed - lax.optimization_barrier(jnp.mean(summed, axis=-1, keepdims=True))
    spread = lax.optimization_barrier(jnp.mean(center * center, axis=-1, keepdims=True))
    return center * lax.rsqrt(spread + norm_epsilon) * norm_gain + norm_shift

def group_step(weight_set, state_rows, seg_row, running):
    qkv_weight, out_weight, ffn_in_weight, ffn_out_weight, ffn_in_bias, ffn_out_bias, norm1_gain, norm1_shift, norm2_gain, norm2_shift, halt_weight, halt_bias = weight_set
    width_all = state_rows.shape[1]
    places = positions(seg_row)
    embedded = state_rows + signal_table(places, width_all) + signal_table(jnp.full((1,), STEP, jnp.int32), width_all)
    hidden = low(embedded)
    projected = [low(low_back(jnp.dot(hidden, qkv_weight[member], precision=highest))) for member in range(3)]
    queries = projected[0].reshape(TOK_DEV // BLOCK, BLOCK, HEADS, HEAD_SIZE)
    keys_all = projected[1].reshape(TOK_DEV, HEADS, HEAD_SIZE)
    values_all = projected[2].reshape(TOK_DEV, HEADS, HEAD_SIZE)
    seg_blocks = seg_row.reshape(TOK_DEV // BLOCK, BLOCK)
    score_scale = 1.0 / math.sqrt(HEAD_SIZE)

    def attend(inputs):
        query_block, seg_block = inputs
        scores = low_back(jnp.einsum('bhe,khe->hbk', query_block, keys_all, precision=highest) * score_scale)
        same_seq = (seg_block[:, None] == seg_row[None, :])[None]
        scores = jnp.where(same_seq, scores, masked_score)
        probs_low = low(jax.nn.softmax(scores, axis=-1))
        return jnp.einsum('hbk,khe->bhe', probs_low, values_all, precision=highest)
    mixed_heads = lax.map(jax.checkpoint(attend), (queries, seg_blocks)).reshape(TOK_DEV, HEADS * HEAD_SIZE)
    mixed_heads = low(low_back(mixed_heads))
    branch = low_back(jnp.dot(mixed_heads, out_weight.T, precision=highest))
    first_rows = layer_norm(embedded + branch, norm1_gain, norm1_shift)
    inner_sum = low_back(jnp.dot(low(first_rows), ffn_in_weight, precision=highest) + ffn_in_bias)
    active = low(jax.nn.gelu(inner_sum))
    outward = low_back(jnp.dot(active, ffn_out_weight.T, precision=highest)) + ffn_out_bias
    second = layer_norm(first_rows + outward, norm2_gain, norm2_shift)
    halting = jax.nn.sigmoid(jnp.dot(second, halt_weight, precision=highest) + halt_bias[0])
    return state_rows + (running * halting)[:, None] * (second - state_rows)

def reference(state_in, qkv_weight, out_weight, ffn_in_weight, ffn_out_weight, ffn_in_bias, ffn_out_bias, norm1_gain, norm1_shift, norm2_gain, norm2_shift, halt_weight, halt_bias, seg_ids, halt_mask, cotangent):
    weight_set = tuple((member.astype(jnp.float32) for member in (qkv_weight, out_weight, ffn_in_weight, ffn_out_weight, ffn_in_bias, ffn_out_bias, norm1_gain, norm1_shift, norm2_gain, norm2_shift, halt_weight, halt_bias)))
    rows_all = state_in.astype(jnp.float32).reshape(GROUPS, TOK_DEV, D)
    running_all = halt_mask.astype(jnp.float32).reshape(GROUPS, TOK_DEV)

    def forward(weights_in, rows_in):

        def per_group(carried, inputs):
            state_rows, seg_row, running = inputs
            return (carried, group_step(weights_in, state_rows, seg_row, running))
        _, results = lax.scan(jax.checkpoint(per_group), jnp.zeros((), jnp.float32), (rows_in, seg_ids, running_all))
        return results
    updated, pullback = jax.vjp(forward, weight_set, rows_all)
    grad_weights, grad_rows = pullback(cotangent.astype(jnp.float32).reshape(GROUPS, TOK_DEV, D))
    return (updated.reshape(TOKENS, D).astype(jnp.bfloat16), grad_rows.reshape(TOKENS, D), grad_weights[0], grad_weights[1], grad_weights[2], grad_weights[3], grad_weights[4], grad_weights[5], grad_weights[6], grad_weights[7], grad_weights[8], grad_weights[9], grad_weights[10], grad_weights[11])
```

```python
import functools
import math

import jax
import jax.numpy as jnp
from jax import lax
from jax.experimental import pallas as pl
from jax.experimental.pallas import tpu as pltpu
from jax.sharding import PartitionSpec as P

HEAD_SIZE = 64
STEP = 2
SEQ_MIN = 1024
LANES = 128
UNIT = 64

norm_epsilon = 1e-06
masked_score = -1e30
log2e = 1.4426950408889634

f32 = jnp.float32
bf16 = jnp.bfloat16
NT = (((1,), (1,)), ((), ()))
NN = (((1,), (0,)), ((), ()))
TN = (((0,), (0,)), ((), ()))

CORE = [(0, 1), (1, 0), (2, 3), (3, 2)]
ACROSS = [(0, 2), (2, 0), (1, 3), (3, 1)]
EDGE_OUT = [(2, 0), (1, 3)]
EDGE_BACK = [(0, 2), (3, 1)]
EDGE_SWAP = [(1, 2), (2, 1)]

X, Y, Z0, Z1 = 2, 4, 8, 16
ORDERS = ((Z1, Z0, Y, X), (Z1, Y, X, Z0))

vmem = pl.BlockSpec(memory_space=pltpu.VMEM)
smem = pl.BlockSpec(memory_space=pltpu.SMEM)


def mm(a, b, dims=NN):
    return lax.dot_general(a, b, dims, preferred_element_type=f32)


def call(kernel, name, outs, ins, scratch=(), flops=0, moved=0, limit=56):
    return pl.pallas_call(
        kernel,
        name=name,
        out_shape=[jax.ShapeDtypeStruct(s, t) for s, t in outs],
        in_specs=[smem] + [vmem] * (len(ins) - 1),
        out_specs=[vmem] * len(outs),
        scratch_shapes=[pltpu.VMEM(s, t) for s, t in scratch],
        compiler_params=pltpu.CompilerParams(vmem_limit_bytes=limit << 20),
        cost_estimate=pl.CostEstimate(flops=flops, bytes_accessed=moved, transcendentals=0),
    )(*ins)


def send(array, bits):
    count = 4 * lax.axis_size("dp")
    pairs = [(i, i ^ bits[i & 1]) for i in range(count)]
    return lax.ppermute(array, ("dp", "head"), pairs)


def owner(unit, core):
    found = []
    for order in ORDERS:
        over_dp, over_x = 0, 0
        for place, bit in enumerate(order):
            flag = (unit >> place) & 1
            if bit == X:
                over_x = flag
            else:
                over_dp = over_dp + flag * (bit >> 2)
        found.append((over_dp, over_x))
    return (
        jnp.where(core == 0, found[0][0], found[1][0]),
        jnp.where(core == 0, found[0][1], found[1][1]),
    )


def unit_of(number, core):
    found = [0, 0]
    for k, order in enumerate(ORDERS):
        for place, bit in enumerate(order):
            found[k] = found[k] + ((number // bit) & 1) * (1 << place)
    return jnp.where(core == 0, found[0], found[1])


def qkv_owner(unit):
    return ((unit >> 3) & 1) + ((unit >> 1) & 1) * 2 + (unit & 1) * 4, (unit >> 2) & 1


def window_valid(sc, first, shape):
    split, head, x, local = sc[0], sc[1], sc[2], sc[5]
    row = lax.broadcasted_iota(jnp.int32, shape, 0) + first
    token = jnp.where(
        row < local,
        head * local + row,
        jnp.where(
            row < 2 * local,
            (head ^ 1) * local + row - local,
            row + jnp.where(x == 0, 0, SEQ_MIN - 2 * local),
        ),
    )
    return jnp.where(token < split, 0, 1) == x


def three_parts(value, lane, at):
    high = value.astype(bf16).astype(f32)
    rest = value - high
    middle = rest.astype(bf16).astype(f32)
    low = rest - middle
    return jnp.where(
        lane == at, high, jnp.where(lane == at + 1, middle, jnp.where(lane == at + 2, low, 0.0))
    )


def lanes_of(shape):
    return lax.broadcasted_iota(jnp.int32, shape, 1)


def embed_kernel(sc, state, rates, constant, running, embedded, hidden, edge, run):
    local = state.shape[0]
    half = rates.shape[1]
    token = lax.broadcasted_iota(jnp.int32, (local, half), 0) + sc[1] * local
    place = token - jnp.where(token < sc[0], 0, sc[0])
    angles = place.astype(f32) * rates[...]
    for side, value in ((0, jnp.sin(angles)), (1, jnp.cos(angles))):
        to = slice(side * half, (side + 1) * half)
        embedded[:, to] = state[:, to].astype(f32) + value + constant[:, to]
    hidden[...] = embedded[...].astype(bf16)
    at = pl.multiple_of(jnp.where(sc[2] == 0, local - edge.shape[0], 0), 128)
    edge[...] = embedded[pl.ds(at, edge.shape[0]), :].astype(bf16)
    run[...] = jnp.broadcast_to(running[...].astype(f32), run.shape)


def attend_rows(rows, tall, qf, kb, vb, emit):
    lane = lanes_of((tall, LANES))
    results = []
    for j in range(4):
        query = qf[j, rows, :]
        scores = mm(query, kb[j], NT)
        peak = jnp.max(scores, axis=1, keepdims=True)
        weights = jnp.exp2((scores - peak) * log2e).astype(bf16)
        summed = mm(weights, vb[j])
        total = jnp.sum(jnp.where(lane == 64, summed, 0.0), axis=1, keepdims=True)
        log_total = jnp.broadcast_to(peak + jnp.log(total), (tall, LANES))
        parts = three_parts(-log_total, lane, 64)
        kept = jnp.where((lane < 64) | (lane == 67), query.astype(f32), parts).astype(bf16)
        results.append(summed / total)
        if j % 2:
            both = jnp.where(lane < 64, results[j - 1], pltpu.roll(results[j], 64, 1))
            emit(j, kept, both)
        else:
            emit(j, kept, None)


def front_kernel(
    sc,
    own,
    sib,
    edge,
    unit0,
    unit1,
    unit2,
    unit3,
    qf_own,
    kb,
    vb,
    weight,
    qb_far,
    mixed32,
    mix_sib,
    mix_edge,
    qf_far,
):
    x, dp = sc[2], sc[4]
    for place, held in enumerate((unit0, unit1, unit2, unit3)):
        for sub in range(held.shape[0]):
            over_dp, over_x = qkv_owner(place * 4 + sub)
            row = pl.multiple_of((dp ^ over_dp) * UNIT, UNIT)
            for m in range(3):
                column = pl.multiple_of(m * 256 + (x ^ over_x) * LANES, LANES)
                weight[pl.ds(row, UNIT), pl.ds(column, LANES)] = held[sub, m]
    local = own.shape[0]
    for source, base in ((own, 0), (sib, local), (edge, 2 * local)):
        tall = 256 if source is edge else 320
        lane = lanes_of((tall, LANES))
        ones = jnp.where((lane >= 64) & (lane < 67), 1.0, 0.0).astype(f32)
        mask_lane = lane == 67

        def rows(index, carry, source=source, base=base, tall=tall):
            start = pl.multiple_of(index * tall, 64)
            out = pl.multiple_of(base + index * tall, 64)
            projected = mm(source[pl.ds(start, tall), :], weight[...])
            valid = window_valid(sc, out, (tall, LANES))
            key_tail = jnp.where(mask_lane & jnp.logical_not(valid), masked_score, ones)
            for j in range(4):
                blocks = []
                for m in range(3):
                    at = m * 256 + (j // 2) * LANES
                    block = projected[:, at : at + LANES]
                    if j % 2:
                        block = pltpu.roll(block, 64, 1)
                    blocks.append(block)
                query = jnp.where(
                    lane < 64, blocks[0] * 0.125, jnp.where(mask_lane, 1.0, 0.0)
                ).astype(bf16)
                if source is own:
                    qf_own[j, pl.ds(out, tall), :] = query
                else:
                    qf_far[j, pl.ds(pl.multiple_of(out - local, 64), tall), :] = query
                kb[j, pl.ds(out, tall), :] = jnp.where(lane < 64, blocks[1], key_tail).astype(bf16)
                vb[j, pl.ds(out, tall), :] = jnp.where(lane < 64, blocks[2], ones).astype(bf16)
            return carry

        lax.fori_loop(0, source.shape[0] // tall, rows, 0)

    for base, target, tall in ((0, mix_sib, local), (local, mix_edge, mix_edge.shape[0])):

        def block(index, carry, base=base, target=target, tall=tall):
            start = pl.multiple_of(index * tall, 64)
            at = pl.ds(pl.multiple_of(base + index * tall, 64), tall)

            def emit(j, kept, both):
                qb_far[j, at, :] = kept
                if both is not None:
                    to = slice((j // 2) * LANES, (j // 2 + 1) * LANES)
                    mixed32[at, to] = both
                    target[pl.ds(start, tall), to] = both.astype(bf16)

            attend_rows(at, tall, qf_far, kb, vb, emit)
            return carry

        lax.fori_loop(0, target.shape[0] // tall, block, 0)


def attend_own_kernel(sc, qf, kb, vb, qb, mixed32, mixed):
    tall = mixed.shape[0]

    def block(index, carry):
        at = pl.ds(pl.multiple_of(index * tall, 64), tall)

        def emit(j, kept, both):
            qb[j, at, :] = kept
            if both is not None:
                to = slice((j // 2) * LANES, (j // 2 + 1) * LANES)
                mixed32[at, to] = both
                mixed[at, to] = both.astype(bf16)

        attend_rows(at, tall, qf, kb, vb, emit)
        return carry

    lax.fori_loop(0, mixed.shape[0] // tall, block, 0)


def back_rows(sc, first, tall, qb, qrows, kb, vb, grads, mixed32, mrows, keys_t, values_t, emit):
    lane = lanes_of((tall, LANES))
    valid = window_valid(sc, first, (tall, LANES))
    for p in range(2):
        to = slice(p * LANES, (p + 1) * LANES)
        incoming = jnp.where(valid, grads(to).astype(f32), 0.0)
        product = incoming * mixed32[mrows, to]
        grad_queries = []
        for k in range(2):
            j = 2 * p + k
            half = (lane < 64) if k == 0 else (lane >= 64)
            delta = jnp.sum(jnp.where(half, product, 0.0), axis=1, keepdims=True)
            parts = three_parts(jnp.broadcast_to(-delta, (tall, LANES)), lane, 64)
            shifted = incoming if k == 0 else pltpu.roll(incoming, 64, 1)
            arriving = jnp.where(lane < 64, shifted, parts)
            query = qb[j, qrows, :]
            probs = jnp.exp2(mm(query, kb[j], NT) * log2e)
            grad_probs = mm(arriving.astype(bf16), vb[j], NT)
            grad_scores = (probs * grad_probs).astype(bf16)
            arriving_t = jnp.transpose(arriving)[0:64, :].astype(bf16)
            query_t = jnp.transpose(query.astype(f32))[0:64, :].astype(bf16)
            values_t[j] += mm(arriving_t, probs.astype(bf16))
            keys_t[j] += mm(query_t, grad_scores)
            grad_queries.append(mm(grad_scores, kb[j]) * 0.125)
        emit(
            p,
            jnp.where(lane < 64, grad_queries[0], pltpu.roll(grad_queries[1], 64, 1)).astype(bf16),
        )


def back_own_kernel(sc, qb, kb, vb, mixed32, grad, out, keys_t, values_t):
    keys_t[...] = jnp.zeros_like(keys_t)
    values_t[...] = jnp.zeros_like(values_t)
    tall = out.shape[0]

    def block(index, carry):
        start = pl.multiple_of(index * tall, 128)
        at = pl.ds(start, tall)

        def emit(p, value):
            out[at, p * LANES : (p + 1) * LANES] = value

        back_rows(
            sc, start, tall, qb, at, kb, vb, lambda to: grad[at, to], mixed32, at, keys_t, values_t, emit
        )
        return carry

    lax.fori_loop(0, out.shape[0] // tall, block, 0)


def back_far_kernel(sc, qb, kb, vb, mixed32, grad, keys_in, values_in, out, keys_t, values_t):
    keys_t[...] = keys_in[...]
    values_t[...] = values_in[...]
    local = out.shape[0]
    tall = local

    def block(index, carry):
        start = pl.multiple_of(index * tall, 128)
        at = pl.ds(start, tall)

        def emit(p, value):
            out[at, p * LANES : (p + 1) * LANES] = value

        back_rows(
            sc,
            start + local,
            tall,
            qb,
            at,
            kb,
            vb,
            lambda to: grad[at, to],
            mixed32,
            at,
            keys_t,
            values_t,
            emit,
        )
        return carry

    lax.fori_loop(0, local // tall, block, 0)


def back_edge_kernel(
    sc,
    qb,
    kb,
    vb,
    mixed32,
    grad,
    keys_in,
    values_in,
    dq_own,
    dq_sib,
    own,
    sib,
    edge,
    out,
    unit0,
    unit1,
    unit2,
    unit3,
    keys_t,
    values_t,
    full,
):
    x, dp = sc[2], sc[4]
    local = own.shape[0]
    edge_rows = edge.shape[0]
    keys_t[...] = keys_in[...]
    values_t[...] = values_in[...]
    out[0:local, 0:256] = dq_own[...]
    out[local : 2 * local, 0:256] = dq_sib[...]
    tall = edge_rows

    def block(index, carry):
        start = pl.multiple_of(index * tall, 128)
        at = pl.ds(start, tall)
        far = pl.ds(pl.multiple_of(local + index * tall, 128), tall)
        to_rows = pl.ds(pl.multiple_of(2 * local + index * tall, 128), tall)

        def emit(p, value):
            out[to_rows, p * LANES : (p + 1) * LANES] = value

        back_rows(
            sc,
            start + 2 * local,
            tall,
            qb,
            far,
            kb,
            vb,
            lambda to: grad[at, to],
            mixed32,
            far,
            keys_t,
            values_t,
            emit,
        )
        return carry

    lax.fori_loop(0, edge_rows // tall, block, 0)
    for m, held in ((1, keys_t), (2, values_t)):
        for p in range(2):
            pair = jnp.concatenate([held[2 * p], held[2 * p + 1]], axis=0)
            to = slice(m * 256 + p * LANES, m * 256 + (p + 1) * LANES)
            out[:, to] = jnp.transpose(pair).astype(bf16)
    for m in range(3):
        to = slice(m * 256, (m + 1) * 256)
        total = 0.0
        for source, base in ((own, 0), (sib, local), (edge, 2 * local)):
            total += mm(source[...], out[base : base + source.shape[0], to], TN)
        full[:, to] = total.astype(bf16)
    for place, target in enumerate((unit0, unit1, unit2, unit3)):
        for sub in range(target.shape[0]):
            over_dp, over_x = qkv_owner(place * 4 + sub)
            row = pl.multiple_of((dp ^ over_dp) * UNIT, UNIT)
            for m in range(3):
                column = pl.multiple_of(m * 256 + (x ^ over_x) * LANES, LANES)
                target[sub, m] = full[pl.ds(row, UNIT), pl.ds(column, LANES)]


def norm_parts(rows):
    width = rows.shape[1]
    center = rows - jnp.sum(rows, axis=1, keepdims=True) * (1.0 / width)
    spread = jnp.sum(center * center, axis=1, keepdims=True) * (1.0 / width)
    scale = lax.rsqrt(spread + norm_epsilon)
    return center * scale, scale


def norm_back(normed, scale, gain, incoming):
    width = normed.shape[1]
    e = incoming * gain
    mean_e = jnp.sum(e, axis=1, keepdims=True) * (1.0 / width)
    mean_en = jnp.sum(e * normed, axis=1, keepdims=True) * (1.0 / width)
    return (e - mean_e - normed * mean_en) * scale


def middle_kernel(
    sc,
    embedded,
    state,
    cotangent,
    running,
    mix_own,
    mix_sib,
    edge_own,
    edge_sib,
    own_a,
    own_b,
    sib_a,
    sib_b,
    vectors,
    bias_in,
    new_state,
    base,
    grad_own,
    grad_sib,
    edge_for_own,
    edge_for_sib,
    sum_own,
    sum_sib,
    mixed,
    first_low,
    active,
    grad_out_low,
    grad_inner,
    grad_branch,
    sums,
    w_out,
    w_in,
    w_back,
    slope,
):
    head, x, c, dp = sc[1], sc[2], sc[3], sc[4]
    hidden = w_in.shape[1]
    width = w_out.shape[0]
    hidden_block = hidden // 4
    units = 16

    def unit_place(unit, core):
        over_dp, over_x = owner(unit, core)
        rows = pl.ds(pl.multiple_of((dp ^ over_dp) * UNIT, UNIT), UNIT)
        block = (x ^ over_x) * 2 + core
        narrow = pl.ds(pl.multiple_of(block * LANES, LANES), LANES)
        wide = pl.ds(pl.multiple_of(block * hidden_block, hidden_block), hidden_block)
        return rows, narrow, wide

    for held, first_unit, core in (
        (own_a, 0, c),
        (own_b, 8, c),
        (sib_a, 0, 1 - c),
        (sib_b, 8, 1 - c),
    ):

        def place(unit, carry, held=held, first_unit=first_unit, core=core):
            rows, narrow, wide = unit_place(unit + first_unit, core)
            w_out[rows, narrow] = held[unit, :, 0:LANES]
            w_in[rows, wide] = held[unit, :, LANES : LANES + hidden_block]
            w_back[rows, wide] = held[unit, :, LANES + hidden_block :]
            return carry

        lax.fori_loop(0, units // 2, place, 0)
    rows_all = embedded.shape[0]
    edge_rows = edge_own.shape[0]
    at = pl.multiple_of(jnp.where(x == 0, rows_all - edge_rows, 0), 128)
    edge_at = pl.ds(at, edge_rows)
    token = lax.broadcasted_iota(jnp.int32, (edge_rows, LANES), 0) + at + head * rows_all
    elsewhere = jnp.where(token < sc[0], 0, 1) != x
    for p in range(2):
        part = slice(p * LANES, (p + 1) * LANES)
        for held, edge, core in ((mix_own, edge_own, c), (mix_sib, edge_sib, 1 - c)):
            lanes = pl.ds(pl.multiple_of((2 * p + core) * LANES, LANES), LANES)
            mixed[:, lanes] = held[:, part]
            mixed[edge_at, lanes] = jnp.where(elsewhere, edge[:, part], mixed[edge_at, lanes])

    gain_one, shift_one = vectors[0:1, :], vectors[1:2, :]
    gain_two, shift_two = vectors[2:3, :], vectors[3:4, :]
    halt_vector, bias_out = vectors[4:5, :], vectors[5:6, :]
    halt_offset = vectors[6:7, 0:1]

    branch = mm(mixed[...], w_out[...], NT)
    normed_one, scale_one = norm_parts(embedded[...] + branch)
    first = normed_one * gain_one + shift_one
    first_low[...] = first.astype(bf16)
    chunk = 256
    steps = hidden // chunk
    k0 = math.sqrt(2.0 / math.pi)

    outward = first + bias_out
    for index in range(steps):
        cols = slice(index * chunk, (index + 1) * chunk)
        u = mm(first_low[...], w_in[:, cols]) + bias_in[:, cols]
        square = u * u
        t = jnp.tanh(k0 * u * (1.0 + 0.044715 * square))
        half = 0.5 * (1.0 + t)
        act = (u * half).astype(bf16)
        active[:, cols] = act
        slope[:, cols] = half + 0.5 * u * (1.0 - t * t) * (k0 * (1.0 + 3 * 0.044715 * square))
        outward = outward + mm(act, w_back[:, cols], NT)
    normed_two, scale_two = norm_parts(outward)
    second = normed_two * gain_two + shift_two
    halting = jax.nn.sigmoid(jnp.sum(second * halt_vector, axis=1, keepdims=True) + halt_offset)
    run = running[:, 0:1]
    rows_in = state[...].astype(f32)
    difference = second - rows_in
    share = run * halting
    new_state[...] = (rows_in + share * difference).astype(bf16)
    g = cotangent[...].astype(f32)
    carry_c = jnp.sum(g * difference, axis=1, keepdims=True)
    push = share * (1.0 - halting) * carry_c
    grad_second = share * g + push * halt_vector
    sums[...] = jnp.zeros_like(sums)

    def total(row, value):
        sums[row : row + 1, :] = jnp.sum(value, axis=0, keepdims=True)

    total(5, push * second)
    sums[6:7, :] = jnp.broadcast_to(jnp.sum(push, axis=0, keepdims=True), (1, width))
    total(3, grad_second * normed_two)
    total(4, grad_second)
    grad_outward = norm_back(normed_two, scale_two, gain_two, grad_second)
    total(0, grad_outward)
    grad_out_low[...] = grad_outward.astype(bf16)

    grad_first = grad_outward
    for index in range(steps):
        cols = slice(index * chunk, (index + 1) * chunk)
        gi = (mm(grad_out_low[...], w_back[:, cols]) * slope[:, cols]).astype(bf16)
        grad_inner[:, cols] = gi
        row, lane0 = 8 + (index * chunk) // width, (index * chunk) % width
        sums[row : row + 1, lane0 : lane0 + chunk] = jnp.sum(
            gi.astype(f32), axis=0, keepdims=True
        )
        grad_first = grad_first + mm(gi, w_in[:, cols], NT)
    total(1, grad_first * normed_one)
    total(2, grad_first)
    grad_resid = norm_back(normed_one, scale_one, gain_one, grad_first)
    base[...] = grad_resid + (1.0 - share) * g
    grad_branch[...] = grad_resid.astype(bf16)
    grad_mixed = mm(grad_branch[...], w_out[...]).astype(bf16)
    for p in range(2):
        blocks = [grad_mixed[:, (2 * p + k) * LANES : (2 * p + k + 1) * LANES] for k in range(2)]
        to = slice(p * LANES, (p + 1) * LANES)
        grad_own[:, to] = jnp.where(c == 0, blocks[0], blocks[1])
        grad_sib[:, to] = jnp.where(c == 0, blocks[1], blocks[0])
    edge_for_own[...] = grad_own[edge_at, :]
    edge_for_sib[...] = grad_sib[edge_at, :]

    turned_branch = jnp.transpose(grad_branch[...])
    turned_first = jnp.transpose(first_low[...])
    turned_out = jnp.transpose(grad_out_low[...])
    high = sums[...].astype(bf16)
    low = (sums[...] - high.astype(f32)).astype(bf16)
    for out, core in ((sum_sib, 1 - c), (sum_own, c)):
        for over_x in range(2):
            block = (x ^ over_x) * 2 + core
            narrow = pl.ds(pl.multiple_of(block * LANES, LANES), LANES)
            wide = pl.ds(pl.multiple_of(block * hidden_block, hidden_block), hidden_block)
            for turned, source, lanes, lane0 in (
                (turned_branch, mixed, narrow, 0),
                (turned_first, grad_inner, wide, LANES),
                (turned_out, active, wide, LANES + hidden_block),
            ):
                value = mm(turned, source[:, lanes]).astype(bf16)
                for k in range(width // UNIT):
                    unit = unit_of((dp ^ k) * 4 + over_x * X, core)
                    to = pl.ds(pl.multiple_of(unit * UNIT, UNIT), UNIT)
                    out[to, lane0 : lane0 + value.shape[1]] = value[k * UNIT : (k + 1) * UNIT, :]
        tail = slice(units * UNIT, units * UNIT + 16)
        out[tail, 0:width] = high
        out[tail, width : 2 * width] = low
        out[tail, 2 * width :] = jnp.zeros_like(out[tail, 2 * width :])


def hidden_back_kernel(sc, grads, weight, base, own, sib, edge):
    local = own.shape[0]
    for target, first, tall in ((sib, local, 320), (edge, 2 * local, 256), (own, 0, 320)):

        def rows(index, carry, target=target, first=first, tall=tall):
            start = pl.multiple_of(index * tall, 64)
            at = pl.ds(pl.multiple_of(first + index * tall, 64), tall)
            value = mm(grads[at, :], weight[...], NT)
            to = pl.ds(start, tall)
            if target is own:
                target[to, :] = value + base[to, :]
            else:
                target[to, :] = value.astype(bf16)
            return carry

        lax.fori_loop(0, target.shape[0] // tall, rows, 0)


def split_tail(rows, width):
    return rows[:, :width].astype(f32) + rows[:, width : 2 * width].astype(f32)


def fold_kernel(sc, own, arrived, sums_in, leave, stay, sums):
    width = sums.shape[1]
    rows = own.shape[0]
    half = stay.shape[0]
    stay[...] = (own[0:half, :].astype(f32) + arrived[0:half, :].astype(f32)).astype(bf16)
    leave[0:half, :] = (
        own[half : 2 * half, :].astype(f32) + arrived[half : 2 * half, :].astype(f32)
    ).astype(bf16)
    if rows == 2 * half:
        mine = sums_in[...]
    else:
        mine = split_tail(own[2 * half :, :], width)
    total = mine + split_tail(arrived[2 * half :, :], width)
    high = total.astype(bf16)
    low = (total - high.astype(f32)).astype(bf16)
    leave[half:, 0:width] = high
    leave[half:, width : 2 * width] = low
    leave[half:, 2 * width :] = jnp.zeros_like(leave[half:, 2 * width :])
    sums[...] = high.astype(f32) + low.astype(f32)


def last_fold_kernel(sc, own, arrived, sums_in, out_part, in_part, back_part, sums):
    width = sums.shape[1]
    rows = own.shape[0]
    total = own[...].astype(f32) + arrived[0:rows, :].astype(f32)
    hidden_block = in_part.shape[1]
    out_part[...] = total[:, :LANES]
    in_part[...] = total[:, LANES : LANES + hidden_block]
    back_part[...] = total[:, LANES + hidden_block :]
    sums[...] = sums_in[...] + split_tail(arrived[rows:, :], width)


def fold(sc, own, arrived, sums, width):
    half = (arrived.shape[0] - 16) // 2
    wide = own.shape[1]
    return call(
        fold_kernel,
        "fold",
        [((half + 16, wide), bf16), ((half, wide), bf16), ((16, width), f32)],
        [sc, own, arrived, sums],
        flops=4 * half * wide,
        moved=8 * half * wide,
        limit=24,
    )


def add(a, b):
    return a.astype(f32) + b.astype(f32)


def after(array, *others):
    return lax.optimization_barrier((array, *others))[0]


def body(
    state_in,
    qkv_weight,
    out_weight,
    ffn_in_weight,
    ffn_out_weight,
    ffn_in_bias,
    ffn_out_bias,
    norm1_gain,
    norm1_shift,
    norm2_gain,
    norm2_shift,
    halt_weight,
    halt_bias,
    seg_ids,
    halt_mask,
    cotangent,
):
    dp = lax.axis_index("dp")
    head = lax.axis_index("head")
    x, c = head // 2, head % 2
    local, width = state_in.shape
    window = 4 * local - SEQ_MIN
    edge = window - 2 * local
    hidden = ffn_in_bias.shape[0]
    unit_wide = LANES + 2 * (hidden // 4)
    ringed = qkv_weight.shape[1] == UNIT and lax.axis_size("dp") == 8

    hops = list(zip(*ORDERS))
    seg_row = seg_ids[0]
    split = jnp.sum(jnp.where(seg_row == 0, 1, 0), dtype=jnp.int32)
    sc = jnp.stack([split, head, x, c, dp if ringed else 0 * dp, jnp.int32(local)])
    sc = sc.astype(jnp.int32)
    half_width = width // 2
    rates = jnp.exp(
        jnp.arange(half_width, dtype=f32) * (-math.log(10000.0) / (half_width - 1))
    )[None]
    constant = jnp.concatenate([jnp.sin(STEP * rates), jnp.cos(STEP * rates)], axis=1)
    embedded, hidden_own, hidden_out, running = call(
        embed_kernel,
        "embed",
        [
            ((local, width), f32),
            ((local, width), bf16),
            ((edge, width), bf16),
            ((local, LANES), f32),
        ],
        [sc, state_in, rates, constant, halt_mask[:, None]],
        flops=local * width * 100,
        moved=4 << 20,
    )
    rest = jnp.concatenate([out_weight, ffn_in_weight, ffn_out_weight], axis=1)
    if ringed:
        first_hop = send(qkv_weight[None], (Z1, Z1))
        held = jnp.concatenate([qkv_weight[None], first_hop], axis=0)
        rest_own = after(rest, first_hop)[None]
        rest_far = send(rest_own, hops[0])
        held = after(held, embedded)
        second_hop = send(held, (Z0, Z0))
    hidden_sib = lax.ppermute(hidden_own, "head", CORE)
    far = lax.ppermute(hidden_out, "head", EDGE_OUT)
    hidden_edge = far + lax.ppermute(far, "head", CORE)
    if ringed:
        held = jnp.concatenate([held, second_hop], axis=0)
        qkv_units = [held] + [send(held, (bit, bit)) for bit in (X, Y, X | Y)]
        rest_own = jnp.concatenate([rest_own, after(rest_far, second_hop)], axis=0)
        rest_far = send(rest_own, hops[1])
        rest_own = jnp.concatenate([rest_own, after(rest_far, hidden_edge)], axis=0)
        rest_far = send(rest_own, hops[2])
        hidden_front = after(hidden_own, rest_own)
    else:
        qkv_units, rest_whole = gather_whole(qkv_weight, rest, x, c)
        hidden_front = hidden_own

    far_rows = local + edge
    (
        qf_own,
        kb,
        vb,
        qkv_full,
        qb_far,
        mixed32_far,
        mix_for_sib,
        mix_edge,
    ) = call(
        front_kernel,
        "front",
        [
            ((4, local, LANES), bf16),
            ((4, window, LANES), bf16),
            ((4, window, LANES), bf16),
            ((width, 6 * LANES), bf16),
            ((4, far_rows, LANES), bf16),
            ((far_rows, 2 * LANES), f32),
            ((local, 2 * LANES), bf16),
            ((edge, 2 * LANES), bf16),
        ],
        [sc, hidden_front, hidden_sib, hidden_edge, *qkv_units],
        scratch=[((4, far_rows, LANES), bf16)],
        flops=2 * window * width * 6 * LANES + 2 * 8 * far_rows * window * 256,
        moved=12 << 20,
    )
    if ringed:
        rest_a = jnp.concatenate([rest_own, after(rest_far, mix_edge)], axis=0)
        rest_b = send(rest_a, hops[3])
        qf_own = after(qf_own, rest_a)
    else:
        rest_a, rest_b = rest_whole[:8], rest_whole[8:]
    sib_a = lax.ppermute(rest_a, "head", CORE)
    mix_sib = lax.ppermute(mix_for_sib, "head", CORE)
    edge_own = lax.ppermute(mix_edge, "head", EDGE_BACK)
    edge_sib = lax.ppermute(mix_edge, "head", EDGE_SWAP)
    qb_own, mixed32_own, mix_own = call(
        attend_own_kernel,
        "attend_own",
        [((4, local, LANES), bf16), ((local, 2 * LANES), f32), ((local, 2 * LANES), bf16)],
        [sc, qf_own, kb, vb],
        flops=2 * 8 * local * window * 256,
        moved=6 << 20,
    )

    sib_b = lax.ppermute(after(rest_b, mix_own), "head", CORE)
    vectors = jnp.stack(
        [
            norm1_gain,
            norm1_shift,
            norm2_gain,
            norm2_shift,
            halt_weight,
            ffn_out_bias,
            jnp.broadcast_to(halt_bias, (width,)),
            jnp.zeros((width,), f32),
        ]
    )
    (
        new_state,
        base,
        grad_own,
        grad_for_sib,
        edge_for_own,
        edge_for_sib,
        sum_own,
        sum_sib,
    ) = call(
        middle_kernel,
        "middle",
        [
            ((local, width), bf16),
            ((local, width), f32),
            ((local, 2 * LANES), bf16),
            ((local, 2 * LANES), bf16),
            ((edge, 2 * LANES), bf16),
            ((edge, 2 * LANES), bf16),
            ((16 * UNIT + 16, unit_wide), bf16),
            ((16 * UNIT + 16, unit_wide), bf16),
        ],
        [
            sc,
            embedded,
            state_in,
            cotangent,
            running,
            mix_own,
            mix_sib,
            edge_own,
            edge_sib,
            rest_a,
            rest_b,
            sib_a,
            sib_b,
            vectors,
            ffn_in_bias[None],
        ],
        scratch=[
            ((local, width), bf16),
            ((local, width), bf16),
            ((local, hidden), bf16),
            ((local, width), bf16),
            ((local, hidden), bf16),
            ((local, width), bf16),
            ((16, width), f32),
            ((width, width), bf16),
            ((width, hidden), bf16),
            ((width, hidden), bf16),
            ((local, hidden), f32),
        ],
        flops=2 * local * width * (3 * width + 6 * hidden),
        moved=20 << 20,
    )
    grad_sib = lax.ppermute(grad_for_sib, "head", CORE)
    grad_edge = lax.ppermute(edge_for_own, "head", EDGE_OUT) + lax.ppermute(
        edge_for_sib, "head", EDGE_SWAP
    )

    if ringed:
        sum_arrived = lax.ppermute(sum_sib, "head", CORE)
    heads_t = ((4, HEAD_SIZE, window), f32)
    dq_own, keys_t, values_t = call(
        back_own_kernel,
        "back_own",
        [((local, 2 * LANES), bf16), heads_t, heads_t],
        [sc, qb_own, kb, vb, mixed32_own, grad_own],
        flops=2 * 20 * local * window * 256,
        moved=10 << 20,
    )
    if ringed:
        empty = jnp.zeros((16, width), f32)
        leave, stay, sums = fold(sc, sum_own, after(sum_arrived, dq_own), empty, width)
        sum_arrived = send(leave, hops[3])
        grad_sib = after(grad_sib, stay)
    dq_sib, keys_t, values_t = call(
        back_far_kernel,
        "back_sib",
        [((local, 2 * LANES), bf16), heads_t, heads_t],
        [sc, qb_far, kb, vb, mixed32_far, grad_sib, keys_t, values_t],
        flops=2 * 20 * local * window * 256,
        moved=14 << 20,
    )
    if ringed:
        leave, stay, sums = fold(sc, stay, after(sum_arrived, dq_sib), sums, width)
        sum_arrived = send(leave, hops[2])
        grad_edge = after(grad_edge, stay)
    grad_projected, *qkv_sums = call(
        back_edge_kernel,
        "back_edge",
        [((window, 6 * LANES), bf16)] + [((4, 3, UNIT, LANES), bf16)] * 4,
        [
            sc,
            qb_far,
            kb,
            vb,
            mixed32_far,
            grad_edge,
            keys_t,
            values_t,
            dq_own,
            dq_sib,
            hidden_own,
            hidden_sib,
            hidden_edge,
        ],
        scratch=[heads_t, heads_t, ((width, 6 * LANES), bf16)],
        flops=2 * 20 * edge * window * 256 + 2 * window * width * 6 * LANES,
        moved=14 << 20,
    )
    if ringed:
        here, *away = qkv_sums
        arrived = [send(a, (bit, bit)) for a, bit in zip(away, (X, Y, X | Y))]
        leave, stay, sums = fold(sc, stay, after(sum_arrived, here), sums, width)
        sum_arrived = send(leave, hops[1])
        base = after(base, stay)
    state_own, state_sib, state_edge = call(
        hidden_back_kernel,
        "hidden_back",
        [((local, width), f32), ((local, width), bf16), ((edge, width), bf16)],
        [sc, grad_projected, qkv_full, base],
        flops=2 * window * width * 6 * LANES,
        moved=6 << 20,
    )
    if ringed:
        here = (add(here, arrived[0]) + add(arrived[1], arrived[2])).astype(bf16)
        arrived = [send(here[k], (bit, bit)) for k, bit in ((2, Z0), (1, Z1), (3, Z0 | Z1))]
        leave, stay, sums = fold(sc, stay, after(sum_arrived, here), sums, width)
        sum_arrived = send(leave, hops[0])
        grad_qkv_weight = add(here[0], arrived[0]) + add(arrived[1], arrived[2])
        quarter = hidden // 4
        grad_out, grad_in, grad_back, small = call(
            last_fold_kernel,
            "last_fold",
            [
                ((UNIT, LANES), f32),
                ((UNIT, quarter), f32),
                ((UNIT, quarter), f32),
                ((16, width), f32),
            ],
            [sc, stay, sum_arrived, sums],
            limit=24,
        )
        first = lax.ppermute(small, "head", [(0, 1), (2, 3)])
        small = jnp.where(c == 0, small, first)
    else:
        grad_qkv_weight, rest_grad, small = scatter_whole(qkv_sums, sum_own, sum_sib, width, x)
        grad_out = rest_grad[:, :LANES]
        grad_in = rest_grad[:, LANES : LANES + hidden // 4]
        grad_back = rest_grad[:, LANES + hidden // 4 :]

    at = jnp.where(x == 0, local - edge, 0)
    state_far = add(
        lax.ppermute(state_edge, "head", EDGE_BACK), lax.ppermute(state_edge, "head", EDGE_SWAP)
    )
    grad_state = add(state_own, lax.ppermute(state_sib, "head", CORE))
    grad_state = lax.dynamic_update_slice_in_dim(
        grad_state, lax.dynamic_slice_in_dim(grad_state, at, edge) + state_far, at, 0
    )
    return (
        new_state,
        grad_state,
        grad_qkv_weight,
        grad_out,
        grad_in,
        grad_back,
        small[8 : 8 + hidden // width].reshape(hidden),
        small[0],
        small[1],
        small[2],
        small[3],
        small[4],
        small[5],
        small[6, 0:1],
    )


def unit_owners():
    table = []
    for order in ORDERS:
        for unit in range(16):
            number = sum(bit for place, bit in enumerate(order) if (unit >> place) & 1)
            table.append((number >> 2, (number >> 1) & 1))
    return table[:16], table[16:]


def gather_whole(qkv_weight, rest, x, c):
    def both(array, axis):
        whole = lax.all_gather(array, "dp", axis=axis, tiled=True)
        other = lax.ppermute(whole, "head", ACROSS)
        return jnp.stack([whole, other])

    qkv, rest = both(qkv_weight, 1), both(rest, 0)
    width = rest.shape[1]
    qkv = qkv.reshape(2, 3, width // UNIT, UNIT, LANES)
    rest = rest.reshape(2, width // UNIT, UNIT, rest.shape[2])
    units = [qkv_owner(unit) for unit in range(16)]
    qkv = jnp.stack([qkv[over_x, :, over_dp] for over_dp, over_x in units])
    cores = [jnp.stack([rest[ox, od] for od, ox in table]) for table in unit_owners()]
    return [qkv[4 * k : 4 * k + 4] for k in range(4)], jnp.where(c == 0, *cores)


def scatter_whole(qkv_sums, sum_own, sum_sib, width, x):
    c = lax.axis_index("head") % 2
    rows = 16 * UNIT
    rest = add(sum_own, lax.ppermute(sum_sib, "head", CORE))
    tail = rest[rows:]
    small = lax.psum(tail[:, :width] + tail[:, width : 2 * width], ("dp", "head")) * 0.5
    rest = rest[:rows].reshape(16, UNIT, rest.shape[1])
    qkv = jnp.concatenate(qkv_sums, axis=0).astype(f32)

    def order(table, array):
        back = {owner_of: unit for unit, owner_of in enumerate(table)}
        return [jnp.stack([array[back[od, ox]] for od in range(8)]) for ox in range(2)]

    parts = [order(table, rest) for table in unit_owners()]
    rest = [jnp.where(c == 0, a, b).reshape(width, rest.shape[2]) for a, b in zip(*parts)]
    qkv = order([qkv_owner(unit) for unit in range(16)], qkv)
    qkv = [jnp.transpose(q, (1, 0, 2, 3)).reshape(3, width, LANES) for q in qkv]
    rest = rest[0] + lax.ppermute(rest[1], "head", ACROSS)
    qkv = qkv[0] + lax.ppermute(qkv[1], "head", ACROSS)
    return (
        lax.psum_scatter(qkv, "dp", scatter_dimension=1, tiled=True),
        lax.psum_scatter(rest, "dp", scatter_dimension=0, tiled=True),
        small,
    )


def solution(mesh):
    tokens = P(("dp", "head"), None)
    weights = P("dp", "head")
    return jax.shard_map(
        body,
        mesh=mesh,
        in_specs=(
            tokens,
            P(None, "dp", "head"),
            weights,
            weights,
            weights,
            P(),
            P(),
            P(),
            P(),
            P(),
            P(),
            P(),
            P(),
            P("dp", None),
            P(("dp", "head")),
            tokens,
        ),
        out_specs=(
            tokens,
            tokens,
            P(None, "dp", "head"),
            weights,
            weights,
            weights,
            P(),
            P(),
            P(),
            P(),
            P(),
            P(),
            P(),
            P(),
        ),
        check_vma=False,
    )
```

```python
import functools
import math

import jax
import jax.numpy as jnp
from jax import lax
from jax.experimental import pallas as pl
from jax.experimental.pallas import tpu as pltpu
from jax.sharding import PartitionSpec as P

HEAD_SIZE = 64
STEP = 2
SEQ_MIN = 1024
LANES = 128
UNIT = 64
MICROSECOND = 1150 * 10**6

norm_epsilon = 1e-06
masked_score = -1e30
log2e = 1.4426950408889634

f32 = jnp.float32
bf16 = jnp.bfloat16
NT = (((1,), (1,)), ((), ()))
NN = (((1,), (0,)), ((), ()))
TN = (((0,), (0,)), ((), ()))

CORE = [(0, 1), (1, 0), (2, 3), (3, 2)]
ACROSS = [(0, 2), (2, 0), (1, 3), (3, 1)]
SWAP = [(1, 2), (2, 1)]
TO_EDGE = [(0, 1), (3, 2)]
FROM_EDGE = [(1, 0), (2, 3)]

X, Y, Z0, Z1 = 2, 4, 8, 16
ORDERS = ((Z1, Z0, Y, X), (Z1, Y, X, Z0))
QKV_ORDERS = ((Z1, Z0, X, Y), (Z1, Z0, Y, X))

vmem = pl.BlockSpec(memory_space=pltpu.VMEM)
smem = pl.BlockSpec(memory_space=pltpu.SMEM)


def mm(a, b, dims=NN):
    return lax.dot_general(a, b, dims, preferred_element_type=f32)


def call(kernel, name, outs, ins, scratch=(), flops=0, limit=56, scalars=(), scalars_out=()):
    return pl.pallas_call(
        kernel,
        name=name,
        out_shape=[jax.ShapeDtypeStruct(s, t) for s, t in outs],
        in_specs=[smem if k == 0 or k in scalars else vmem for k in range(len(ins))],
        out_specs=[smem if k in scalars_out else vmem for k in range(len(outs))],
        scratch_shapes=[pltpu.VMEM(s, t) for s, t in scratch],
        compiler_params=pltpu.CompilerParams(vmem_limit_bytes=limit << 20),
        cost_estimate=pl.CostEstimate(flops=flops, bytes_accessed=0, transcendentals=0),
    )(*ins)


def send(array, bits):
    count = 4 * lax.axis_size("dp")
    pairs = [(i, i ^ bits[i & 1]) for i in range(count)]
    return lax.ppermute(array, ("dp", "head"), pairs)


def owner(unit, core, orders=ORDERS):
    found = []
    for order in orders:
        over_dp, over_x = 0, 0
        for place, bit in enumerate(order):
            flag = (unit >> place) & 1
            if bit == X:
                over_x = flag
            else:
                over_dp = over_dp + flag * (bit >> 2)
        found.append((over_dp, over_x))
    return (
        jnp.where(core == 0, found[0][0], found[1][0]),
        jnp.where(core == 0, found[0][1], found[1][1]),
    )


def unit_of(number, core, orders=ORDERS):
    found = [0, 0]
    for k, order in enumerate(orders):
        for place, bit in enumerate(order):
            found[k] = found[k] + ((number // bit) & 1) * (1 << place)
    return jnp.where(core == 0, found[0], found[1])


def window_token(sc, first, shape):
    head, x, local = sc[1], sc[2], sc[5]
    row = lax.broadcasted_iota(jnp.int32, shape, 0) + first
    return jnp.where(
        row < local,
        head * local + row,
        jnp.where(
            row < 2 * local,
            (head ^ 1) * local + row - local,
            row + jnp.where(x == 0, 0, SEQ_MIN - 2 * local),
        ),
    )


def window_valid(sc, first, shape):
    return jnp.where(window_token(sc, first, shape) < sc[0], 0, 1) == sc[2]


def lanes_of(shape):
    return lax.broadcasted_iota(jnp.int32, shape, 1)


def turns(fraction):
    square = fraction * fraction
    sine, cosine = 0.0, 0.0
    for k in range(8, -1, -1):
        sign = -1.0 if k % 2 else 1.0
        sine = sine * square + sign * (2 * math.pi) ** (2 * k + 1) / math.factorial(2 * k + 1)
        cosine = cosine * square + sign * (2 * math.pi) ** (2 * k) / math.factorial(2 * k)
    return sine * fraction, cosine


def embed_kernel(ids, segments, state, edge_here, edge_core, sc, embedded, hidden, hidden_edge):
    local, width = state.shape
    half = width // 2
    sc[0] = jnp.sum(jnp.where(segments[...] == 0, 1, 0))
    for k in range(1, 6):
        sc[k] = ids[k]

    def signal(places, rows):
        order = lanes_of((rows, half)).astype(f32)
        rates = jnp.exp(order * (-math.log(10000.0) / (half - 1))) * (0.5 / math.pi)
        turn = places * rates
        return turns(turn - jnp.floor(turn + 0.5))

    steps = signal(float(STEP), 1)
    for source, first in ((state, 0), (edge_here, 2 * local)):
        rows = source.shape[0]
        token = window_token(sc, first, (rows, half))
        place = token - jnp.where(token < sc[0], 0, sc[0])
        for side, value in enumerate(signal(place.astype(f32), rows)):
            to = slice(side * half, (side + 1) * half)
            rows_in = source[:, to].astype(f32)
            if source is edge_here:
                rows_in = rows_in + edge_core[:, to].astype(f32)
            total = rows_in + value + steps[side]
            if source is state:
                embedded[:, to] = total
                hidden[:, to] = total.astype(bf16)
            else:
                hidden_edge[:, to] = total.astype(bf16)


def attend_rows(rows, qf, kb, vb, mixed32, logs, mixed, place):
    tall = mixed.shape[0]
    lane = lanes_of((tall, LANES))
    log_totals = jnp.zeros((tall, LANES), f32)
    results = []
    for j in range(4):
        scores = mm(qf[j, rows, :], kb[j], NT)
        peak = jnp.max(scores, axis=1, keepdims=True)
        weights = jnp.exp2((scores - peak) * log2e).astype(bf16)
        summed = mm(weights, vb[j])
        log_totals = jnp.where(lane == 64 + j, peak + jnp.log(summed), log_totals)
        results.append(summed * (1.0 / pltpu.roll(summed, 64, 1)))
        if j % 2:
            both = jnp.where(lane < 64, results[j - 1], pltpu.roll(results[j], 64, 1))
            to = slice((j // 2) * LANES, (j // 2 + 1) * LANES)
            mixed32[:, to] = both
            mixed[:, place(j // 2)] = both.astype(bf16)
    logs[...] = log_totals


def front_kernel(
    sc,
    own,
    sib,
    edge,
    units_a,
    units_b,
    qf,
    kb,
    vb,
    qt,
    weight,
    mixed32,
    logs,
    mix_edge,
):
    x, c, dp = sc[2], sc[3], sc[4]
    for place, held in enumerate((units_a, units_b)):
        for sub in range(8):
            over_dp, over_x = owner(place * 8 + sub, c, QKV_ORDERS)
            row = pl.multiple_of((dp ^ over_dp) * UNIT, UNIT)
            for m in range(3):
                column = pl.multiple_of(m * 256 + (x ^ over_x) * LANES, LANES)
                weight[pl.ds(row, UNIT), pl.ds(column, LANES)] = held[sub, m]
    local = own.shape[0]
    for source, base in ((own, 0), (sib, local), (edge, 2 * local)):
        tall = 256 if source is edge else local
        lane = lanes_of((tall, LANES))

        def rows(index, carry, source=source, base=base, tall=tall, lane=lane):
            start = pl.multiple_of(index * tall, 128)
            out = pl.multiple_of(base + index * tall, 128)
            at = pl.ds(out, tall)
            projected = mm(source[pl.ds(start, tall), :], weight[...])
            valid = window_valid(sc, out, (tall, LANES))
            key_tail = jnp.where((lane == 64) & jnp.logical_not(valid), masked_score, 0.0)
            for p in range(2):
                blocks = [
                    projected[:, m * 256 + p * LANES : m * 256 + (p + 1) * LANES]
                    for m in range(3)
                ]
                blocks[0] = blocks[0] * 0.125
                qt[p, :, at] = jnp.transpose(blocks[0]).astype(bf16)
                for k in range(2):
                    if k:
                        blocks = [pltpu.roll(block, 64, 1) for block in blocks]
                    j = 2 * p + k
                    first = lane < 64
                    qf[j, at, :] = jnp.where(
                        first, blocks[0], jnp.where(lane == 64, 1.0, 0.0)
                    ).astype(bf16)
                    kb[j, at, :] = jnp.where(first, blocks[1], key_tail).astype(bf16)
                    vb[j, at, :] = jnp.where(first, blocks[2], 1.0).astype(bf16)
            return carry

        lax.fori_loop(0, source.shape[0] // tall, rows, 0)

    mix_edge[...] = jnp.zeros_like(mix_edge)
    attend_rows(
        pl.ds(2 * local, mix_edge.shape[0]),
        qf,
        kb,
        vb,
        mixed32,
        logs,
        mix_edge,
        lambda p: pl.ds(pl.multiple_of((2 * p + c) * LANES, LANES), LANES),
    )


def attend_kernel(first, sc, qf, kb, vb, mixed32, logs, mixed):
    attend_rows(
        pl.ds(first, mixed.shape[0]),
        qf,
        kb,
        vb,
        mixed32,
        logs,
        mixed,
        lambda p: slice(p * LANES, (p + 1) * LANES),
    )


def back_rows(sc, first, qf, kb, vb, qt, grad, mixed32, logs, part, before, keys_t, values_t, out):
    tall = part.size
    lane = lanes_of((tall, LANES))
    valid = window_valid(sc, first, (tall, LANES))
    rows = pl.ds(first, tall)
    for p in range(2):
        to = slice(p * LANES, (p + 1) * LANES)
        incoming = jnp.where(valid, grad(part, p), 0.0)
        product = incoming * mixed32[part, to]
        incoming_t = jnp.transpose(incoming).astype(bf16)
        grad_queries = []
        for k in range(2):
            j = 2 * p + k
            half = (lane < 64) if k == 0 else (lane >= 64)
            delta = jnp.sum(jnp.where(half, product, 0.0), axis=1, keepdims=True)
            log_total = logs[part, 64 + j : 65 + j] * log2e
            arriving = incoming if k == 0 else pltpu.roll(incoming, 64, 1)
            arriving = jnp.where(lane < 64, arriving, 0.0).astype(bf16)
            probs = jnp.exp2(mm(qf[j, rows, :], kb[j], NT) * log2e - log_total)
            grad_probs = mm(arriving, vb[j], NT)
            grad_scores = (probs * (grad_probs - delta)).astype(bf16)
            piece = slice(64 * k, 64 * k + 64)
            values = mm(incoming_t[piece, :], probs.astype(bf16))
            keys = mm(qt[p, piece, rows], grad_scores)
            keys_t[j] = before[0][j] + keys if before else keys
            values_t[j] = before[1][j] + values if before else values
            grad_queries.append(mm(grad_scores, kb[j]) * 0.125)
        out[:, to] = jnp.where(
            lane < 64, grad_queries[0], pltpu.roll(grad_queries[1], 64, 1)
        ).astype(bf16)


def back_kernel(groups, sc, qf, kb, vb, qt, *rest):
    count = len(groups)
    before, (keys_t, values_t) = rest[3 * count : -count - 2], rest[-2:]
    for k, (first, start, rows) in enumerate(groups):
        mixed32, logs, grad = rest[3 * k : 3 * k + 3]
        back_rows(
            sc,
            first,
            qf,
            kb,
            vb,
            qt,
            lambda part, p, grad=grad: grad[part, p * LANES : (p + 1) * LANES].astype(f32),
            mixed32,
            logs,
            pl.ds(start, rows),
            before,
            keys_t,
            values_t,
            rest[k - count - 2],
        )
        before = (keys_t, values_t)


def back_edge_kernel(
    late,
    sc,
    qf,
    kb,
    vb,
    qt,
    mixed32,
    logs,
    edge_here,
    edge_core,
    mixed32_sib,
    logs_sib,
    grad_sib,
    keys_in,
    values_in,
    dq_first,
    dq_own,
    dq_sib,
    own,
    sib,
    edge,
    out,
    stay,
    leave,
    keys_t,
    values_t,
    full,
    dq_late,
    dq_edge,
):
    x, c, dp = sc[2], sc[3], sc[4]
    local = own.shape[0]
    before = (keys_in, values_in)

    def from_sib(part, p):
        return grad_sib[part, p * LANES : (p + 1) * LANES].astype(f32)

    def from_edge(part, p):
        here, there = slice(p * LANES, (p + 1) * LANES), slice((p + 2) * LANES, (p + 3) * LANES)
        return edge_here[part, here].astype(f32) + edge_core[part, there].astype(f32)

    for first, part, operands, target in (
        (2 * local - late, pl.ds(local - late, late), (from_sib, mixed32_sib, logs_sib), dq_late),
        (2 * local, pl.ds(0, edge.shape[0]), (from_edge, mixed32, logs), dq_edge),
    ):
        back_rows(
            sc, first, qf, kb, vb, qt, *operands, part, before, keys_t, values_t, target
        )
        before = (keys_t, values_t)
    at = 0
    for piece in (dq_first, dq_own, dq_sib, dq_late, dq_edge):
        out[at : at + piece.shape[0], 0:256] = piece[...]
        at += piece.shape[0]
    for m, held in ((1, keys_t), (2, values_t)):
        for p in range(2):
            pair = jnp.concatenate([held[2 * p], held[2 * p + 1]], axis=0)
            to = slice(m * 256 + p * LANES, m * 256 + (p + 1) * LANES)
            out[:, to] = jnp.transpose(pair).astype(bf16)
    for m in range(3):
        to = slice(m * 256, (m + 1) * 256)
        total = 0.0
        for source, base in ((own, 0), (sib, local), (edge, 2 * local)):
            total += mm(source[...], out[base : base + source.shape[0], to], TN)
        full[:, to] = total.astype(bf16)
    for place, target in enumerate((stay, leave)):
        for sub in range(8):
            over_dp, over_x = owner(place * 8 + sub, c, QKV_ORDERS)
            row = pl.multiple_of((dp ^ over_dp) * UNIT, UNIT)
            for m in range(3):
                column = pl.multiple_of(m * 256 + (x ^ over_x) * LANES, LANES)
                target[sub, m] = full[pl.ds(row, UNIT), pl.ds(column, LANES)]


def norm_parts(rows):
    width = rows.shape[1]
    center = rows - jnp.sum(rows, axis=1, keepdims=True) * (1.0 / width)
    spread = jnp.sum(center * center, axis=1, keepdims=True) * (1.0 / width)
    scale = lax.rsqrt(spread + norm_epsilon)
    return center * scale, scale


def norm_back(normed, scale, gain, incoming):
    width = normed.shape[1]
    e = incoming * gain
    mean_e = jnp.sum(e, axis=1, keepdims=True) * (1.0 / width)
    mean_en = jnp.sum(e * normed, axis=1, keepdims=True) * (1.0 / width)
    return (e - mean_e - normed * mean_en) * scale


def middle_kernel(
    sc,
    embedded,
    state,
    cotangent,
    running,
    mix_own,
    mix_sib,
    mix_edge,
    own_a,
    own_b,
    sib_a,
    sib_b,
    halt_offset,
    gain_one,
    shift_one,
    gain_two,
    shift_two,
    halt_vector,
    bias_out,
    bias_in,
    new_state,
    base,
    grad_own,
    grad_sib,
    grad_edge,
    mixed,
    first_low,
    active,
    grad_out_low,
    grad_inner,
    grad_branch,
    sums,
    w_out,
    w_in,
    w_back,
    slope,
):
    head, x, c, dp = sc[1], sc[2], sc[3], sc[4]
    hidden = w_in.shape[1]
    width = w_out.shape[0]
    hidden_block = hidden // 4
    units = 16

    def unit_place(unit, core):
        over_dp, over_x = owner(unit, core)
        rows = pl.ds(pl.multiple_of((dp ^ over_dp) * UNIT, UNIT), UNIT)
        block = (x ^ over_x) * 2 + core
        narrow = pl.ds(pl.multiple_of(block * LANES, LANES), LANES)
        wide = pl.ds(pl.multiple_of(block * hidden_block, hidden_block), hidden_block)
        return rows, narrow, wide

    for held, first_unit, core in (
        (own_a, 0, c),
        (own_b, 8, c),
        (sib_a, 0, 1 - c),
        (sib_b, 8, 1 - c),
    ):

        def place(unit, carry, held=held, first_unit=first_unit, core=core):
            rows, narrow, wide = unit_place(unit + first_unit, core)
            w_out[rows, narrow] = held[unit, :, 0:LANES]
            w_in[rows, wide] = held[unit, :, LANES : LANES + hidden_block]
            w_back[rows, wide] = held[unit, :, LANES + hidden_block :]
            return carry

        lax.fori_loop(0, units // 2, place, 0)
    rows_all = embedded.shape[0]
    edge_rows = mix_edge.shape[0]
    at = pl.multiple_of(jnp.where(x == 0, rows_all - edge_rows, 0), 128)
    edge_at = pl.ds(at, edge_rows)
    token = lax.broadcasted_iota(jnp.int32, (edge_rows, LANES), 0) + at + head * rows_all
    elsewhere = jnp.where(token < sc[0], 0, 1) != x
    for p in range(2):
        part = slice(p * LANES, (p + 1) * LANES)
        for held, core in ((mix_own, c), (mix_sib, 1 - c)):
            lanes = pl.ds(pl.multiple_of((2 * p + core) * LANES, LANES), LANES)
            mixed[:, lanes] = held[:, part]
            mixed[edge_at, lanes] = jnp.where(elsewhere, mix_edge[:, lanes], mixed[edge_at, lanes])

    diagonal = lax.broadcasted_iota(jnp.int32, (LANES, LANES), 0) == lanes_of((LANES, LANES))
    run_all = jnp.concatenate(
        [
            jnp.sum(
                jnp.where(diagonal, running[k : k + 1, :].astype(f32), 0.0), axis=1, keepdims=True
            )
            for k in range(running.shape[0])
        ],
        axis=0,
    )
    gains = tuple(
        g[...] for g in (gain_one, shift_one, gain_two, shift_two, halt_vector, bias_out)
    )
    tall = rows_all // 2
    for start in range(0, rows_all, tall):
        rows = slice(start, start + tall)

        def total(row, value, lanes=slice(None), start=start):
            value = jnp.sum(value, axis=0, keepdims=True)
            at_row = (slice(row, row + 1), lanes)
            sums[at_row] = value if start == 0 else sums[at_row] + value

        middle_rows(
            rows,
            total,
            run_all[rows, :],
            halt_offset[0],
            gains,
            bias_in,
            embedded,
            state,
            cotangent,
            new_state,
            base,
            grad_own,
            grad_sib,
            mixed,
            first_low,
            active,
            grad_out_low,
            grad_inner,
            grad_branch,
            w_out,
            w_in,
            w_back,
            slope,
            c,
        )
    sums[7:8, :] = jnp.zeros_like(sums[7:8, :])
    sums[12:, :] = jnp.zeros_like(sums[12:, :])
    grad_edge[:, 0 : 2 * LANES] = grad_sib[edge_at, :]
    grad_edge[:, 2 * LANES :] = grad_own[edge_at, :]


def middle_rows(
    rows,
    total,
    run,
    halt_offset,
    gains,
    bias_in,
    embedded,
    state,
    cotangent,
    new_state,
    base,
    grad_own,
    grad_sib,
    mixed,
    first_low,
    active,
    grad_out_low,
    grad_inner,
    grad_branch,
    w_out,
    w_in,
    w_back,
    slope,
    c,
):
    gain_one, shift_one, gain_two, shift_two, halt_vector, bias_out = gains
    width = w_out.shape[0]
    branch = mm(mixed[rows, :], w_out[...], NT)
    normed_one, scale_one = norm_parts(embedded[rows, :] + branch)
    first = normed_one * gain_one + shift_one
    low = first.astype(bf16)
    first_low[rows, :] = low
    chunk = 256
    steps = w_in.shape[1] // chunk
    k0 = math.sqrt(2.0 / math.pi)

    outward = first + bias_out
    for index in range(steps):
        cols = slice(index * chunk, (index + 1) * chunk)
        u = mm(low, w_in[:, cols]) + bias_in[:, cols]
        square = u * u
        t = jnp.tanh(k0 * u * (1.0 + 0.044715 * square))
        half = 0.5 * (1.0 + t)
        act = (u * half).astype(bf16)
        active[rows, cols] = act
        slope[rows, cols] = half + 0.5 * u * (1.0 - t * t) * (k0 * (1.0 + 3 * 0.044715 * square))
        outward = outward + mm(act, w_back[:, cols], NT)
    normed_two, scale_two = norm_parts(outward)
    second = normed_two * gain_two + shift_two
    halting = jax.nn.sigmoid(jnp.sum(second * halt_vector, axis=1, keepdims=True) + halt_offset)
    rows_in = state[rows, :].astype(f32)
    difference = second - rows_in
    share = run * halting
    new_state[rows, :] = (rows_in + share * difference).astype(bf16)
    g = cotangent[rows, :].astype(f32)
    carry_c = jnp.sum(g * difference, axis=1, keepdims=True)
    push = share * (1.0 - halting) * carry_c
    grad_second = share * g + push * halt_vector
    total(5, push * second)
    total(6, jnp.broadcast_to(push, second.shape))
    total(3, grad_second * normed_two)
    total(4, grad_second)
    grad_outward = norm_back(normed_two, scale_two, gain_two, grad_second)
    total(0, grad_outward)
    out_low = grad_outward.astype(bf16)
    grad_out_low[rows, :] = out_low

    grad_first = grad_outward
    for index in range(steps):
        cols = slice(index * chunk, (index + 1) * chunk)
        gi = (mm(out_low, w_back[:, cols]) * slope[rows, cols]).astype(bf16)
        grad_inner[rows, cols] = gi
        lane0 = (index * chunk) % width
        total(8 + (index * chunk) // width, gi.astype(f32), slice(lane0, lane0 + chunk))
        grad_first = grad_first + mm(gi, w_in[:, cols], NT)
    total(1, grad_first * normed_one)
    total(2, grad_first)
    grad_resid = norm_back(normed_one, scale_one, gain_one, grad_first)
    base[rows, :] = grad_resid + (1.0 - share) * g
    branch_low = grad_resid.astype(bf16)
    grad_branch[rows, :] = branch_low
    grad_mixed = mm(branch_low, w_out[...]).astype(bf16)
    for p in range(2):
        blocks = [grad_mixed[:, (2 * p + k) * LANES : (2 * p + k + 1) * LANES] for k in range(2)]
        to = slice(p * LANES, (p + 1) * LANES)
        grad_own[rows, to] = jnp.where(c == 0, blocks[0], blocks[1])
        grad_sib[rows, to] = jnp.where(c == 0, blocks[1], blocks[0])


def weight_kernel(
    sc, mixed, first_low, active, grad_out_low, grad_inner, grad_branch, sums, sum_own, sum_sib
):
    x, c, dp = sc[2], sc[3], sc[4]
    width = mixed.shape[1]
    hidden_block = active.shape[1] // 4
    units = 16
    turned_branch = jnp.transpose(grad_branch[...])
    turned_first = jnp.transpose(first_low[...])
    turned_out = jnp.transpose(grad_out_low[...])
    high = sums[...].astype(bf16)
    low = (sums[...] - high.astype(f32)).astype(bf16)
    for out, core in ((sum_sib, 1 - c), (sum_own, c)):
        for over_x in range(2):
            block = (x ^ over_x) * 2 + core
            narrow = pl.ds(pl.multiple_of(block * LANES, LANES), LANES)
            wide = pl.ds(pl.multiple_of(block * hidden_block, hidden_block), hidden_block)
            for turned, source, lanes, lane0 in (
                (turned_branch, mixed, narrow, 0),
                (turned_first, grad_inner, wide, LANES),
                (turned_out, active, wide, LANES + hidden_block),
            ):
                value = mm(turned, source[:, lanes]).astype(bf16)
                for k in range(width // UNIT):
                    unit = unit_of((dp ^ k) * 4 + over_x * X, core)
                    to = pl.ds(pl.multiple_of(unit * UNIT, UNIT), UNIT)
                    out[to, lane0 : lane0 + value.shape[1]] = value[k * UNIT : (k + 1) * UNIT, :]
        tail = slice(units * UNIT, units * UNIT + 16)
        out[tail, 0:width] = high
        out[tail, width : 2 * width] = low
        out[tail, 2 * width :] = jnp.zeros_like(out[tail, 2 * width :])


def hidden_back_kernel(sc, grads, weight, base, own, sib, edge):
    local = own.shape[0]
    for target, first, tall in ((sib, local, 320), (edge, 2 * local, 256), (own, 0, 320)):

        def rows(index, carry, target=target, first=first, tall=tall):
            start = pl.multiple_of(index * tall, 64)
            at = pl.ds(pl.multiple_of(first + index * tall, 64), tall)
            value = mm(grads[at, :], weight[...], NT)
            to = pl.ds(start, tall)
            if target is own:
                target[to, :] = value + base[to, :]
            else:
                target[to, :] = value.astype(bf16)
            return carry

        lax.fori_loop(0, target.shape[0] // tall, rows, 0)


def finish_kernel(sc, own, sib, edge, out):
    out[...] = own[...] + sib[...].astype(f32)
    rows = edge.shape[0]
    at = pl.ds(pl.multiple_of(jnp.where(sc[2] == 0, out.shape[0] - rows, 0), 128), rows)
    out[at, :] += edge[...].astype(f32)


def split_tail(rows, width):
    return rows[:, :width].astype(f32) + rows[:, width : 2 * width].astype(f32)


def fold_kernel(sc, own, arrived, sums_in, leave, stay, sums):
    width = sums.shape[1]
    rows = own.shape[0]
    half = stay.shape[0]
    stay[...] = (own[0:half, :].astype(f32) + arrived[0:half, :].astype(f32)).astype(bf16)
    leave[0:half, :] = (
        own[half : 2 * half, :].astype(f32) + arrived[half : 2 * half, :].astype(f32)
    ).astype(bf16)
    if rows == 2 * half:
        mine = sums_in[...]
    else:
        mine = split_tail(own[2 * half :, :], width)
    total = mine + split_tail(arrived[2 * half :, :], width)
    high = total.astype(bf16)
    low = (total - high.astype(f32)).astype(bf16)
    leave[half:, 0:width] = high
    leave[half:, width : 2 * width] = low
    leave[half:, 2 * width :] = jnp.zeros_like(leave[half:, 2 * width :])
    sums[...] = high.astype(f32) + low.astype(f32)


def last_fold_kernel(sc, own, arrived, sums_in, out_part, in_part, back_part, sums):
    width = sums.shape[1]
    rows = own.shape[0]
    total = own[...].astype(f32) + arrived[0:rows, :].astype(f32)
    hidden_block = in_part.shape[1]
    out_part[...] = total[:, :LANES]
    in_part[...] = total[:, LANES : LANES + hidden_block]
    back_part[...] = total[:, LANES + hidden_block :]
    sums[...] = sums_in[...] + split_tail(arrived[rows:, :], width)


def fold(sc, own, arrived, sums, width):
    half = (arrived.shape[0] - 16) // 2
    wide = own.shape[1]
    return call(
        fold_kernel,
        "fold",
        [((half + 16, wide), bf16), ((half, wide), bf16), ((16, width), f32)],
        [sc, own, arrived, sums],
        flops=MICROSECOND,
        limit=16,
    )


def qkv_fold_kernel(sc, own, arrived, leave, stay):
    half = stay.shape[0]
    total = own[...].astype(f32) + arrived[...].astype(f32)
    stay[...] = total[0:half].astype(bf16)
    leave[...] = total[half:].astype(bf16)


def qkv_fold(sc, own, arrived):
    half = ((own.shape[0] // 2, *own.shape[1:]), bf16)
    return call(
        qkv_fold_kernel, "qkv_fold", [half, half], [sc, own, arrived], flops=MICROSECOND, limit=16
    )


def add(a, b):
    return a.astype(f32) + b.astype(f32)


def after(array, *others):
    return lax.optimization_barrier((array, *others))[0]


def body(
    state_in,
    qkv_weight,
    out_weight,
    ffn_in_weight,
    ffn_out_weight,
    ffn_in_bias,
    ffn_out_bias,
    norm1_gain,
    norm1_shift,
    norm2_gain,
    norm2_shift,
    halt_weight,
    halt_bias,
    seg_ids,
    halt_mask,
    cotangent,
):
    dp = lax.axis_index("dp")
    head = lax.axis_index("head")
    x, c = head // 2, head % 2
    local, width = state_in.shape
    window = 4 * local - SEQ_MIN
    edge = window - 2 * local
    hidden = ffn_in_bias.shape[0]
    unit_wide = LANES + 2 * (hidden // 4)
    ringed = qkv_weight.shape[1] == UNIT and lax.axis_size("dp") == 8

    ids = jnp.stack([0 * dp, head, x, c, dp if ringed else 0 * dp, 0 * dp + local])
    ids = ids.astype(jnp.int32)
    at = jnp.where(x == 0, local - edge, 0)
    hops, qkv_hops = list(zip(*ORDERS)), list(zip(*QKV_ORDERS))
    rest = jnp.concatenate([out_weight, ffn_in_weight, ffn_out_weight], axis=1)
    state_rows = state_in
    swapped = lax.ppermute(lax.dynamic_slice_in_dim(state_in, at, edge), "head", SWAP)
    crossed = lax.ppermute(swapped, "head", FROM_EDGE)
    state_ready = state_in
    if ringed:
        rest_own = rest[None]
        rest_far = send(rest_own, hops[0])
        qkv_far = send(qkv_weight[None], qkv_hops[0])
        held = jnp.concatenate([qkv_weight[None], qkv_far], axis=0)
        qkv_far = send(held, qkv_hops[1])
        state_ready = after(state_in, held)
    sc, embedded, hidden_own, hidden_edge = call(
        embed_kernel,
        "embed",
        [
            ((6,), jnp.int32),
            ((local, width), f32),
            ((local, width), bf16),
            ((edge, width), bf16),
        ],
        [ids, seg_ids, state_ready, swapped, crossed],
        flops=4 * MICROSECOND,
        limit=20,
        scalars_out=(0,),
    )
    hidden_sib = lax.ppermute(hidden_own, "head", CORE)
    if ringed:
        held = jnp.concatenate([held, after(qkv_far, hidden_edge)], axis=0)
        qkv_far = send(held, qkv_hops[2])
        rest_own = jnp.concatenate([rest_own, after(rest_far, held)], axis=0)
        rest_far = send(rest_own, hops[1])
        held = jnp.concatenate([held, after(qkv_far, rest_own)], axis=0)
        qkv_units = [held, send(held, qkv_hops[3])]
        rest_own = jnp.concatenate([rest_own, after(rest_far, held)], axis=0)
        rest_far = send(rest_own, hops[2])
        hidden_front = after(hidden_own, rest_own)
    else:
        qkv_units, rest_whole = gather_whole(qkv_weight, rest, x, c)
        hidden_front = hidden_own

    wide = ((4, window, LANES), bf16)
    qf, kb, vb, qt, qkv_full, mixed32_edge, logs_edge, mix_edge = call(
        front_kernel,
        "front",
        [
            wide,
            wide,
            wide,
            ((2, LANES, window), bf16),
            ((width, 6 * LANES), bf16),
            ((edge, 2 * LANES), f32),
            ((edge, LANES), f32),
            ((edge, width), bf16),
        ],
        [sc, hidden_front, hidden_sib, hidden_edge, *qkv_units],
        flops=7 * MICROSECOND,
        limit=28,
    )
    mix_cross = lax.ppermute(mix_edge, "head", TO_EDGE)
    if ringed:
        rest_a = jnp.concatenate([rest_own, after(rest_far, mix_edge)], axis=0)
        rest_b = send(rest_a, hops[3])
        qf_ready = after(qf, rest_a)
    else:
        rest_a, rest_b, qf_ready = rest_whole[:8], rest_whole[8:], qf
    sib_a = lax.ppermute(rest_a, "head", CORE)
    attend = lambda rows: [
        ((rows, 2 * LANES), f32),
        ((rows, LANES), f32),
        ((rows, 2 * LANES), bf16),
    ]
    mixed32_sib, logs_sib, mix_for_sib = call(
        functools.partial(attend_kernel, local),
        "attend_sib",
        attend(local),
        [sc, qf_ready, kb, vb],
        flops=7 * MICROSECOND,
        limit=20,
    )
    mix_sib = lax.ppermute(mix_for_sib, "head", CORE)
    mix_edge = mix_edge + after(mix_cross, mix_for_sib)
    mix_swapped = lax.ppermute(mix_edge, "head", SWAP)
    mixed32_own, logs_own, mix_own = call(
        functools.partial(attend_kernel, 0),
        "attend_own",
        attend(local),
        [sc, after(qf_ready, mix_edge), kb, vb],
        flops=7 * MICROSECOND,
        limit=20,
    )
    sib_b = lax.ppermute(after(rest_b, mix_own), "head", CORE)
    (
        new_state,
        base,
        grad_own,
        grad_for_sib,
        edge_for_others,
        *low_rows,
    ) = call(
        middle_kernel,
        "middle",
        [
            ((local, width), bf16),
            ((local, width), f32),
            ((local, 2 * LANES), bf16),
            ((local, 2 * LANES), bf16),
            ((edge, width), bf16),
            ((local, width), bf16),
            ((local, width), bf16),
            ((local, hidden), bf16),
            ((local, width), bf16),
            ((local, hidden), bf16),
            ((local, width), bf16),
            ((16, width), f32),
        ],
        [
            sc,
            embedded,
            state_in,
            cotangent,
            halt_mask.reshape(local // LANES, LANES),
            mix_own,
            mix_sib,
            mix_swapped,
            rest_a,
            rest_b,
            sib_a,
            sib_b,
            halt_bias,
            norm1_gain[None],
            norm1_shift[None],
            norm2_gain[None],
            norm2_shift[None],
            halt_weight[None],
            ffn_out_bias[None],
            ffn_in_bias[None],
        ],
        scalars=(12,),
        scratch=[
            ((width, width), bf16),
            ((width, hidden), bf16),
            ((width, hidden), bf16),
            ((local, hidden), f32),
        ],
        flops=17 * MICROSECOND,
        limit=34,
    )
    grad_sib = lax.ppermute(grad_for_sib, "head", CORE)
    grad_swapped = lax.ppermute(edge_for_others, "head", SWAP)
    sum_own, sum_sib = call(
        weight_kernel,
        "weights",
        [((16 * UNIT + 16, unit_wide), bf16)] * 2,
        [sc, *low_rows],
        flops=5 * MICROSECOND,
        limit=28,
    )
    heads_t = ((4, HEAD_SIZE, window), f32)
    shared = [sc, qf, kb, vb, qt]

    def back(groups, name, *others):
        return call(
            functools.partial(back_kernel, groups),
            name,
            [((rows, 2 * LANES), bf16) for _, _, rows in groups] + [heads_t, heads_t],
            [*shared, *others],
            flops=sum(rows for _, _, rows in groups) * MICROSECOND // 60,
            limit=30,
        )

    early, late = 256, 128
    if ringed:
        sum_arrived = lax.ppermute(after(sum_sib, grad_sib), "head", CORE)
    dq_first, keys_t, values_t = back(
        ((0, 0, early),), "back_first", mixed32_own, logs_own, grad_own
    )
    grad_crossed = lax.ppermute(after(grad_swapped, dq_first), "head", FROM_EDGE)
    if ringed:
        empty = jnp.zeros((16, width), f32)
        leave, stay, sums = fold(sc, sum_own, after(sum_arrived, dq_first), empty, width)
        sum_arrived = send(leave, hops[3])
        grad_own = after(grad_own, stay)
    dq_own, dq_sib, keys_t, values_t = back(
        ((early, early, local - early), (local, 0, local - late)),
        "back_most",
        mixed32_own,
        logs_own,
        grad_own,
        mixed32_sib,
        logs_sib,
        grad_sib,
        keys_t,
        values_t,
    )
    if ringed:
        leave, stay, sums = fold(sc, stay, after(sum_arrived, dq_sib), sums, width)
        sum_arrived = send(leave, hops[2])
        grad_swapped = after(grad_swapped, stay)
    qkv_half = ((8, 3, UNIT, LANES), bf16)
    grad_projected, qkv_stay, qkv_leave = call(
        functools.partial(back_edge_kernel, late),
        "back_edge",
        [((window, 6 * LANES), bf16), qkv_half, qkv_half],
        [
            *shared,
            mixed32_edge,
            logs_edge,
            grad_swapped,
            grad_crossed,
            mixed32_sib,
            logs_sib,
            grad_sib,
            keys_t,
            values_t,
            dq_first,
            dq_own,
            dq_sib,
            hidden_own,
            hidden_sib,
            hidden_edge,
        ],
        scratch=[
            heads_t,
            heads_t,
            ((width, 6 * LANES), bf16),
            ((late, 2 * LANES), bf16),
            ((edge, 2 * LANES), bf16),
        ],
        flops=9 * MICROSECOND,
        limit=32,
    )
    if ringed:
        qkv_far = send(qkv_leave, qkv_hops[3])
        leave, stay, sums = fold(sc, stay, after(sum_arrived, qkv_leave), sums, width)
        sum_arrived = send(leave, hops[1])
        base = after(base, stay)
    state_own, state_sib, state_far = call(
        hidden_back_kernel,
        "hidden_back",
        [((local, width), f32), ((local, width), bf16), ((edge, width), bf16)],
        [sc, grad_projected, qkv_full, base],
        flops=3 * MICROSECOND,
        limit=20,
    )
    state_sib = lax.ppermute(state_sib, "head", CORE)
    state_cross = lax.ppermute(state_far, "head", TO_EDGE)
    if ringed:
        qkv_leave, qkv_stay = qkv_fold(sc, after(qkv_stay, state_own), qkv_far)
        qkv_far = send(qkv_leave, qkv_hops[2])
        state_cross = after(state_cross, qkv_leave)
    state_far = add(state_far, state_cross).astype(bf16)
    state_swapped = lax.ppermute(state_far, "head", SWAP)
    if ringed:
        leave, stay, sums = fold(sc, stay, after(sum_arrived, state_far), sums, width)
        sum_arrived = send(leave, hops[0])
        qkv_leave, qkv_stay = qkv_fold(sc, after(qkv_stay, stay), qkv_far)
        qkv_far = send(qkv_leave, qkv_hops[1])
        qkv_leave, qkv_stay = qkv_fold(sc, qkv_stay, qkv_far)
        qkv_far = send(qkv_leave, qkv_hops[0])
        state_own = after(state_own, qkv_leave)
    (grad_state,) = call(
        finish_kernel,
        "finish",
        [((local, width), f32)],
        [sc, state_own, state_sib, state_swapped],
        flops=2 * MICROSECOND,
        limit=16,
    )
    quarter = hidden // 4
    if ringed:
        grad_out, grad_in, grad_back, small = call(
            last_fold_kernel,
            "last_fold",
            [
                ((UNIT, LANES), f32),
                ((UNIT, quarter), f32),
                ((UNIT, quarter), f32),
                ((16, width), f32),
            ],
            [sc, stay, after(sum_arrived, grad_state), sums],
            flops=MICROSECOND,
            limit=16,
        )
        first = lax.ppermute(small, "head", [(0, 1), (2, 3)])
        small = jnp.where(c == 0, small, first)
        grad_qkv_weight = add(qkv_stay, qkv_far)[0]
    else:
        grad_qkv_weight, rest_grad, small = scatter_whole(
            [qkv_stay, qkv_leave], sum_own, sum_sib, width, x
        )
        grad_out = rest_grad[:, :LANES]
        grad_in = rest_grad[:, LANES : LANES + quarter]
        grad_back = rest_grad[:, LANES + quarter :]

    return (
        new_state,
        grad_state,
        grad_qkv_weight,
        grad_out,
        grad_in,
        grad_back,
        small[8 : 8 + hidden // width].reshape(hidden),
        small[0],
        small[1],
        small[2],
        small[3],
        small[4],
        small[5],
        small[6, 0:1],
    )


def unit_owners(orders):
    tables = []
    for order in orders:
        numbers = [
            sum(bit for place, bit in enumerate(order) if (unit >> place) & 1)
            for unit in range(16)
        ]
        tables.append([(number >> 2, (number >> 1) & 1) for number in numbers])
    return tables


def gather_whole(qkv_weight, rest, x, c):
    def both(array, axis):
        whole = lax.all_gather(array, "dp", axis=axis, tiled=True)
        other = lax.ppermute(whole, "head", ACROSS)
        return jnp.stack([whole, other])

    qkv, rest = both(qkv_weight, 1), both(rest, 0)
    width = rest.shape[1]
    qkv = qkv.reshape(2, 3, width // UNIT, UNIT, LANES)
    rest = rest.reshape(2, width // UNIT, UNIT, rest.shape[2])

    def units(array, orders):
        return jnp.where(
            c == 0, *(jnp.stack([array[ox, od] for od, ox in t]) for t in unit_owners(orders))
        )

    qkv = units(jnp.swapaxes(qkv, 1, 2), QKV_ORDERS)
    return [qkv[:8], qkv[8:]], units(rest, ORDERS)


def scatter_whole(qkv_sums, sum_own, sum_sib, width, x):
    c = lax.axis_index("head") % 2
    rows = 16 * UNIT
    rest = add(sum_own, lax.ppermute(sum_sib, "head", CORE))
    tail = rest[rows:]
    small = lax.psum(tail[:, :width] + tail[:, width : 2 * width], ("dp", "head")) * 0.5
    rest = rest[:rows].reshape(16, UNIT, rest.shape[1])
    qkv = jnp.concatenate(qkv_sums, axis=0).astype(f32)

    def order(orders, array):
        whole = []
        for table in unit_owners(orders):
            back = {owner_of: unit for unit, owner_of in enumerate(table)}
            whole.append(
                [jnp.stack([array[back[od, ox]] for od in range(8)]) for ox in range(2)]
            )
        return [jnp.where(c == 0, *pair) for pair in zip(*whole)]

    rest = [r.reshape(width, r.shape[2]) for r in order(ORDERS, rest)]
    qkv = [
        jnp.swapaxes(q, 0, 1).reshape(3, width, LANES) for q in order(QKV_ORDERS, qkv)
    ]
    rest = rest[0] + lax.ppermute(rest[1], "head", ACROSS)
    qkv = qkv[0] + lax.ppermute(qkv[1], "head", ACROSS)
    return (
        lax.psum_scatter(qkv, "dp", scatter_dimension=1, tiled=True),
        lax.psum_scatter(rest, "dp", scatter_dimension=0, tiled=True),
        small,
    )


def solution(mesh):
    tokens = P(("dp", "head"), None)
    weights = P("dp", "head")
    return jax.shard_map(
        body,
        mesh=mesh,
        in_specs=(
            tokens,
            P(None, "dp", "head"),
            weights,
            weights,
            weights,
            P(),
            P(),
            P(),
            P(),
            P(),
            P(),
            P(),
            P(),
            P("dp", None),
            P(("dp", "head")),
            tokens,
        ),
        out_specs=(
            tokens,
            tokens,
            P(None, "dp", "head"),
            weights,
            weights,
            weights,
            P(),
            P(),
            P(),
            P(),
            P(),
            P(),
            P(),
            P(),
        ),
        check_vma=False,
    )
```

```python
import functools
import math

import jax
import jax.numpy as jnp
from jax import lax
from jax.experimental import pallas as pl
from jax.experimental.pallas import tpu as pltpu
from jax.sharding import PartitionSpec as P

HEAD_SIZE = 64
STEP = 2
SEQ_MIN = 1024
LANES = 128
UNIT = 64
MICROSECOND = 1150 * 10**6

norm_epsilon = 1e-06
masked_score = -1e30
log2e = 1.4426950408889634

f32 = jnp.float32
bf16 = jnp.bfloat16
NT = (((1,), (1,)), ((), ()))
NN = (((1,), (0,)), ((), ()))
TN = (((0,), (0,)), ((), ()))

CORE = [(0, 1), (1, 0), (2, 3), (3, 2)]
ACROSS = [(0, 2), (2, 0), (1, 3), (3, 1)]

X, Y, Z0, Z1 = 2, 4, 8, 16
ORDERS = ((Z1, Z0, Y, X), (Z1, Y, X, Z0))
QKV_ORDERS = ((Z1, Z0, X, Y), (Z1, Z0, Y, X))

vmem = pl.BlockSpec(memory_space=pltpu.VMEM)
smem = pl.BlockSpec(memory_space=pltpu.SMEM)
hbm = pl.BlockSpec(memory_space=pltpu.HBM)


def mm(a, b, dims=NN):
    return lax.dot_general(a, b, dims, preferred_element_type=f32)


def call(
    kernel, name, outs, ins, scratch=(), flops=0, limit=56, scalars=(), scalars_out=(), far=(), copies=0
):
    def space(k):
        return smem if k == 0 or k in scalars else hbm if k in far else vmem

    return pl.pallas_call(
        kernel,
        name=name,
        out_shape=[jax.ShapeDtypeStruct(s, t) for s, t in outs],
        in_specs=[space(k) for k in range(len(ins))],
        out_specs=[smem if k in scalars_out else vmem for k in range(len(outs))],
        scratch_shapes=[pltpu.VMEM(s, t) for s, t in scratch]
        + ([pltpu.SemaphoreType.DMA((copies,))] if copies else []),
        compiler_params=pltpu.CompilerParams(vmem_limit_bytes=limit << 20),
        cost_estimate=pl.CostEstimate(flops=flops, bytes_accessed=0, transcendentals=0),
    )(*ins)


def send(array, bits):
    count = 4 * lax.axis_size("dp")
    pairs = [(i, i ^ bits[i & 1]) for i in range(count)]
    return lax.ppermute(array, ("dp", "head"), pairs)


def owner(unit, core, orders=ORDERS):
    found = []
    for order in orders:
        over_dp, over_x = 0, 0
        for place, bit in enumerate(order):
            flag = (unit >> place) & 1
            if bit == X:
                over_x = flag
            else:
                over_dp = over_dp + flag * (bit >> 2)
        found.append((over_dp, over_x))
    return (
        jnp.where(core == 0, found[0][0], found[1][0]),
        jnp.where(core == 0, found[0][1], found[1][1]),
    )


def unit_of(number, core, orders=ORDERS):
    found = [0, 0]
    for k, order in enumerate(orders):
        for place, bit in enumerate(order):
            found[k] = found[k] + ((number // bit) & 1) * (1 << place)
    return jnp.where(core == 0, found[0], found[1])


def window_start(sc, first):
    head, x, local = sc[1], sc[2], sc[5]
    return jnp.where(
        first < local,
        head * local + first,
        jnp.where(
            first < 2 * local,
            (head ^ 1) * local + first - local,
            first + jnp.where(x == 0, 0, SEQ_MIN - 2 * local),
        ),
    )


def window_token(sc, first, shape):
    return window_start(sc, first) + lax.broadcasted_iota(jnp.int32, shape, 0)


def window_valid(sc, first, shape):
    return jnp.where(window_token(sc, first, shape) < sc[0], 0, 1) == sc[2]


def lanes_of(shape):
    return lax.broadcasted_iota(jnp.int32, shape, 1)


def turns(fraction):
    square = fraction * fraction
    sine, cosine = 0.0, 0.0
    for k in range(8, -1, -1):
        sign = -1.0 if k % 2 else 1.0
        sine = sine * square + sign * (2 * math.pi) ** (2 * k + 1) / math.factorial(2 * k + 1)
        cosine = cosine * square + sign * (2 * math.pi) ** (2 * k) / math.factorial(2 * k)
    return sine * fraction, cosine


def embed_kernel(
    ids,
    segments_far,
    state_far,
    edge_here,
    edge_core,
    sc,
    embedded,
    hidden,
    hidden_edge,
    segments,
    state,
    arrived,
):
    copies = [
        pltpu.make_async_copy(far, near, arrived.at[k])
        for k, (far, near) in enumerate(((segments_far, segments), (state_far, state)))
    ]
    for copy in copies:
        copy.start()
    local, width = state.shape
    half = width // 2
    tall = LANES
    for k in range(1, 6):
        sc[k] = ids[k]
    order = lanes_of((1, half)).astype(f32)
    rates = jnp.exp(order * (-math.log(10000.0) / (half - 1))) * (0.5 / math.pi)

    def signal(places):
        turn = places * rates
        return turns(turn - jnp.floor(turn + 0.5))

    steps = signal(float(STEP))
    row = lax.broadcasted_iota(jnp.int32, (tall, half), 0)
    sine, cosine = signal(row.astype(f32))
    copies[0].wait()
    split = jnp.sum(jnp.where(segments[...] == 0, 1, 0))
    sc[0] = split
    copies[1].wait()
    for source, first in ((state, 0), (edge_here, 2 * local)):
        for start in range(0, source.shape[0], tall):
            rows = slice(start, start + tall)
            token = window_token(ids, first + start, (tall, half))
            begin = window_start(ids, first + start)
            early = token < split
            zero = signal(begin.astype(f32))
            one = signal((begin - split).astype(f32))
            base_sine = jnp.where(early, zero[0], one[0])
            base_cosine = jnp.where(early, zero[1], one[1])
            for side, value in (
                (0, base_sine * cosine + base_cosine * sine),
                (1, base_cosine * cosine - base_sine * sine),
            ):
                to = slice(side * half, (side + 1) * half)
                rows_in = source[rows, to].astype(f32)
                if source is edge_here:
                    rows_in = jnp.where(ids[2] == ids[3], rows_in, edge_core[rows, to].astype(f32))
                total = rows_in + (value + steps[side])
                if source is state:
                    embedded[rows, to] = total
                    hidden[rows, to] = total.astype(bf16)
                else:
                    hidden_edge[rows, to] = total.astype(bf16)


def attend_rows(rows, qf, kb, vb, mixed32, logs, mixed):
    tall = mixed.shape[0]
    lane = lanes_of((tall, LANES))
    log_totals = jnp.zeros((tall, LANES), f32)
    results = []
    for j in range(4):
        scores = mm(qf[j, rows, :], kb[j], NT)
        peak = jnp.max(scores, axis=1, keepdims=True)
        weights = jnp.exp2((scores - peak) * log2e).astype(bf16)
        summed = mm(weights, vb[j])
        log_totals = jnp.where(lane == 64 + j, peak + jnp.log(summed), log_totals)
        results.append(summed * (1.0 / pltpu.roll(summed, 64, 1)))
        if j % 2:
            both = jnp.where(lane < 64, results[j - 1], pltpu.roll(results[j], 64, 1))
            to = slice((j // 2) * LANES, (j // 2 + 1) * LANES)
            mixed32[:, to] = both
            mixed[:, to] = both.astype(bf16)
    logs[...] = log_totals


def front_kernel(
    sc,
    own,
    sib,
    edge,
    units_a,
    units_b,
    qf,
    kb,
    vb,
    qt,
    weight,
    mixed32,
    logs,
    mix_edge,
):
    x, c, dp = sc[2], sc[3], sc[4]
    for place, held in enumerate((units_a, units_b)):
        for sub in range(8):
            over_dp, over_x = owner(place * 8 + sub, c, QKV_ORDERS)
            row = pl.multiple_of((dp ^ over_dp) * UNIT, UNIT)
            for m in range(3):
                column = pl.multiple_of(m * 256 + (x ^ over_x) * LANES, LANES)
                weight[pl.ds(row, UNIT), pl.ds(column, LANES)] = held[sub, m]
    local = own.shape[0]
    for source, base in ((own, 0), (sib, local), (edge, 2 * local)):
        tall = 256 if source is edge else local
        lane = lanes_of((tall, LANES))

        def rows(index, carry, source=source, base=base, tall=tall, lane=lane):
            start = pl.multiple_of(index * tall, 128)
            out = pl.multiple_of(base + index * tall, 128)
            at = pl.ds(out, tall)
            projected = mm(source[pl.ds(start, tall), :], weight[...])
            valid = window_valid(sc, out, (tall, LANES))
            key_tail = jnp.where((lane == 64) & jnp.logical_not(valid), masked_score, 0.0)
            for p in range(2):
                blocks = [
                    projected[:, m * 256 + p * LANES : m * 256 + (p + 1) * LANES]
                    for m in range(3)
                ]
                blocks[0] = blocks[0] * 0.125
                qt[p, :, at] = jnp.transpose(blocks[0]).astype(bf16)
                for k in range(2):
                    if k:
                        blocks = [pltpu.roll(block, 64, 1) for block in blocks]
                    j = 2 * p + k
                    first = lane < 64
                    qf[j, at, :] = jnp.where(
                        first, blocks[0], jnp.where(lane == 64, 1.0, 0.0)
                    ).astype(bf16)
                    kb[j, at, :] = jnp.where(first, blocks[1], key_tail).astype(bf16)
                    vb[j, at, :] = jnp.where(first, blocks[2], 1.0).astype(bf16)
            return carry

        lax.fori_loop(0, source.shape[0] // tall, rows, 0)

    attend_rows(pl.ds(2 * local, mix_edge.shape[0]), qf, kb, vb, mixed32, logs, mix_edge)


def attend_kernel(first, sc, qf, kb, vb, mixed32, logs, mixed):
    attend_rows(pl.ds(first, mixed.shape[0]), qf, kb, vb, mixed32, logs, mixed)


def back_rows(sc, first, qf, kb, vb, qt, grad, mixed32, logs, part, before, keys_t, values_t, out):
    tall = part.size
    lane = lanes_of((tall, LANES))
    valid = window_valid(sc, first, (tall, LANES))
    rows = pl.ds(first, tall)
    for p in range(2):
        to = slice(p * LANES, (p + 1) * LANES)
        incoming = jnp.where(valid, grad(part, p), 0.0)
        product = incoming * mixed32[part, to]
        incoming_t = jnp.transpose(incoming).astype(bf16)
        grad_queries = []
        for k in range(2):
            j = 2 * p + k
            half = (lane < 64) if k == 0 else (lane >= 64)
            delta = jnp.sum(jnp.where(half, product, 0.0), axis=1, keepdims=True)
            log_total = logs[part, 64 + j : 65 + j] * log2e
            arriving = incoming if k == 0 else pltpu.roll(incoming, 64, 1)
            arriving = jnp.where(lane < 64, arriving, 0.0).astype(bf16)
            probs = jnp.exp2(mm(qf[j, rows, :], kb[j], NT) * log2e - log_total)
            grad_probs = mm(arriving, vb[j], NT)
            grad_scores = (probs * (grad_probs - delta)).astype(bf16)
            piece = slice(64 * k, 64 * k + 64)
            values = mm(incoming_t[piece, :], probs.astype(bf16))
            keys = mm(qt[p, piece, rows], grad_scores)
            keys_t[j] = before[0][j] + keys if before else keys
            values_t[j] = before[1][j] + values if before else values
            grad_queries.append(mm(grad_scores, kb[j]) * 0.125)
        out[:, to] = jnp.where(
            lane < 64, grad_queries[0], pltpu.roll(grad_queries[1], 64, 1)
        ).astype(bf16)


def back_kernel(groups, sc, qf, kb, vb, qt, *rest):
    count = len(groups)
    before, (keys_t, values_t) = rest[3 * count : -count - 2], rest[-2:]
    for k, (first, start, rows) in enumerate(groups):
        mixed32, logs, grad = rest[3 * k : 3 * k + 3]
        back_rows(
            sc,
            first,
            qf,
            kb,
            vb,
            qt,
            lambda part, p, grad=grad: grad[part, p * LANES : (p + 1) * LANES].astype(f32),
            mixed32,
            logs,
            pl.ds(start, rows),
            before,
            keys_t,
            values_t,
            rest[k - count - 2],
        )
        before = (keys_t, values_t)


def back_edge_kernel(
    late,
    sc,
    qf,
    kb,
    vb,
    qt,
    mixed32,
    logs,
    edge_here,
    edge_core,
    mixed32_sib,
    logs_sib,
    grad_sib,
    keys_in,
    values_in,
    dq_first,
    dq_own,
    dq_sib,
    own,
    sib,
    edge,
    out,
    stay,
    leave,
    keys_t,
    values_t,
    full,
    dq_late,
    dq_edge,
):
    x, c, dp = sc[2], sc[3], sc[4]
    local = own.shape[0]
    before = (keys_in, values_in)

    def from_sib(part, p):
        return grad_sib[part, p * LANES : (p + 1) * LANES].astype(f32)

    def from_edge(part, p):
        there, here = slice(p * LANES, (p + 1) * LANES), slice((p + 2) * LANES, (p + 3) * LANES)
        return jnp.where(
            x == c, edge_here[part, here].astype(f32), edge_core[part, there].astype(f32)
        )

    for first, part, operands, target in (
        (2 * local - late, pl.ds(local - late, late), (from_sib, mixed32_sib, logs_sib), dq_late),
        (2 * local, pl.ds(0, edge.shape[0]), (from_edge, mixed32, logs), dq_edge),
    ):
        back_rows(
            sc, first, qf, kb, vb, qt, *operands, part, before, keys_t, values_t, target
        )
        before = (keys_t, values_t)
    at = 0
    for piece in (dq_first, dq_own, dq_sib, dq_late, dq_edge):
        out[at : at + piece.shape[0], 0:256] = piece[...]
        at += piece.shape[0]
    for m, held in ((1, keys_t), (2, values_t)):
        for p in range(2):
            pair = jnp.concatenate([held[2 * p], held[2 * p + 1]], axis=0)
            to = slice(m * 256 + p * LANES, m * 256 + (p + 1) * LANES)
            out[:, to] = jnp.transpose(pair).astype(bf16)
    for m in range(3):
        to = slice(m * 256, (m + 1) * 256)
        total = 0.0
        for source, base in ((own, 0), (sib, local), (edge, 2 * local)):
            total += mm(source[...], out[base : base + source.shape[0], to], TN)
        full[:, to] = total.astype(bf16)
    for place, target in enumerate((stay, leave)):
        for sub in range(8):
            over_dp, over_x = owner(place * 8 + sub, c, QKV_ORDERS)
            row = pl.multiple_of((dp ^ over_dp) * UNIT, UNIT)
            for m in range(3):
                column = pl.multiple_of(m * 256 + (x ^ over_x) * LANES, LANES)
                target[sub, m] = full[pl.ds(row, UNIT), pl.ds(column, LANES)]


def norm_parts(rows):
    width = rows.shape[1]
    center = rows - jnp.sum(rows, axis=1, keepdims=True) * (1.0 / width)
    spread = jnp.sum(center * center, axis=1, keepdims=True) * (1.0 / width)
    scale = lax.rsqrt(spread + norm_epsilon)
    return center * scale, scale


def norm_back(normed, scale, gain, incoming):
    width = normed.shape[1]
    e = incoming * gain
    mean_e = jnp.sum(e, axis=1, keepdims=True) * (1.0 / width)
    mean_en = jnp.sum(e * normed, axis=1, keepdims=True) * (1.0 / width)
    return (e - mean_e - normed * mean_en) * scale


def middle_kernel(
    sc,
    embedded,
    state,
    cotangent,
    running,
    mix_own,
    mix_sib,
    edge_own,
    edge_sib,
    own_a,
    own_b,
    sib_a,
    sib_b,
    halt_offset,
    gain_one,
    shift_one,
    gain_two,
    shift_two,
    halt_vector,
    bias_out,
    bias_in,
    new_state,
    base,
    grad_own,
    grad_sib,
    grad_edge,
    mixed,
    first_low,
    active,
    grad_out_low,
    grad_inner,
    grad_branch,
    sums,
    w_out,
    w_in,
    w_back,
    slope,
):
    head, x, c, dp = sc[1], sc[2], sc[3], sc[4]
    hidden = w_in.shape[1]
    width = w_out.shape[0]
    hidden_block = hidden // 4
    units = 16

    def unit_place(unit, core):
        over_dp, over_x = owner(unit, core)
        rows = pl.ds(pl.multiple_of((dp ^ over_dp) * UNIT, UNIT), UNIT)
        block = (x ^ over_x) * 2 + core
        narrow = pl.ds(pl.multiple_of(block * LANES, LANES), LANES)
        wide = pl.ds(pl.multiple_of(block * hidden_block, hidden_block), hidden_block)
        return rows, narrow, wide

    for held, first_unit, core in (
        (own_a, 0, c),
        (own_b, 8, c),
        (sib_a, 0, 1 - c),
        (sib_b, 8, 1 - c),
    ):

        def place(unit, carry, held=held, first_unit=first_unit, core=core):
            rows, narrow, wide = unit_place(unit + first_unit, core)
            w_out[rows, narrow] = held[unit, :, 0:LANES]
            w_in[rows, wide] = held[unit, :, LANES : LANES + hidden_block]
            w_back[rows, wide] = held[unit, :, LANES + hidden_block :]
            return carry

        lax.fori_loop(0, units // 2, place, 0)
    rows_all = embedded.shape[0]
    edge_rows = edge_own.shape[0]
    at = pl.multiple_of(jnp.where(x == 0, rows_all - edge_rows, 0), 128)
    edge_at = pl.ds(at, edge_rows)
    token = lax.broadcasted_iota(jnp.int32, (edge_rows, LANES), 0) + at + head * rows_all
    elsewhere = jnp.where(token < sc[0], 0, 1) != x
    for p in range(2):
        part = slice(p * LANES, (p + 1) * LANES)
        for held, edge, core in ((mix_own, edge_own, c), (mix_sib, edge_sib, 1 - c)):
            lanes = pl.ds(pl.multiple_of((2 * p + core) * LANES, LANES), LANES)
            mixed[:, lanes] = held[:, part]
            mixed[edge_at, lanes] = jnp.where(elsewhere, edge[:, part], mixed[edge_at, lanes])

    diagonal = lax.broadcasted_iota(jnp.int32, (LANES, LANES), 0) == lanes_of((LANES, LANES))
    run_all = jnp.concatenate(
        [
            jnp.sum(
                jnp.where(diagonal, running[k : k + 1, :].astype(f32), 0.0), axis=1, keepdims=True
            )
            for k in range(running.shape[0])
        ],
        axis=0,
    )
    gains = tuple(
        g[...] for g in (gain_one, shift_one, gain_two, shift_two, halt_vector, bias_out)
    )
    tall = rows_all // 2
    for start in range(0, rows_all, tall):
        rows = slice(start, start + tall)

        def total(row, value, lanes=slice(None), start=start):
            value = jnp.sum(value, axis=0, keepdims=True)
            at_row = (slice(row, row + 1), lanes)
            sums[at_row] = value if start == 0 else sums[at_row] + value

        middle_rows(
            rows,
            total,
            run_all[rows, :],
            halt_offset[0],
            gains,
            bias_in,
            embedded,
            state,
            cotangent,
            new_state,
            base,
            grad_own,
            grad_sib,
            mixed,
            first_low,
            active,
            grad_out_low,
            grad_inner,
            grad_branch,
            w_out,
            w_in,
            w_back,
            slope,
            c,
        )
    sums[7:8, :] = jnp.zeros_like(sums[7:8, :])
    sums[12:, :] = jnp.zeros_like(sums[12:, :])
    grad_edge[:, 0 : 2 * LANES] = grad_sib[edge_at, :]
    grad_edge[:, 2 * LANES :] = grad_own[edge_at, :]


def middle_rows(
    rows,
    total,
    run,
    halt_offset,
    gains,
    bias_in,
    embedded,
    state,
    cotangent,
    new_state,
    base,
    grad_own,
    grad_sib,
    mixed,
    first_low,
    active,
    grad_out_low,
    grad_inner,
    grad_branch,
    w_out,
    w_in,
    w_back,
    slope,
    c,
):
    gain_one, shift_one, gain_two, shift_two, halt_vector, bias_out = gains
    width = w_out.shape[0]
    branch = mm(mixed[rows, :], w_out[...], NT)
    normed_one, scale_one = norm_parts(embedded[rows, :] + branch)
    first = normed_one * gain_one + shift_one
    low = first.astype(bf16)
    first_low[rows, :] = low
    chunk = 256
    steps = w_in.shape[1] // chunk
    k0 = math.sqrt(2.0 / math.pi)

    outward = first + bias_out
    for index in range(steps):
        cols = slice(index * chunk, (index + 1) * chunk)
        u = mm(low, w_in[:, cols]) + bias_in[:, cols]
        square = u * u
        t = jnp.tanh(k0 * u * (1.0 + 0.044715 * square))
        half = 0.5 * (1.0 + t)
        act = (u * half).astype(bf16)
        active[rows, cols] = act
        slope[rows, cols] = half + 0.5 * u * (1.0 - t * t) * (k0 * (1.0 + 3 * 0.044715 * square))
        outward = outward + mm(act, w_back[:, cols], NT)
    normed_two, scale_two = norm_parts(outward)
    second = normed_two * gain_two + shift_two
    halting = jax.nn.sigmoid(jnp.sum(second * halt_vector, axis=1, keepdims=True) + halt_offset)
    rows_in = state[rows, :].astype(f32)
    difference = second - rows_in
    share = run * halting
    new_state[rows, :] = (rows_in + share * difference).astype(bf16)
    g = cotangent[rows, :].astype(f32)
    carry_c = jnp.sum(g * difference, axis=1, keepdims=True)
    push = share * (1.0 - halting) * carry_c
    grad_second = share * g + push * halt_vector
    total(5, push * second)
    total(6, jnp.broadcast_to(push, second.shape))
    total(3, grad_second * normed_two)
    total(4, grad_second)
    grad_outward = norm_back(normed_two, scale_two, gain_two, grad_second)
    total(0, grad_outward)
    out_low = grad_outward.astype(bf16)
    grad_out_low[rows, :] = out_low

    grad_first = grad_outward
    for index in range(steps):
        cols = slice(index * chunk, (index + 1) * chunk)
        gi = (mm(out_low, w_back[:, cols]) * slope[rows, cols]).astype(bf16)
        grad_inner[rows, cols] = gi
        lane0 = (index * chunk) % width
        total(8 + (index * chunk) // width, gi.astype(f32), slice(lane0, lane0 + chunk))
        grad_first = grad_first + mm(gi, w_in[:, cols], NT)
    total(1, grad_first * normed_one)
    total(2, grad_first)
    grad_resid = norm_back(normed_one, scale_one, gain_one, grad_first)
    base[rows, :] = grad_resid + (1.0 - share) * g
    branch_low = grad_resid.astype(bf16)
    grad_branch[rows, :] = branch_low
    grad_mixed = mm(branch_low, w_out[...]).astype(bf16)
    for p in range(2):
        blocks = [grad_mixed[:, (2 * p + k) * LANES : (2 * p + k + 1) * LANES] for k in range(2)]
        to = slice(p * LANES, (p + 1) * LANES)
        grad_own[rows, to] = jnp.where(c == 0, blocks[0], blocks[1])
        grad_sib[rows, to] = jnp.where(c == 0, blocks[1], blocks[0])


def weight_kernel(
    sc, mixed, first_low, active, grad_out_low, grad_inner, grad_branch, sums, sum_own, sum_sib
):
    x, c, dp = sc[2], sc[3], sc[4]
    width = mixed.shape[1]
    hidden_block = active.shape[1] // 4
    units = 16
    turned_branch = jnp.transpose(grad_branch[...])
    turned_first = jnp.transpose(first_low[...])
    turned_out = jnp.transpose(grad_out_low[...])
    high = sums[...].astype(bf16)
    low = (sums[...] - high.astype(f32)).astype(bf16)
    for out, core in ((sum_sib, 1 - c), (sum_own, c)):
        for over_x in range(2):
            block = (x ^ over_x) * 2 + core
            narrow = pl.ds(pl.multiple_of(block * LANES, LANES), LANES)
            wide = pl.ds(pl.multiple_of(block * hidden_block, hidden_block), hidden_block)
            for turned, source, lanes, lane0 in (
                (turned_branch, mixed, narrow, 0),
                (turned_first, grad_inner, wide, LANES),
                (turned_out, active, wide, LANES + hidden_block),
            ):
                value = mm(turned, source[:, lanes]).astype(bf16)
                for k in range(width // UNIT):
                    unit = unit_of((dp ^ k) * 4 + over_x * X, core)
                    to = pl.ds(pl.multiple_of(unit * UNIT, UNIT), UNIT)
                    out[to, lane0 : lane0 + value.shape[1]] = value[k * UNIT : (k + 1) * UNIT, :]
        tail = slice(units * UNIT, units * UNIT + 16)
        out[tail, 0:width] = high
        out[tail, width : 2 * width] = low
        out[tail, 2 * width :] = jnp.zeros_like(out[tail, 2 * width :])


def hidden_back_kernel(sc, grads, weight, base, own, sib, edge):
    local = own.shape[0]
    for target, first, tall in ((sib, local, 320), (edge, 2 * local, 256), (own, 0, 320)):

        def rows(index, carry, target=target, first=first, tall=tall):
            start = pl.multiple_of(index * tall, 64)
            at = pl.ds(pl.multiple_of(first + index * tall, 64), tall)
            value = mm(grads[at, :], weight[...], NT)
            to = pl.ds(start, tall)
            if target is own:
                target[to, :] = value + base[to, :]
            else:
                target[to, :] = value.astype(bf16)
            return carry

        lax.fori_loop(0, target.shape[0] // tall, rows, 0)


def finish_kernel(sc, own, sib, edge_here, edge_core, out):
    out[...] = own[...] + sib[...].astype(f32)
    rows = edge_here.shape[0]
    at = pl.ds(pl.multiple_of(jnp.where(sc[2] == 0, out.shape[0] - rows, 0), 128), rows)
    edge = edge_here[...].astype(f32) + edge_core[...].astype(f32)
    out[at, :] += jnp.where(sc[2] == sc[3], 0.0, edge)


def split_tail(rows, width):
    return rows[:, :width].astype(f32) + rows[:, width : 2 * width].astype(f32)


def fold_kernel(sc, own, arrived, sums_in, leave, stay, sums):
    width = sums.shape[1]
    rows = own.shape[0]
    half = stay.shape[0]
    stay[...] = (own[0:half, :].astype(f32) + arrived[0:half, :].astype(f32)).astype(bf16)
    leave[0:half, :] = (
        own[half : 2 * half, :].astype(f32) + arrived[half : 2 * half, :].astype(f32)
    ).astype(bf16)
    if rows == 2 * half:
        mine = sums_in[...]
    else:
        mine = split_tail(own[2 * half :, :], width)
    total = mine + split_tail(arrived[2 * half :, :], width)
    high = total.astype(bf16)
    low = (total - high.astype(f32)).astype(bf16)
    leave[half:, 0:width] = high
    leave[half:, width : 2 * width] = low
    leave[half:, 2 * width :] = jnp.zeros_like(leave[half:, 2 * width :])
    sums[...] = high.astype(f32) + low.astype(f32)


def last_fold_kernel(sc, own, arrived, sums_in, out_part, in_part, back_part, sums):
    width = sums.shape[1]
    rows = own.shape[0]
    total = own[...].astype(f32) + arrived[0:rows, :].astype(f32)
    hidden_block = in_part.shape[1]
    out_part[...] = total[:, :LANES]
    in_part[...] = total[:, LANES : LANES + hidden_block]
    back_part[...] = total[:, LANES + hidden_block :]
    sums[...] = sums_in[...] + split_tail(arrived[rows:, :], width)


def fold(sc, own, arrived, sums, width):
    half = (arrived.shape[0] - 16) // 2
    wide = own.shape[1]
    return call(
        fold_kernel,
        "fold",
        [((half + 16, wide), bf16), ((half, wide), bf16), ((16, width), f32)],
        [sc, own, arrived, sums],
        limit=16,
    )


def qkv_fold_kernel(sc, own, arrived, leave, stay):
    half = stay.shape[0]
    total = own[...].astype(f32) + arrived[...].astype(f32)
    stay[...] = total[0:half].astype(bf16)
    leave[...] = total[half:].astype(bf16)


def qkv_fold(sc, own, arrived):
    half = ((own.shape[0] // 2, *own.shape[1:]), bf16)
    return call(
        qkv_fold_kernel, "qkv_fold", [half, half], [sc, own, arrived], limit=16
    )


def add(a, b):
    return a.astype(f32) + b.astype(f32)


def after(array, *others):
    return lax.optimization_barrier((array, *others))[0]


def body(
    state_in,
    qkv_weight,
    out_weight,
    ffn_in_weight,
    ffn_out_weight,
    ffn_in_bias,
    ffn_out_bias,
    norm1_gain,
    norm1_shift,
    norm2_gain,
    norm2_shift,
    halt_weight,
    halt_bias,
    seg_ids,
    halt_mask,
    cotangent,
):
    dp = lax.axis_index("dp")
    head = lax.axis_index("head")
    x, c = head // 2, head % 2
    local, width = state_in.shape
    window = 4 * local - SEQ_MIN
    edge = window - 2 * local
    hidden = ffn_in_bias.shape[0]
    unit_wide = LANES + 2 * (hidden // 4)
    ringed = qkv_weight.shape[1] == UNIT and lax.axis_size("dp") == 8

    ids = jnp.stack([0 * dp, head, x, c, dp if ringed else 0 * dp, 0 * dp + local])
    ids = ids.astype(jnp.int32)
    at = jnp.where(x == 0, local - edge, 0)
    hops, qkv_hops = list(zip(*ORDERS)), list(zip(*QKV_ORDERS))
    rest = jnp.concatenate([out_weight, ffn_in_weight, ffn_out_weight], axis=1)
    edge_rows = lax.dynamic_slice_in_dim(state_in, at, edge)
    edge_here = lax.ppermute(edge_rows, "head", ACROSS)
    if ringed:
        rest_own = rest[None]
        rest_far = send(rest_own, hops[0])
        qkv_far = send(qkv_weight[None], qkv_hops[0])
        held = jnp.concatenate([qkv_weight[None], after(qkv_far, rest_own, edge_rows)], axis=0)
        qkv_far = send(held, qkv_hops[1])
        edge_here = after(edge_here, held)
    edge_core = lax.ppermute(edge_here, "head", CORE)
    sc, embedded, hidden_own, hidden_edge = call(
        embed_kernel,
        "embed",
        [
            ((6,), jnp.int32),
            ((local, width), f32),
            ((local, width), bf16),
            ((edge, width), bf16),
        ],
        [ids, seg_ids, state_in, edge_here, edge_core],
        scratch=[(seg_ids.shape, jnp.int32), (state_in.shape, bf16)],
        flops=2 * MICROSECOND,
        limit=20,
        scalars_out=(0,),
        far=(1, 2),
        copies=2,
    )
    hidden_sib = lax.ppermute(hidden_own, "head", CORE)
    if ringed:
        held = jnp.concatenate([held, after(qkv_far, hidden_edge)], axis=0)
        qkv_far = send(held, qkv_hops[2])
        rest_own = jnp.concatenate([rest_own, after(rest_far, held)], axis=0)
        rest_far = send(rest_own, hops[1])
        held = jnp.concatenate([held, after(qkv_far, rest_own)], axis=0)
        qkv_units = [held, send(held, qkv_hops[3])]
        rest_own = jnp.concatenate([rest_own, after(rest_far, held)], axis=0)
        rest_far = send(rest_own, hops[2])
        hidden_front = after(hidden_own, rest_own)
    else:
        qkv_units, rest_whole = gather_whole(qkv_weight, rest, x, c)
        hidden_front = hidden_own

    wide = ((4, window, LANES), bf16)
    qf, kb, vb, qt, qkv_full, mixed32_edge, logs_edge, mix_edge = call(
        front_kernel,
        "front",
        [
            wide,
            wide,
            wide,
            ((2, LANES, window), bf16),
            ((width, 6 * LANES), bf16),
            ((edge, 2 * LANES), f32),
            ((edge, LANES), f32),
            ((edge, 2 * LANES), bf16),
        ],
        [sc, hidden_front, hidden_sib, hidden_edge, *qkv_units],
        flops=7 * MICROSECOND,
        limit=28,
    )
    edge_own = lax.ppermute(mix_edge, "head", ACROSS)
    if ringed:
        rest_a = jnp.concatenate([rest_own, after(rest_far, mix_edge)], axis=0)
        rest_b = send(rest_a, hops[3])
        qf_ready = after(qf, rest_a)
    else:
        rest_a, rest_b, qf_ready = rest_whole[:8], rest_whole[8:], qf
    sib_a = lax.ppermute(rest_a, "head", CORE)
    attend = lambda rows: [
        ((rows, 2 * LANES), f32),
        ((rows, LANES), f32),
        ((rows, 2 * LANES), bf16),
    ]
    mixed32_sib, logs_sib, mix_for_sib = call(
        functools.partial(attend_kernel, local),
        "attend_sib",
        attend(local),
        [sc, qf_ready, kb, vb],
        flops=7 * MICROSECOND,
        limit=20,
    )
    mix_sib = lax.ppermute(mix_for_sib, "head", CORE)
    edge_sib = lax.ppermute(after(edge_own, mix_for_sib), "head", CORE)
    mixed32_own, logs_own, mix_own = call(
        functools.partial(attend_kernel, 0),
        "attend_own",
        attend(local),
        [sc, after(qf_ready, mix_for_sib), kb, vb],
        flops=7 * MICROSECOND,
        limit=20,
    )
    sib_b = lax.ppermute(after(rest_b, mix_own, mix_sib, edge_sib), "head", CORE)
    (
        new_state,
        base,
        grad_own,
        grad_for_sib,
        edge_for_others,
        *low_rows,
    ) = call(
        middle_kernel,
        "middle",
        [
            ((local, width), bf16),
            ((local, width), f32),
            ((local, 2 * LANES), bf16),
            ((local, 2 * LANES), bf16),
            ((edge, width), bf16),
            ((local, width), bf16),
            ((local, width), bf16),
            ((local, hidden), bf16),
            ((local, width), bf16),
            ((local, hidden), bf16),
            ((local, width), bf16),
            ((16, width), f32),
        ],
        [
            sc,
            embedded,
            state_in,
            cotangent,
            halt_mask.reshape(local // LANES, LANES),
            mix_own,
            mix_sib,
            edge_own,
            edge_sib,
            rest_a,
            rest_b,
            sib_a,
            sib_b,
            halt_bias,
            norm1_gain[None],
            norm1_shift[None],
            norm2_gain[None],
            norm2_shift[None],
            halt_weight[None],
            ffn_out_bias[None],
            ffn_in_bias[None],
        ],
        scalars=(13,),
        scratch=[
            ((width, width), bf16),
            ((width, hidden), bf16),
            ((width, hidden), bf16),
            ((local, hidden), f32),
        ],
        flops=13 * MICROSECOND,
        limit=26,
    )
    grad_sib = lax.ppermute(grad_for_sib, "head", CORE)
    grad_here = lax.ppermute(edge_for_others, "head", ACROSS)
    sum_own, sum_sib = call(
        weight_kernel,
        "weights",
        [((16 * UNIT + 16, unit_wide), bf16)] * 2,
        [sc, *low_rows],
        flops=5 * MICROSECOND,
        limit=28,
    )
    heads_t = ((4, HEAD_SIZE, window), f32)
    shared = [sc, qf, kb, vb, qt]

    def back(groups, name, *others):
        return call(
            functools.partial(back_kernel, groups),
            name,
            [((rows, 2 * LANES), bf16) for _, _, rows in groups] + [heads_t, heads_t],
            [*shared, *others],
            flops=sum(rows for _, _, rows in groups) * MICROSECOND // 60,
            limit=30,
        )

    early, late = 256, 128
    if ringed:
        sum_arrived = lax.ppermute(after(sum_sib, grad_sib), "head", CORE)
    dq_first, keys_t, values_t = back(
        ((0, 0, early),), "back_first", mixed32_own, logs_own, grad_own
    )
    if ringed:
        empty = jnp.zeros((16, width), f32)
        leave, stay, sums = fold(sc, sum_own, after(sum_arrived, dq_first), empty, width)
        sum_arrived = send(leave, hops[3])
        grad_own = after(grad_own, stay)
    dq_own, dq_sib, keys_t, values_t = back(
        ((early, early, local - early), (local, 0, local - late)),
        "back_most",
        mixed32_own,
        logs_own,
        grad_own,
        mixed32_sib,
        logs_sib,
        grad_sib,
        keys_t,
        values_t,
    )
    if ringed:
        leave, stay, sums = fold(sc, stay, after(sum_arrived, dq_sib), sums, width)
        sum_arrived = send(leave, hops[2])
        qf_last = after(qf, stay)
    else:
        qf_last = qf
    grad_core = lax.ppermute(after(grad_here, dq_sib), "head", CORE)
    qkv_half = ((8, 3, UNIT, LANES), bf16)
    grad_projected, qkv_stay, qkv_leave = call(
        functools.partial(back_edge_kernel, late),
        "back_edge",
        [((window, 6 * LANES), bf16), qkv_half, qkv_half],
        [
            sc,
            qf_last,
            *shared[2:],
            mixed32_edge,
            logs_edge,
            grad_here,
            grad_core,
            mixed32_sib,
            logs_sib,
            grad_sib,
            keys_t,
            values_t,
            dq_first,
            dq_own,
            dq_sib,
            hidden_own,
            hidden_sib,
            hidden_edge,
        ],
        scratch=[
            heads_t,
            heads_t,
            ((width, 6 * LANES), bf16),
            ((late, 2 * LANES), bf16),
            ((edge, 2 * LANES), bf16),
        ],
        flops=9 * MICROSECOND,
        limit=32,
    )
    if ringed:
        qkv_far = send(qkv_leave, qkv_hops[3])
        leave, stay, sums = fold(sc, stay, after(sum_arrived, qkv_leave), sums, width)
        sum_arrived = send(leave, hops[1])
        base = after(base, stay)
    state_own, state_sib, state_far = call(
        hidden_back_kernel,
        "hidden_back",
        [((local, width), f32), ((local, width), bf16), ((edge, width), bf16)],
        [sc, grad_projected, qkv_full, base],
        flops=3 * MICROSECOND,
        limit=20,
    )
    state_sib = lax.ppermute(state_sib, "head", CORE)
    if ringed:
        leave, stay, sums = fold(sc, stay, after(sum_arrived, state_own, qkv_far), sums, width)
        sum_arrived = send(leave, hops[0])
        qkv_leave, qkv_stay = qkv_fold(sc, after(qkv_stay, stay), qkv_far)
        qkv_far = send(qkv_leave, qkv_hops[2])
        qkv_leave, qkv_stay = qkv_fold(sc, qkv_stay, qkv_far)
        qkv_far = send(qkv_leave, qkv_hops[1])
        state_far = after(state_far, qkv_leave)
        qkv_leave, qkv_stay = qkv_fold(sc, qkv_stay, qkv_far)
        qkv_far = send(qkv_leave, qkv_hops[0])
        sum_arrived = after(sum_arrived, qkv_leave)
    state_here = lax.ppermute(state_far, "head", ACROSS)
    quarter = hidden // 4
    if ringed:
        grad_out, grad_in, grad_back, small = call(
            last_fold_kernel,
            "last_fold",
            [
                ((UNIT, LANES), f32),
                ((UNIT, quarter), f32),
                ((UNIT, quarter), f32),
                ((16, width), f32),
            ],
            [sc, stay, sum_arrived, sums],
            limit=16,
        )
        state_own = after(state_own, grad_out)
        first = lax.ppermute(small, "head", [(0, 1), (2, 3)])
        small = jnp.where(c == 0, small, first)
    else:
        grad_qkv_weight, rest_grad, small = scatter_whole(
            [qkv_stay, qkv_leave], sum_own, sum_sib, width, x
        )
        grad_out = rest_grad[:, :LANES]
        grad_in = rest_grad[:, LANES : LANES + quarter]
        grad_back = rest_grad[:, LANES + quarter :]

    state_core = lax.ppermute(state_here, "head", CORE)
    (grad_state,) = call(
        finish_kernel,
        "finish",
        [((local, width), f32)],
        [sc, state_own, state_sib, state_here, state_core],
        limit=16,
    )
    if ringed:
        grad_qkv_weight = add(after(qkv_stay, grad_state), qkv_far)[0]
    return (
        new_state,
        grad_state,
        grad_qkv_weight,
        grad_out,
        grad_in,
        grad_back,
        small[8 : 8 + hidden // width].reshape(hidden),
        small[0],
        small[1],
        small[2],
        small[3],
        small[4],
        small[5],
        small[6, 0:1],
    )


def unit_owners(orders):
    tables = []
    for order in orders:
        numbers = [
            sum(bit for place, bit in enumerate(order) if (unit >> place) & 1)
            for unit in range(16)
        ]
        tables.append([(number >> 2, (number >> 1) & 1) for number in numbers])
    return tables


def gather_whole(qkv_weight, rest, x, c):
    def both(array, axis):
        whole = lax.all_gather(array, "dp", axis=axis, tiled=True)
        other = lax.ppermute(whole, "head", ACROSS)
        return jnp.stack([whole, other])

    qkv, rest = both(qkv_weight, 1), both(rest, 0)
    width = rest.shape[1]
    qkv = qkv.reshape(2, 3, width // UNIT, UNIT, LANES)
    rest = rest.reshape(2, width // UNIT, UNIT, rest.shape[2])

    def units(array, orders):
        return jnp.where(
            c == 0, *(jnp.stack([array[ox, od] for od, ox in t]) for t in unit_owners(orders))
        )

    qkv = units(jnp.swapaxes(qkv, 1, 2), QKV_ORDERS)
    return [qkv[:8], qkv[8:]], units(rest, ORDERS)


def scatter_whole(qkv_sums, sum_own, sum_sib, width, x):
    c = lax.axis_index("head") % 2
    rows = 16 * UNIT
    rest = add(sum_own, lax.ppermute(sum_sib, "head", CORE))
    tail = rest[rows:]
    small = lax.psum(tail[:, :width] + tail[:, width : 2 * width], ("dp", "head")) * 0.5
    rest = rest[:rows].reshape(16, UNIT, rest.shape[1])
    qkv = jnp.concatenate(qkv_sums, axis=0).astype(f32)

    def order(orders, array):
        whole = []
        for table in unit_owners(orders):
            back = {owner_of: unit for unit, owner_of in enumerate(table)}
            whole.append(
                [jnp.stack([array[back[od, ox]] for od in range(8)]) for ox in range(2)]
            )
        return [jnp.where(c == 0, *pair) for pair in zip(*whole)]

    rest = [r.reshape(width, r.shape[2]) for r in order(ORDERS, rest)]
    qkv = [
        jnp.swapaxes(q, 0, 1).reshape(3, width, LANES) for q in order(QKV_ORDERS, qkv)
    ]
    rest = rest[0] + lax.ppermute(rest[1], "head", ACROSS)
    qkv = qkv[0] + lax.ppermute(qkv[1], "head", ACROSS)
    return (
        lax.psum_scatter(qkv, "dp", scatter_dimension=1, tiled=True),
        lax.psum_scatter(rest, "dp", scatter_dimension=0, tiled=True),
        small,
    )


def solution(mesh):
    tokens = P(("dp", "head"), None)
    weights = P("dp", "head")
    return jax.shard_map(
        body,
        mesh=mesh,
        in_specs=(
            tokens,
            P(None, "dp", "head"),
            weights,
            weights,
            weights,
            P(),
            P(),
            P(),
            P(),
            P(),
            P(),
            P(),
            P(),
            P("dp", None),
            P(("dp", "head")),
            tokens,
        ),
        out_specs=(
            tokens,
            tokens,
            P(None, "dp", "head"),
            weights,
            weights,
            weights,
            P(),
            P(),
            P(),
            P(),
            P(),
            P(),
            P(),
            P(),
        ),
        check_vma=False,
    )
```

```python
import functools
import math

import jax
import jax.numpy as jnp
from jax import lax
from jax.experimental import pallas as pl
from jax.experimental.pallas import tpu as pltpu
from jax.sharding import PartitionSpec as P

HEAD_SIZE = 64
STEP = 2
SEQ_MIN = 1024
LANES = 128
UNIT = 64
MICROSECOND = 1150 * 10**6

norm_epsilon = 1e-06
masked_score = -1e30
log2e = 1.4426950408889634

f32 = jnp.float32
bf16 = jnp.bfloat16
NT = (((1,), (1,)), ((), ()))
NN = (((1,), (0,)), ((), ()))
TN = (((0,), (0,)), ((), ()))

CORE = [(0, 1), (1, 0), (2, 3), (3, 2)]
ACROSS = [(0, 2), (2, 0), (1, 3), (3, 1)]

X, Y, Z0, Z1 = 2, 4, 8, 16
ORDERS = ((Z1, Z0, Y, X), (Z1, Y, X, Z0))
SUM_ORDERS = ((Z1, Z0, Y, X), (Z1, Z0, X, Y))
QKV_ORDERS = ((Z1, Z0, X, Y), (Z1, Z0, Y, X))

vmem = pl.BlockSpec(memory_space=pltpu.VMEM)
smem = pl.BlockSpec(memory_space=pltpu.SMEM)
hbm = pl.BlockSpec(memory_space=pltpu.HBM)


def mm(a, b, dims=NN):
    return lax.dot_general(a, b, dims, preferred_element_type=f32)


def call(
    kernel, name, outs, ins, scratch=(), flops=0, limit=56, scalars=(), scalars_out=(), far=(), copies=0
):
    def space(k):
        return smem if k == 0 or k in scalars else hbm if k in far else vmem

    return pl.pallas_call(
        kernel,
        name=name,
        out_shape=[jax.ShapeDtypeStruct(s, t) for s, t in outs],
        in_specs=[space(k) for k in range(len(ins))],
        out_specs=[smem if k in scalars_out else vmem for k in range(len(outs))],
        scratch_shapes=[pltpu.VMEM(s, t) for s, t in scratch]
        + ([pltpu.SemaphoreType.DMA((copies,))] if copies else []),
        compiler_params=pltpu.CompilerParams(vmem_limit_bytes=limit << 20),
        cost_estimate=pl.CostEstimate(flops=flops, bytes_accessed=0, transcendentals=0),
    )(*ins)


def send(array, bits):
    count = 4 * lax.axis_size("dp")
    pairs = [(i, i ^ bits[i & 1]) for i in range(count)]
    return lax.ppermute(array, ("dp", "head"), pairs)


def owner(unit, core, orders=ORDERS):
    found = []
    for order in orders:
        over_dp, over_x = 0, 0
        for place, bit in enumerate(order):
            flag = (unit >> place) & 1
            if bit == X:
                over_x = flag
            else:
                over_dp = over_dp + flag * (bit >> 2)
        found.append((over_dp, over_x))
    return (
        jnp.where(core == 0, found[0][0], found[1][0]),
        jnp.where(core == 0, found[0][1], found[1][1]),
    )


def unit_of(number, core, orders=ORDERS):
    found = [0, 0]
    for k, order in enumerate(orders):
        for place, bit in enumerate(order):
            found[k] = found[k] + ((number // bit) & 1) * (1 << place)
    return jnp.where(core == 0, found[0], found[1])


def window_start(sc, first):
    head, x, local = sc[1], sc[2], sc[5]
    return jnp.where(
        first < local,
        head * local + first,
        jnp.where(
            first < 2 * local,
            (head ^ 1) * local + first - local,
            first + jnp.where(x == 0, 0, SEQ_MIN - 2 * local),
        ),
    )


def window_token(sc, first, shape):
    return window_start(sc, first) + lax.broadcasted_iota(jnp.int32, shape, 0)


def window_valid(sc, first, shape):
    return jnp.where(window_token(sc, first, shape) < sc[0], 0, 1) == sc[2]


def lanes_of(shape):
    return lax.broadcasted_iota(jnp.int32, shape, 1)


def turns(fraction):
    square = fraction * fraction
    sine, cosine = 0.0, 0.0
    for k in range(8, -1, -1):
        sign = -1.0 if k % 2 else 1.0
        sine = sine * square + sign * (2 * math.pi) ** (2 * k + 1) / math.factorial(2 * k + 1)
        cosine = cosine * square + sign * (2 * math.pi) ** (2 * k) / math.factorial(2 * k)
    return sine * fraction, cosine


def embed_kernel(
    ids,
    segments_far,
    state_far,
    edge_here,
    edge_core,
    sc,
    embedded,
    hidden,
    hidden_edge,
    segments,
    state,
    arrived,
):
    copies = [
        pltpu.make_async_copy(far, near, arrived.at[k])
        for k, (far, near) in enumerate(((segments_far, segments), (state_far, state)))
    ]
    for copy in copies:
        copy.start()
    local, width = state.shape
    half = width // 2
    tall = LANES
    for k in range(1, 6):
        sc[k] = ids[k]
    order = lanes_of((1, half)).astype(f32)
    rates = jnp.exp(order * (-math.log(10000.0) / (half - 1))) * (0.5 / math.pi)

    def signal(places):
        turn = places * rates
        return turns(turn - jnp.floor(turn + 0.5))

    steps = signal(float(STEP))
    row = lax.broadcasted_iota(jnp.int32, (tall, half), 0)
    sine, cosine = signal(row.astype(f32))
    copies[0].wait()
    split = jnp.sum(jnp.where(segments[...] == 0, 1, 0))
    sc[0] = split
    copies[1].wait()
    for source, first in ((state, 0), (edge_here, 2 * local)):
        for start in range(0, source.shape[0], tall):
            rows = slice(start, start + tall)
            token = window_token(ids, first + start, (tall, half))
            begin = window_start(ids, first + start)
            early = token < split
            zero = signal(begin.astype(f32))
            one = signal((begin - split).astype(f32))
            base_sine = jnp.where(early, zero[0], one[0])
            base_cosine = jnp.where(early, zero[1], one[1])
            for side, value in (
                (0, base_sine * cosine + base_cosine * sine),
                (1, base_cosine * cosine - base_sine * sine),
            ):
                to = slice(side * half, (side + 1) * half)
                rows_in = source[rows, to].astype(f32)
                if source is edge_here:
                    rows_in = jnp.where(ids[2] == ids[3], rows_in, edge_core[rows, to].astype(f32))
                total = rows_in + (value + steps[side])
                if source is state:
                    embedded[rows, to] = total
                    hidden[rows, to] = total.astype(bf16)
                else:
                    hidden_edge[rows, to] = total.astype(bf16)


def attend_rows(rows, qf, kb, vb, mixed32, logs, mixed):
    tall = mixed.shape[0]
    lane = lanes_of((tall, LANES))
    log_totals = jnp.zeros((tall, LANES), f32)
    results = []
    for j in range(4):
        scores = mm(qf[j, rows, :], kb[j], NT)
        peak = jnp.max(scores, axis=1, keepdims=True)
        weights = jnp.exp2((scores - peak) * log2e).astype(bf16)
        summed = mm(weights, vb[j])
        log_totals = jnp.where(lane == 64 + j, peak + jnp.log(summed), log_totals)
        results.append(summed * (1.0 / pltpu.roll(summed, 64, 1)))
        if j % 2:
            both = jnp.where(lane < 64, results[j - 1], pltpu.roll(results[j], 64, 1))
            to = slice((j // 2) * LANES, (j // 2 + 1) * LANES)
            mixed32[:, to] = both
            mixed[:, to] = both.astype(bf16)
    logs[...] = log_totals


def front_kernel(
    sc,
    own,
    sib,
    edge,
    units_a,
    units_b,
    qf,
    kb,
    vb,
    qt,
    weight,
    mixed32,
    logs,
    mix_edge,
):
    x, c, dp = sc[2], sc[3], sc[4]
    for place, held in enumerate((units_a, units_b)):
        for sub in range(8):
            over_dp, over_x = owner(place * 8 + sub, c, QKV_ORDERS)
            row = pl.multiple_of((dp ^ over_dp) * UNIT, UNIT)
            for m in range(3):
                column = pl.multiple_of(m * 256 + (x ^ over_x) * LANES, LANES)
                weight[pl.ds(row, UNIT), pl.ds(column, LANES)] = held[sub, m]
    local = own.shape[0]
    for source, base in ((own, 0), (sib, local), (edge, 2 * local)):
        tall = 256 if source is edge else local
        lane = lanes_of((tall, LANES))

        def rows(index, carry, source=source, base=base, tall=tall, lane=lane):
            start = pl.multiple_of(index * tall, 128)
            out = pl.multiple_of(base + index * tall, 128)
            at = pl.ds(out, tall)
            projected = mm(source[pl.ds(start, tall), :], weight[...])
            valid = window_valid(sc, out, (tall, LANES))
            key_tail = jnp.where((lane == 64) & jnp.logical_not(valid), masked_score, 0.0)
            for p in range(2):
                blocks = [
                    projected[:, m * 256 + p * LANES : m * 256 + (p + 1) * LANES]
                    for m in range(3)
                ]
                blocks[0] = blocks[0] * 0.125
                qt[p, :, at] = jnp.transpose(blocks[0]).astype(bf16)
                for k in range(2):
                    if k:
                        blocks = [pltpu.roll(block, 64, 1) for block in blocks]
                    j = 2 * p + k
                    first = lane < 64
                    qf[j, at, :] = jnp.where(
                        first, blocks[0], jnp.where(lane == 64, 1.0, 0.0)
                    ).astype(bf16)
                    kb[j, at, :] = jnp.where(first, blocks[1], key_tail).astype(bf16)
                    vb[j, at, :] = jnp.where(first, blocks[2], 1.0).astype(bf16)
            return carry

        lax.fori_loop(0, source.shape[0] // tall, rows, 0)

    attend_rows(pl.ds(2 * local, mix_edge.shape[0]), qf, kb, vb, mixed32, logs, mix_edge)


def attend_kernel(first, sc, qf, kb, vb, mixed32, logs, mixed):
    attend_rows(pl.ds(first, mixed.shape[0]), qf, kb, vb, mixed32, logs, mixed)


def back_rows(sc, first, qf, kb, vb, qt, grad, mixed32, logs, part, before, keys_t, values_t, out):
    tall = part.size
    lane = lanes_of((tall, LANES))
    valid = window_valid(sc, first, (tall, LANES))
    rows = pl.ds(first, tall)
    for p in range(2):
        to = slice(p * LANES, (p + 1) * LANES)
        incoming = jnp.where(valid, grad(part, p), 0.0)
        product = incoming * mixed32[part, to]
        incoming_t = jnp.transpose(incoming).astype(bf16)
        grad_queries = []
        for k in range(2):
            j = 2 * p + k
            half = (lane < 64) if k == 0 else (lane >= 64)
            delta = jnp.sum(jnp.where(half, product, 0.0), axis=1, keepdims=True)
            log_total = logs[part, 64 + j : 65 + j] * log2e
            arriving = incoming if k == 0 else pltpu.roll(incoming, 64, 1)
            arriving = jnp.where(lane < 64, arriving, 0.0).astype(bf16)
            probs = jnp.exp2(mm(qf[j, rows, :], kb[j], NT) * log2e - log_total)
            grad_probs = mm(arriving, vb[j], NT)
            grad_scores = (probs * (grad_probs - delta)).astype(bf16)
            piece = slice(64 * k, 64 * k + 64)
            values = mm(incoming_t[piece, :], probs.astype(bf16))
            keys = mm(qt[p, piece, rows], grad_scores)
            keys_t[j] = before[0][j] + keys if before else keys
            values_t[j] = before[1][j] + values if before else values
            grad_queries.append(mm(grad_scores, kb[j]) * 0.125)
        out[:, to] = jnp.where(
            lane < 64, grad_queries[0], pltpu.roll(grad_queries[1], 64, 1)
        ).astype(bf16)


def back_kernel(groups, sc, qf, kb, vb, qt, *rest):
    count = len(groups)
    before, (keys_t, values_t) = rest[3 * count : -count - 2], rest[-2:]
    for k, (first, start, rows) in enumerate(groups):
        mixed32, logs, grad = rest[3 * k : 3 * k + 3]
        back_rows(
            sc,
            first,
            qf,
            kb,
            vb,
            qt,
            lambda part, p, grad=grad: grad[part, p * LANES : (p + 1) * LANES].astype(f32),
            mixed32,
            logs,
            pl.ds(start, rows),
            before,
            keys_t,
            values_t,
            rest[k - count - 2],
        )
        before = (keys_t, values_t)


def back_edge_kernel(
    late,
    sc,
    qf,
    kb,
    vb,
    qt,
    mixed32,
    logs,
    edge_here,
    edge_core,
    mixed32_sib,
    logs_sib,
    grad_sib,
    keys_in,
    values_in,
    dq_first,
    dq_own,
    dq_sib,
    own,
    sib,
    edge,
    out,
    stay,
    leave,
    keys_t,
    values_t,
    full,
    dq_late,
    dq_edge,
):
    x, c, dp = sc[2], sc[3], sc[4]
    local = own.shape[0]
    before = (keys_in, values_in)

    def from_sib(part, p):
        return grad_sib[part, p * LANES : (p + 1) * LANES].astype(f32)

    def from_edge(part, p):
        there, here = slice(p * LANES, (p + 1) * LANES), slice((p + 2) * LANES, (p + 3) * LANES)
        return jnp.where(
            x == c, edge_here[part, here].astype(f32), edge_core[part, there].astype(f32)
        )

    for first, part, operands, target in (
        (2 * local - late, pl.ds(local - late, late), (from_sib, mixed32_sib, logs_sib), dq_late),
        (2 * local, pl.ds(0, edge.shape[0]), (from_edge, mixed32, logs), dq_edge),
    ):
        back_rows(
            sc, first, qf, kb, vb, qt, *operands, part, before, keys_t, values_t, target
        )
        before = (keys_t, values_t)
    at = 0
    for piece in (dq_first, dq_own, dq_sib, dq_late, dq_edge):
        out[at : at + piece.shape[0], 0:256] = piece[...]
        at += piece.shape[0]
    for m, held in ((1, keys_t), (2, values_t)):
        for p in range(2):
            pair = jnp.concatenate([held[2 * p], held[2 * p + 1]], axis=0)
            to = slice(m * 256 + p * LANES, m * 256 + (p + 1) * LANES)
            out[:, to] = jnp.transpose(pair).astype(bf16)
    for m in range(3):
        to = slice(m * 256, (m + 1) * 256)
        total = 0.0
        for source, base in ((own, 0), (sib, local), (edge, 2 * local)):
            total += mm(source[...], out[base : base + source.shape[0], to], TN)
        full[:, to] = total.astype(bf16)
    for place, target in enumerate((stay, leave)):
        for sub in range(8):
            over_dp, over_x = owner(place * 8 + sub, c, QKV_ORDERS)
            row = pl.multiple_of((dp ^ over_dp) * UNIT, UNIT)
            for m in range(3):
                column = pl.multiple_of(m * 256 + (x ^ over_x) * LANES, LANES)
                target[sub, m] = full[pl.ds(row, UNIT), pl.ds(column, LANES)]


def norm_parts(rows):
    width = rows.shape[1]
    center = rows - jnp.sum(rows, axis=1, keepdims=True) * (1.0 / width)
    spread = jnp.sum(center * center, axis=1, keepdims=True) * (1.0 / width)
    scale = lax.rsqrt(spread + norm_epsilon)
    return center * scale, scale


def norm_back(normed, scale, gain, incoming):
    width = normed.shape[1]
    e = incoming * gain
    mean_e = jnp.sum(e, axis=1, keepdims=True) * (1.0 / width)
    mean_en = jnp.sum(e * normed, axis=1, keepdims=True) * (1.0 / width)
    return (e - mean_e - normed * mean_en) * scale


def middle_kernel(
    sc,
    embedded,
    state,
    cotangent,
    running,
    mix_own,
    mix_sib,
    edge_own,
    edge_sib,
    own_a,
    own_b,
    sib_a,
    sib_b,
    halt_offset,
    gain_one,
    shift_one,
    gain_two,
    shift_two,
    halt_vector,
    bias_out,
    bias_in,
    new_state,
    base,
    grad_own,
    grad_sib,
    grad_edge,
    mixed,
    first_low,
    active,
    grad_out_low,
    grad_inner,
    grad_branch,
    sums,
    w_out,
    w_in,
    w_back,
    slope,
):
    head, x, c, dp = sc[1], sc[2], sc[3], sc[4]
    hidden = w_in.shape[1]
    width = w_out.shape[0]
    hidden_block = hidden // 4
    units = 16

    def unit_place(unit, core):
        over_dp, over_x = owner(unit, core)
        rows = pl.ds(pl.multiple_of((dp ^ over_dp) * UNIT, UNIT), UNIT)
        block = (x ^ over_x) * 2 + core
        narrow = pl.ds(pl.multiple_of(block * LANES, LANES), LANES)
        wide = pl.ds(pl.multiple_of(block * hidden_block, hidden_block), hidden_block)
        return rows, narrow, wide

    for held, first_unit, core in (
        (own_a, 0, c),
        (own_b, 8, c),
        (sib_a, 0, 1 - c),
        (sib_b, 8, 1 - c),
    ):

        def place(unit, carry, held=held, first_unit=first_unit, core=core):
            rows, narrow, wide = unit_place(unit + first_unit, core)
            w_out[rows, narrow] = held[unit, :, 0:LANES]
            w_in[rows, wide] = held[unit, :, LANES : LANES + hidden_block]
            w_back[rows, wide] = held[unit, :, LANES + hidden_block :]
            return carry

        lax.fori_loop(0, units // 2, place, 0)
    rows_all = embedded.shape[0]
    edge_rows = edge_own.shape[0]
    at = pl.multiple_of(jnp.where(x == 0, rows_all - edge_rows, 0), 128)
    edge_at = pl.ds(at, edge_rows)
    token = lax.broadcasted_iota(jnp.int32, (edge_rows, LANES), 0) + at + head * rows_all
    elsewhere = jnp.where(token < sc[0], 0, 1) != x
    for p in range(2):
        part = slice(p * LANES, (p + 1) * LANES)
        for held, edge, core in ((mix_own, edge_own, c), (mix_sib, edge_sib, 1 - c)):
            lanes = pl.ds(pl.multiple_of((2 * p + core) * LANES, LANES), LANES)
            mixed[:, lanes] = held[:, part]
            mixed[edge_at, lanes] = jnp.where(elsewhere, edge[:, part], mixed[edge_at, lanes])

    diagonal = lax.broadcasted_iota(jnp.int32, (LANES, LANES), 0) == lanes_of((LANES, LANES))
    run_all = jnp.concatenate(
        [
            jnp.sum(
                jnp.where(diagonal, running[k : k + 1, :].astype(f32), 0.0), axis=1, keepdims=True
            )
            for k in range(running.shape[0])
        ],
        axis=0,
    )
    gains = tuple(
        g[...] for g in (gain_one, shift_one, gain_two, shift_two, halt_vector, bias_out)
    )
    tall = rows_all // 2
    for start in range(0, rows_all, tall):
        rows = slice(start, start + tall)

        def total(row, value, lanes=slice(None), start=start):
            value = jnp.sum(value, axis=0, keepdims=True)
            at_row = (slice(row, row + 1), lanes)
            sums[at_row] = value if start == 0 else sums[at_row] + value

        middle_rows(
            rows,
            total,
            run_all[rows, :],
            halt_offset[0],
            gains,
            bias_in,
            embedded,
            state,
            cotangent,
            new_state,
            base,
            grad_own,
            grad_sib,
            mixed,
            first_low,
            active,
            grad_out_low,
            grad_inner,
            grad_branch,
            w_out,
            w_in,
            w_back,
            slope,
            c,
        )
    sums[7:8, :] = jnp.zeros_like(sums[7:8, :])
    sums[12:, :] = jnp.zeros_like(sums[12:, :])
    grad_edge[:, 0 : 2 * LANES] = grad_sib[edge_at, :]
    grad_edge[:, 2 * LANES :] = grad_own[edge_at, :]


def middle_rows(
    rows,
    total,
    run,
    halt_offset,
    gains,
    bias_in,
    embedded,
    state,
    cotangent,
    new_state,
    base,
    grad_own,
    grad_sib,
    mixed,
    first_low,
    active,
    grad_out_low,
    grad_inner,
    grad_branch,
    w_out,
    w_in,
    w_back,
    slope,
    c,
):
    gain_one, shift_one, gain_two, shift_two, halt_vector, bias_out = gains
    width = w_out.shape[0]
    branch = mm(mixed[rows, :], w_out[...], NT)
    normed_one, scale_one = norm_parts(embedded[rows, :] + branch)
    first = normed_one * gain_one + shift_one
    low = first.astype(bf16)
    first_low[rows, :] = low
    chunk = 256
    steps = w_in.shape[1] // chunk
    k0 = math.sqrt(2.0 / math.pi)

    outward = first + bias_out
    for index in range(steps):
        cols = slice(index * chunk, (index + 1) * chunk)
        u = mm(low, w_in[:, cols]) + bias_in[:, cols]
        square = u * u
        t = jnp.tanh(k0 * u * (1.0 + 0.044715 * square))
        half = 0.5 * (1.0 + t)
        act = (u * half).astype(bf16)
        active[rows, cols] = act
        slope[rows, cols] = half + 0.5 * u * (1.0 - t * t) * (k0 * (1.0 + 3 * 0.044715 * square))
        outward = outward + mm(act, w_back[:, cols], NT)
    normed_two, scale_two = norm_parts(outward)
    second = normed_two * gain_two + shift_two
    halting = jax.nn.sigmoid(jnp.sum(second * halt_vector, axis=1, keepdims=True) + halt_offset)
    rows_in = state[rows, :].astype(f32)
    difference = second - rows_in
    share = run * halting
    new_state[rows, :] = (rows_in + share * difference).astype(bf16)
    g = cotangent[rows, :].astype(f32)
    carry_c = jnp.sum(g * difference, axis=1, keepdims=True)
    push = share * (1.0 - halting) * carry_c
    grad_second = share * g + push * halt_vector
    total(5, push * second)
    total(6, jnp.broadcast_to(push, second.shape))
    total(3, grad_second * normed_two)
    total(4, grad_second)
    grad_outward = norm_back(normed_two, scale_two, gain_two, grad_second)
    total(0, grad_outward)
    out_low = grad_outward.astype(bf16)
    grad_out_low[rows, :] = out_low

    grad_first = grad_outward
    for index in range(steps):
        cols = slice(index * chunk, (index + 1) * chunk)
        gi = (mm(out_low, w_back[:, cols]) * slope[rows, cols]).astype(bf16)
        grad_inner[rows, cols] = gi
        lane0 = (index * chunk) % width
        total(8 + (index * chunk) // width, gi.astype(f32), slice(lane0, lane0 + chunk))
        grad_first = grad_first + mm(gi, w_in[:, cols], NT)
    total(1, grad_first * normed_one)
    total(2, grad_first)
    grad_resid = norm_back(normed_one, scale_one, gain_one, grad_first)
    base[rows, :] = grad_resid + (1.0 - share) * g
    branch_low = grad_resid.astype(bf16)
    grad_branch[rows, :] = branch_low
    grad_mixed = mm(branch_low, w_out[...]).astype(bf16)
    for p in range(2):
        blocks = [grad_mixed[:, (2 * p + k) * LANES : (2 * p + k + 1) * LANES] for k in range(2)]
        to = slice(p * LANES, (p + 1) * LANES)
        grad_own[rows, to] = jnp.where(c == 0, blocks[0], blocks[1])
        grad_sib[rows, to] = jnp.where(c == 0, blocks[1], blocks[0])


def weight_kernel(
    sc, mixed, first_low, active, grad_out_low, grad_inner, grad_branch, sums, sum_own, sum_sib
):
    x, c, dp = sc[2], sc[3], sc[4]
    width = mixed.shape[1]
    hidden_block = active.shape[1] // 4
    units = 16
    turned_branch = jnp.transpose(grad_branch[...])
    turned_first = jnp.transpose(first_low[...])
    turned_out = jnp.transpose(grad_out_low[...])
    high = sums[...].astype(bf16)
    low = (sums[...] - high.astype(f32)).astype(bf16)
    for out, core in ((sum_sib, 1 - c), (sum_own, c)):
        for over_x in range(2):
            block = (x ^ over_x) * 2 + core
            narrow = pl.ds(pl.multiple_of(block * LANES, LANES), LANES)
            wide = pl.ds(pl.multiple_of(block * hidden_block, hidden_block), hidden_block)
            for turned, source, lanes, lane0 in (
                (turned_branch, mixed, narrow, 0),
                (turned_first, grad_inner, wide, LANES),
                (turned_out, active, wide, LANES + hidden_block),
            ):
                value = mm(turned, source[:, lanes]).astype(bf16)
                for k in range(width // UNIT):
                    unit = unit_of((dp ^ k) * 4 + over_x * X, core, SUM_ORDERS)
                    to = pl.ds(pl.multiple_of(unit * UNIT, UNIT), UNIT)
                    out[to, lane0 : lane0 + value.shape[1]] = value[k * UNIT : (k + 1) * UNIT, :]
        tail = slice(units * UNIT, units * UNIT + 16)
        out[tail, 0:width] = high
        out[tail, width : 2 * width] = low
        out[tail, 2 * width :] = jnp.zeros_like(out[tail, 2 * width :])


def hidden_back_kernel(sc, grads, weight, base, own, sib, edge):
    local = own.shape[0]
    for target, first, tall in ((sib, local, 320), (edge, 2 * local, 256), (own, 0, 320)):

        def rows(index, carry, target=target, first=first, tall=tall):
            start = pl.multiple_of(index * tall, 64)
            at = pl.ds(pl.multiple_of(first + index * tall, 64), tall)
            value = mm(grads[at, :], weight[...], NT)
            to = pl.ds(start, tall)
            if target is own:
                target[to, :] = value + base[to, :]
            else:
                target[to, :] = value.astype(bf16)
            return carry

        lax.fori_loop(0, target.shape[0] // tall, rows, 0)


def finish_kernel(sc, own, sib, edge_here, edge_core, out):
    out[...] = own[...] + sib[...].astype(f32)
    rows = edge_here.shape[0]
    at = pl.ds(pl.multiple_of(jnp.where(sc[2] == 0, out.shape[0] - rows, 0), 128), rows)
    edge = edge_here[...].astype(f32) + edge_core[...].astype(f32)
    out[at, :] += jnp.where(sc[2] == sc[3], 0.0, edge)


def split_tail(rows, width):
    return rows[:, :width].astype(f32) + rows[:, width : 2 * width].astype(f32)


def join_tail(leave, rows, value):
    width = value.shape[1]
    high = value.astype(bf16)
    low = (value - high.astype(f32)).astype(bf16)
    leave[rows, 0:width] = high
    leave[rows, width : 2 * width] = low
    leave[rows, 2 * width :] = jnp.zeros((16, leave.shape[1] - 2 * width), bf16)
    return high.astype(f32) + low.astype(f32)


def fold_kernel(stage, sc, own, arrived, sums_in, leave, stay, sums):
    width = sums.shape[1]
    half = stay.shape[0]
    stay[...] = (own[0:half, :].astype(f32) + arrived[0:half, :].astype(f32)).astype(bf16)
    leave[0:half, :] = (
        own[half : 2 * half, :].astype(f32) + arrived[half : 2 * half, :].astype(f32)
    ).astype(bf16)
    first, second = slice(half, half + 16), slice(half + 16, half + 32)
    near = split_tail(arrived[2 * half : 2 * half + 16, :], width)
    if stage == 0:
        sums[...] = join_tail(leave, first, split_tail(own[2 * half :, :], width) + near)
    elif stage == 1:
        sums[0:16, :] = join_tail(leave, first, sums_in[...])
        sums[16:32, :] = join_tail(leave, second, near)
    elif stage == 2:
        opposite = split_tail(arrived[2 * half + 16 :, :], width)
        total = (sums_in[0:16, :] + opposite) + (sums_in[16:32, :] + near)
        sums[...] = join_tail(leave, first, total)
    else:
        sums[...] = join_tail(leave, first, sums_in[...] + near)


def last_fold_kernel(sc, own, arrived, sums_in, *outs):
    out_part, in_part, back_part, bias_in, *vectors, offset = outs
    width = sums_in.shape[1]
    rows = own.shape[0]
    total = own[...].astype(f32) + arrived[0:rows, :].astype(f32)
    hidden_block = in_part.shape[1]
    out_part[...] = total[:, :LANES]
    in_part[...] = total[:, LANES : LANES + hidden_block]
    back_part[...] = total[:, LANES + hidden_block :]
    sums = sums_in[...] + split_tail(arrived[rows:, :], width)
    for k, vector in enumerate(vectors):
        vector[...] = sums[k : k + 1, :]
    offset[...] = sums[6:7, 0:1]
    for k in range(bias_in.shape[1] // width):
        bias_in[:, k * width : (k + 1) * width] = sums[8 + k : 9 + k, :]


def fold(stage, sc, own, arrived, sums, width):
    wide = own.shape[1]
    half = (own.shape[0] - (16 if stage == 0 else 0)) // 2
    tail = 32 if stage == 1 else 16
    return call(
        functools.partial(fold_kernel, stage),
        "fold",
        [((half + tail, wide), bf16), ((half, wide), bf16), ((tail, width), f32)],
        [sc, own, arrived, sums],
        limit=16,
    )


def qkv_fold_kernel(sc, own, arrived, leave, stay):
    half = stay.shape[0]
    total = own[...].astype(f32) + arrived[...].astype(f32)
    stay[...] = total[0:half].astype(bf16)
    leave[...] = total[half:].astype(bf16)


def qkv_spread_kernel(sc, own, arrived, here, over_z1, over_z0, over_both):
    total = own[...].astype(f32) + arrived[...].astype(f32)
    for k, out in enumerate((here, over_z1, over_z0, over_both)):
        out[...] = total[k].astype(out.dtype)


def qkv_fold(sc, own, arrived):
    half = ((own.shape[0] // 2, *own.shape[1:]), bf16)
    return call(
        qkv_fold_kernel, "qkv_fold", [half, half], [sc, own, arrived], limit=16
    )


def add(a, b):
    return a.astype(f32) + b.astype(f32)


def after(array, *others):
    return lax.optimization_barrier((array, *others))[0]


def body(
    state_in,
    qkv_weight,
    out_weight,
    ffn_in_weight,
    ffn_out_weight,
    ffn_in_bias,
    ffn_out_bias,
    norm1_gain,
    norm1_shift,
    norm2_gain,
    norm2_shift,
    halt_weight,
    halt_bias,
    seg_ids,
    halt_mask,
    cotangent,
):
    dp = lax.axis_index("dp")
    head = lax.axis_index("head")
    x, c = head // 2, head % 2
    local, width = state_in.shape
    window = 4 * local - SEQ_MIN
    edge = window - 2 * local
    hidden = ffn_in_bias.shape[0]
    unit_wide = LANES + 2 * (hidden // 4)
    ringed = qkv_weight.shape[1] == UNIT and lax.axis_size("dp") == 8

    ids = jnp.stack([0 * dp, head, x, c, dp if ringed else 0 * dp, 0 * dp + local])
    ids = ids.astype(jnp.int32)
    at = jnp.where(x == 0, local - edge, 0)
    hops, qkv_hops = list(zip(*ORDERS)), list(zip(*QKV_ORDERS))
    sum_hops = list(zip(*SUM_ORDERS))
    rest = jnp.concatenate([out_weight, ffn_in_weight, ffn_out_weight], axis=1)
    edge_rows = lax.dynamic_slice_in_dim(state_in, at, edge)
    edge_here = lax.ppermute(edge_rows, "head", ACROSS)
    if ringed:
        rest_own = rest[None]
        rest_far = send(rest_own, hops[0])
        qkv_far = send(qkv_weight[None], qkv_hops[0])
        held = jnp.concatenate([qkv_weight[None], after(qkv_far, rest_own, edge_rows)], axis=0)
        qkv_far = send(held, qkv_hops[1])
        edge_here = after(edge_here, held)
    edge_core = lax.ppermute(edge_here, "head", CORE)
    sc, embedded, hidden_own, hidden_edge = call(
        embed_kernel,
        "embed",
        [
            ((6,), jnp.int32),
            ((local, width), f32),
            ((local, width), bf16),
            ((edge, width), bf16),
        ],
        [ids, seg_ids, state_in, edge_here, edge_core],
        scratch=[(seg_ids.shape, jnp.int32), (state_in.shape, bf16)],
        flops=2 * MICROSECOND,
        limit=20,
        scalars_out=(0,),
        far=(1, 2),
        copies=2,
    )
    hidden_sib = lax.ppermute(hidden_own, "head", CORE)
    if ringed:
        held = jnp.concatenate([held, after(qkv_far, hidden_edge)], axis=0)
        qkv_far = send(held, qkv_hops[2])
        rest_own = jnp.concatenate([rest_own, after(rest_far, held)], axis=0)
        rest_far = send(rest_own, hops[1])
        held = jnp.concatenate([held, after(qkv_far, rest_own)], axis=0)
        qkv_units = [held, send(held, qkv_hops[3])]
        rest_own = jnp.concatenate([rest_own, after(rest_far, held)], axis=0)
        rest_far = send(rest_own, hops[2])
        hidden_front = after(hidden_own, rest_own)
    else:
        qkv_units, rest_whole = gather_whole(qkv_weight, rest, x, c)
        hidden_front = hidden_own

    wide = ((4, window, LANES), bf16)
    qf, kb, vb, qt, qkv_full, mixed32_edge, logs_edge, mix_edge = call(
        front_kernel,
        "front",
        [
            wide,
            wide,
            wide,
            ((2, LANES, window), bf16),
            ((width, 6 * LANES), bf16),
            ((edge, 2 * LANES), f32),
            ((edge, LANES), f32),
            ((edge, 2 * LANES), bf16),
        ],
        [sc, hidden_front, hidden_sib, hidden_edge, *qkv_units],
        flops=7 * MICROSECOND,
        limit=28,
    )
    edge_own = lax.ppermute(mix_edge, "head", ACROSS)
    if ringed:
        rest_a = jnp.concatenate([rest_own, after(rest_far, mix_edge)], axis=0)
        rest_b = send(rest_a, hops[3])
        qf_ready = after(qf, rest_a)
    else:
        rest_a, rest_b, qf_ready = rest_whole[:8], rest_whole[8:], qf
    sib_a = lax.ppermute(rest_a, "head", CORE)
    attend = lambda rows: [
        ((rows, 2 * LANES), f32),
        ((rows, LANES), f32),
        ((rows, 2 * LANES), bf16),
    ]
    mixed32_sib, logs_sib, mix_for_sib = call(
        functools.partial(attend_kernel, local),
        "attend_sib",
        attend(local),
        [sc, qf_ready, kb, vb],
        flops=7 * MICROSECOND,
        limit=20,
    )
    mix_sib = lax.ppermute(mix_for_sib, "head", CORE)
    edge_sib = lax.ppermute(after(edge_own, mix_for_sib), "head", CORE)
    mixed32_own, logs_own, mix_own = call(
        functools.partial(attend_kernel, 0),
        "attend_own",
        attend(local),
        [sc, after(qf_ready, mix_for_sib), kb, vb],
        flops=7 * MICROSECOND,
        limit=20,
    )
    sib_b = lax.ppermute(after(rest_b, mix_own, mix_sib, edge_sib), "head", CORE)
    (
        new_state,
        base,
        grad_own,
        grad_for_sib,
        edge_for_others,
        *low_rows,
    ) = call(
        middle_kernel,
        "middle",
        [
            ((local, width), bf16),
            ((local, width), f32),
            ((local, 2 * LANES), bf16),
            ((local, 2 * LANES), bf16),
            ((edge, width), bf16),
            ((local, width), bf16),
            ((local, width), bf16),
            ((local, hidden), bf16),
            ((local, width), bf16),
            ((local, hidden), bf16),
            ((local, width), bf16),
            ((16, width), f32),
        ],
        [
            sc,
            embedded,
            state_in,
            cotangent,
            halt_mask.reshape(local // LANES, LANES),
            mix_own,
            mix_sib,
            edge_own,
            edge_sib,
            rest_a,
            rest_b,
            sib_a,
            sib_b,
            halt_bias,
            norm1_gain[None],
            norm1_shift[None],
            norm2_gain[None],
            norm2_shift[None],
            halt_weight[None],
            ffn_out_bias[None],
            ffn_in_bias[None],
        ],
        scalars=(13,),
        scratch=[
            ((width, width), bf16),
            ((width, hidden), bf16),
            ((width, hidden), bf16),
            ((local, hidden), f32),
        ],
        flops=13 * MICROSECOND,
        limit=26,
    )
    grad_sib = lax.ppermute(grad_for_sib, "head", CORE)
    grad_here = lax.ppermute(edge_for_others, "head", ACROSS)
    sum_own, sum_sib = call(
        weight_kernel,
        "weights",
        [((16 * UNIT + 16, unit_wide), bf16)] * 2,
        [sc, *low_rows],
        flops=5 * MICROSECOND,
        limit=28,
    )
    heads_t = ((4, HEAD_SIZE, window), f32)
    shared = [sc, qf, kb, vb, qt]

    def back(groups, name, *others):
        return call(
            functools.partial(back_kernel, groups),
            name,
            [((rows, 2 * LANES), bf16) for _, _, rows in groups] + [heads_t, heads_t],
            [*shared, *others],
            flops=sum(rows for _, _, rows in groups) * MICROSECOND // 60,
            limit=30,
        )

    early, late = 256, 128
    if ringed:
        sum_arrived = lax.ppermute(after(sum_sib, grad_sib), "head", CORE)
    dq_first, keys_t, values_t = back(
        ((0, 0, early),), "back_first", mixed32_own, logs_own, grad_own
    )
    if ringed:
        empty = jnp.zeros((16, width), f32)
        leave, stay, sums = fold(0, sc, sum_own, after(sum_arrived, dq_first), empty, width)
        sum_arrived = send(leave, sum_hops[3])
        grad_own = after(grad_own, stay)
    dq_own, dq_sib, keys_t, values_t = back(
        ((early, early, local - early), (local, 0, local - late)),
        "back_most",
        mixed32_own,
        logs_own,
        grad_own,
        mixed32_sib,
        logs_sib,
        grad_sib,
        keys_t,
        values_t,
    )
    if ringed:
        leave, stay, sums = fold(1, sc, stay, after(sum_arrived, dq_sib), sums, width)
        sum_arrived = send(leave, sum_hops[2])
        qf_last = after(qf, stay)
    else:
        qf_last = qf
    grad_core = lax.ppermute(after(grad_here, dq_sib), "head", CORE)
    qkv_half = ((8, 3, UNIT, LANES), bf16)
    grad_projected, qkv_stay, qkv_leave = call(
        functools.partial(back_edge_kernel, late),
        "back_edge",
        [((window, 6 * LANES), bf16), qkv_half, qkv_half],
        [
            sc,
            qf_last,
            *shared[2:],
            mixed32_edge,
            logs_edge,
            grad_here,
            grad_core,
            mixed32_sib,
            logs_sib,
            grad_sib,
            keys_t,
            values_t,
            dq_first,
            dq_own,
            dq_sib,
            hidden_own,
            hidden_sib,
            hidden_edge,
        ],
        scratch=[
            heads_t,
            heads_t,
            ((width, 6 * LANES), bf16),
            ((late, 2 * LANES), bf16),
            ((edge, 2 * LANES), bf16),
        ],
        flops=9 * MICROSECOND,
        limit=32,
    )
    if ringed:
        qkv_far = send(qkv_leave, qkv_hops[3])
        leave, stay, sums = fold(2, sc, stay, after(sum_arrived, qkv_leave), sums, width)
        sum_arrived = send(leave, sum_hops[1])
        base = after(base, stay)
    state_own, state_sib, state_far = call(
        hidden_back_kernel,
        "hidden_back",
        [((local, width), f32), ((local, width), bf16), ((edge, width), bf16)],
        [sc, grad_projected, qkv_full, base],
        flops=3 * MICROSECOND,
        limit=20,
    )
    state_sib = lax.ppermute(state_sib, "head", CORE)
    if ringed:
        qkv_leave, qkv_stay = qkv_fold(sc, after(qkv_stay, state_own), qkv_far)
        qkv_far = send(qkv_leave, qkv_hops[2])
        leave, stay, sums = fold(3, sc, stay, after(sum_arrived, qkv_leave), sums, width)
        sum_arrived = send(leave, sum_hops[0])
        unit = qkv_leave.shape[1:]
        here, *away = call(
            qkv_spread_kernel,
            "qkv_spread",
            [(unit, f32)] + [(unit, bf16)] * 3,
            [sc, after(qkv_stay, stay), qkv_far],
            limit=16,
        )
        away = [send(a, (bit, bit)) for a, bit in zip(away, (Z1, Z0, Z0 | Z1))]
        sum_arrived, *away = lax.optimization_barrier((sum_arrived, *away))
        grad_qkv_weight = add(here, away[0]) + add(away[1], away[2])
    state_here = lax.ppermute(state_far, "head", ACROSS)
    quarter = hidden // 4
    if ringed:
        grad_out, grad_in, grad_back, bias_sum, *vectors = call(
            last_fold_kernel,
            "last_fold",
            [
                ((UNIT, LANES), f32),
                ((UNIT, quarter), f32),
                ((UNIT, quarter), f32),
                ((1, hidden), f32),
                *[((1, width), f32)] * 6,
                ((1, 1), f32),
            ],
            [sc, stay, sum_arrived, sums],
            limit=16,
        )
        bias_sum, *vectors = [v.reshape(-1) for v in (bias_sum, *vectors)]
    else:
        grad_qkv_weight, rest_grad, small = scatter_whole(
            [qkv_stay, qkv_leave], sum_own, sum_sib, width, x
        )
        grad_out = rest_grad[:, :LANES]
        grad_in = rest_grad[:, LANES : LANES + quarter]
        grad_back = rest_grad[:, LANES + quarter :]
        bias_sum = small[8 : 8 + hidden // width].reshape(hidden)
        vectors = [*[small[k] for k in range(6)], small[6, 0:1]]

    state_core = lax.ppermute(state_here, "head", CORE)
    (grad_state,) = call(
        finish_kernel,
        "finish",
        [((local, width), f32)],
        [sc, state_own, state_sib, state_here, state_core],
        limit=16,
    )
    return (
        new_state,
        grad_state,
        grad_qkv_weight,
        grad_out,
        grad_in,
        grad_back,
        bias_sum,
        *vectors,
    )


def unit_owners(orders):
    tables = []
    for order in orders:
        numbers = [
            sum(bit for place, bit in enumerate(order) if (unit >> place) & 1)
            for unit in range(16)
        ]
        tables.append([(number >> 2, (number >> 1) & 1) for number in numbers])
    return tables


def gather_whole(qkv_weight, rest, x, c):
    def both(array, axis):
        whole = lax.all_gather(array, "dp", axis=axis, tiled=True)
        other = lax.ppermute(whole, "head", ACROSS)
        return jnp.stack([whole, other])

    qkv, rest = both(qkv_weight, 1), both(rest, 0)
    width = rest.shape[1]
    qkv = qkv.reshape(2, 3, width // UNIT, UNIT, LANES)
    rest = rest.reshape(2, width // UNIT, UNIT, rest.shape[2])

    def units(array, orders):
        return jnp.where(
            c == 0, *(jnp.stack([array[ox, od] for od, ox in t]) for t in unit_owners(orders))
        )

    qkv = units(jnp.swapaxes(qkv, 1, 2), QKV_ORDERS)
    return [qkv[:8], qkv[8:]], units(rest, ORDERS)


def scatter_whole(qkv_sums, sum_own, sum_sib, width, x):
    c = lax.axis_index("head") % 2
    rows = 16 * UNIT
    rest = add(sum_own, lax.ppermute(sum_sib, "head", CORE))
    tail = rest[rows:]
    small = lax.psum(tail[:, :width] + tail[:, width : 2 * width], ("dp", "head")) * 0.5
    rest = rest[:rows].reshape(16, UNIT, rest.shape[1])
    qkv = jnp.concatenate(qkv_sums, axis=0).astype(f32)

    def order(orders, array):
        whole = []
        for table in unit_owners(orders):
            back = {owner_of: unit for unit, owner_of in enumerate(table)}
            whole.append(
                [jnp.stack([array[back[od, ox]] for od in range(8)]) for ox in range(2)]
            )
        return [jnp.where(c == 0, *pair) for pair in zip(*whole)]

    rest = [r.reshape(width, r.shape[2]) for r in order(SUM_ORDERS, rest)]
    qkv = [
        jnp.swapaxes(q, 0, 1).reshape(3, width, LANES) for q in order(QKV_ORDERS, qkv)
    ]
    rest = rest[0] + lax.ppermute(rest[1], "head", ACROSS)
    qkv = qkv[0] + lax.ppermute(qkv[1], "head", ACROSS)
    return (
        lax.psum_scatter(qkv, "dp", scatter_dimension=1, tiled=True),
        lax.psum_scatter(rest, "dp", scatter_dimension=0, tiled=True),
        small,
    )


def solution(mesh):
    tokens = P(("dp", "head"), None)
    weights = P("dp", "head")
    return jax.shard_map(
        body,
        mesh=mesh,
        in_specs=(
            tokens,
            P(None, "dp", "head"),
            weights,
            weights,
            weights,
            P(),
            P(),
            P(),
            P(),
            P(),
            P(),
            P(),
            P(),
            P("dp", None),
            P(("dp", "head")),
            tokens,
        ),
        out_specs=(
            tokens,
            tokens,
            P(None, "dp", "head"),
            weights,
            weights,
            weights,
            P(),
            P(),
            P(),
            P(),
            P(),
            P(),
            P(),
            P(),
        ),
        check_vma=False,
    )
```

```python
import functools
import math

import jax
import jax.numpy as jnp
from jax import lax
from jax.experimental import pallas as pl
from jax.experimental.pallas import tpu as pltpu
from jax.sharding import PartitionSpec as P

HEAD_SIZE = 64
STEP = 2
SEQ_MIN = 1024
LANES = 128
UNIT = 64
MICROSECOND = 1150 * 10**6

norm_epsilon = 1e-06
masked_score = -1e30
log2e = 1.4426950408889634

f32 = jnp.float32
bf16 = jnp.bfloat16
NT = (((1,), (1,)), ((), ()))
NN = (((1,), (0,)), ((), ()))
TN = (((0,), (0,)), ((), ()))

CORE = [(0, 1), (1, 0), (2, 3), (3, 2)]
ACROSS = [(0, 2), (2, 0), (1, 3), (3, 1)]

X, Y, Z0, Z1 = 2, 4, 8, 16
ORDERS = ((Z1, Z0, Y, X), (Z1, Y, X, Z0))
SUM_ORDERS = ((Z1, Z0, Y, X), (Z1, Z0, X, Y))
QKV_ORDERS = ((Z1, Z0, X, Y), (Z1, Z0, Y, X))

vmem = pl.BlockSpec(memory_space=pltpu.VMEM)
smem = pl.BlockSpec(memory_space=pltpu.SMEM)
hbm = pl.BlockSpec(memory_space=pltpu.HBM)


def mm(a, b, dims=NN):
    return lax.dot_general(a, b, dims, preferred_element_type=f32)


def call(
    kernel, name, outs, ins, scratch=(), flops=0, limit=56, scalars=(), scalars_out=(), far=(), copies=0
):
    def space(k):
        return smem if k == 0 or k in scalars else hbm if k in far else vmem

    return pl.pallas_call(
        kernel,
        name=name,
        out_shape=[jax.ShapeDtypeStruct(s, t) for s, t in outs],
        in_specs=[space(k) for k in range(len(ins))],
        out_specs=[smem if k in scalars_out else vmem for k in range(len(outs))],
        scratch_shapes=[pltpu.VMEM(s, t) for s, t in scratch]
        + ([pltpu.SemaphoreType.DMA((copies,))] if copies else []),
        compiler_params=pltpu.CompilerParams(vmem_limit_bytes=limit << 20),
        cost_estimate=pl.CostEstimate(flops=flops, bytes_accessed=0, transcendentals=0),
    )(*ins)


def send(array, bits):
    count = 4 * lax.axis_size("dp")
    pairs = [(i, i ^ bits[i & 1]) for i in range(count)]
    return lax.ppermute(array, ("dp", "head"), pairs)


def owner(unit, core, orders=ORDERS):
    found = []
    for order in orders:
        over_dp, over_x = 0, 0
        for place, bit in enumerate(order):
            flag = (unit >> place) & 1
            if bit == X:
                over_x = flag
            else:
                over_dp = over_dp + flag * (bit >> 2)
        found.append((over_dp, over_x))
    return (
        jnp.where(core == 0, found[0][0], found[1][0]),
        jnp.where(core == 0, found[0][1], found[1][1]),
    )


def unit_of(number, core, orders=ORDERS):
    found = [0, 0]
    for k, order in enumerate(orders):
        for place, bit in enumerate(order):
            found[k] = found[k] + ((number // bit) & 1) * (1 << place)
    return jnp.where(core == 0, found[0], found[1])


def window_start(sc, first):
    head, x, local = sc[1], sc[2], sc[5]
    return jnp.where(
        first < local,
        head * local + first,
        jnp.where(
            first < 2 * local,
            (head ^ 1) * local + first - local,
            first + jnp.where(x == 0, 0, SEQ_MIN - 2 * local),
        ),
    )


def window_token(sc, first, shape):
    return window_start(sc, first) + lax.broadcasted_iota(jnp.int32, shape, 0)


def window_valid(sc, first, shape):
    return jnp.where(window_token(sc, first, shape) < sc[0], 0, 1) == sc[2]


def lanes_of(shape):
    return lax.broadcasted_iota(jnp.int32, shape, 1)


def turns(fraction):
    square = fraction * fraction
    sine, cosine = 0.0, 0.0
    for k in range(8, -1, -1):
        sign = -1.0 if k % 2 else 1.0
        sine = sine * square + sign * (2 * math.pi) ** (2 * k + 1) / math.factorial(2 * k + 1)
        cosine = cosine * square + sign * (2 * math.pi) ** (2 * k) / math.factorial(2 * k)
    return sine * fraction, cosine


def embed_kernel(
    ids,
    segments_far,
    state_far,
    edge_here,
    edge_core,
    sc,
    embedded,
    hidden,
    hidden_edge,
    segments,
    state,
    arrived,
):
    copies = [
        pltpu.make_async_copy(far, near, arrived.at[k])
        for k, (far, near) in enumerate(((segments_far, segments), (state_far, state)))
    ]
    for copy in copies:
        copy.start()
    local, width = state.shape
    half = width // 2
    tall = LANES
    for k in range(1, 6):
        sc[k] = ids[k]
    order = lanes_of((1, half)).astype(f32)
    rates = jnp.exp(order * (-math.log(10000.0) / (half - 1))) * (0.5 / math.pi)

    def signal(places):
        turn = places * rates
        return turns(turn - jnp.floor(turn + 0.5))

    steps = signal(float(STEP))
    row = lax.broadcasted_iota(jnp.int32, (tall, half), 0)
    sine, cosine = signal(row.astype(f32))
    copies[0].wait()
    split = jnp.sum(jnp.where(segments[...] == 0, 1, 0))
    sc[0] = split
    copies[1].wait()
    for source, first in ((state, 0), (edge_here, 2 * local)):
        for start in range(0, source.shape[0], tall):
            rows = slice(start, start + tall)
            token = window_token(ids, first + start, (tall, half))
            begin = window_start(ids, first + start)
            early = token < split
            zero = signal(begin.astype(f32))
            one = signal((begin - split).astype(f32))
            base_sine = jnp.where(early, zero[0], one[0])
            base_cosine = jnp.where(early, zero[1], one[1])
            for side, value in (
                (0, base_sine * cosine + base_cosine * sine),
                (1, base_cosine * cosine - base_sine * sine),
            ):
                to = slice(side * half, (side + 1) * half)
                rows_in = source[rows, to].astype(f32)
                if source is edge_here:
                    rows_in = jnp.where(ids[2] == ids[3], rows_in, edge_core[rows, to].astype(f32))
                total = rows_in + (value + steps[side])
                if source is state:
                    embedded[rows, to] = total
                    hidden[rows, to] = total.astype(bf16)
                else:
                    hidden_edge[rows, to] = total.astype(bf16)


def attend_rows(rows, qf, kb, vb, mixed32, logs, mixed):
    tall = mixed.shape[0]
    lane = lanes_of((tall, LANES))
    log_totals = jnp.zeros((tall, LANES), f32)
    results = []
    for j in range(4):
        scores = mm(qf[j, rows, :], kb[j], NT)
        peak = jnp.max(scores, axis=1, keepdims=True)
        weights = jnp.exp2((scores - peak) * log2e).astype(bf16)
        summed = mm(weights, vb[j])
        log_totals = jnp.where(lane == 64 + j, peak + jnp.log(summed), log_totals)
        results.append(summed * (1.0 / pltpu.roll(summed, 64, 1)))
        if j % 2:
            both = jnp.where(lane < 64, results[j - 1], pltpu.roll(results[j], 64, 1))
            to = slice((j // 2) * LANES, (j // 2 + 1) * LANES)
            mixed32[:, to] = both
            mixed[:, to] = both.astype(bf16)
    logs[...] = log_totals


def front_kernel(
    sc,
    own,
    sib,
    edge,
    units_a,
    units_b,
    qf,
    kb,
    vb,
    qt,
    weight,
    mixed32,
    logs,
    mix_edge,
):
    x, c, dp = sc[2], sc[3], sc[4]
    for place, held in enumerate((units_a, units_b)):
        for sub in range(8):
            over_dp, over_x = owner(place * 8 + sub, c, QKV_ORDERS)
            row = pl.multiple_of((dp ^ over_dp) * UNIT, UNIT)
            for m in range(3):
                column = pl.multiple_of(m * 256 + (x ^ over_x) * LANES, LANES)
                weight[pl.ds(row, UNIT), pl.ds(column, LANES)] = held[sub, m]
    local = own.shape[0]
    for source, base in ((own, 0), (sib, local), (edge, 2 * local)):
        tall = 256 if source is edge else local
        lane = lanes_of((tall, LANES))

        def rows(index, carry, source=source, base=base, tall=tall, lane=lane):
            start = pl.multiple_of(index * tall, 128)
            out = pl.multiple_of(base + index * tall, 128)
            at = pl.ds(out, tall)
            projected = mm(source[pl.ds(start, tall), :], weight[...])
            valid = window_valid(sc, out, (tall, LANES))
            key_tail = jnp.where((lane == 64) & jnp.logical_not(valid), masked_score, 0.0)
            for p in range(2):
                blocks = [
                    projected[:, m * 256 + p * LANES : m * 256 + (p + 1) * LANES]
                    for m in range(3)
                ]
                blocks[0] = blocks[0] * 0.125
                qt[p, :, at] = jnp.transpose(blocks[0]).astype(bf16)
                for k in range(2):
                    if k:
                        blocks = [pltpu.roll(block, 64, 1) for block in blocks]
                    j = 2 * p + k
                    first = lane < 64
                    qf[j, at, :] = jnp.where(
                        first, blocks[0], jnp.where(lane == 64, 1.0, 0.0)
                    ).astype(bf16)
                    kb[j, at, :] = jnp.where(first, blocks[1], key_tail).astype(bf16)
                    vb[j, at, :] = jnp.where(first, blocks[2], 1.0).astype(bf16)
            return carry

        lax.fori_loop(0, source.shape[0] // tall, rows, 0)

    attend_rows(pl.ds(2 * local, mix_edge.shape[0]), qf, kb, vb, mixed32, logs, mix_edge)


def attend_kernel(first, sc, qf, kb, vb, mixed32, logs, mixed):
    attend_rows(pl.ds(first, mixed.shape[0]), qf, kb, vb, mixed32, logs, mixed)


def back_rows(sc, first, qf, kb, vb, qt, grad, mixed32, logs, part, before, keys_t, values_t, out):
    tall = part.size
    lane = lanes_of((tall, LANES))
    valid = window_valid(sc, first, (tall, LANES))
    rows = pl.ds(first, tall)
    for p in range(2):
        to = slice(p * LANES, (p + 1) * LANES)
        incoming = jnp.where(valid, grad(part, p), 0.0)
        product = incoming * mixed32[part, to]
        incoming_t = jnp.transpose(incoming).astype(bf16)
        grad_queries = []
        for k in range(2):
            j = 2 * p + k
            half = (lane < 64) if k == 0 else (lane >= 64)
            delta = jnp.sum(jnp.where(half, product, 0.0), axis=1, keepdims=True)
            log_total = logs[part, 64 + j : 65 + j]
            arriving = incoming if k == 0 else pltpu.roll(incoming, 64, 1)
            arriving = jnp.where(lane < 64, arriving, 0.0).astype(bf16)
            probs = jnp.exp2((mm(qf[j, rows, :], kb[j], NT) - log_total) * log2e)
            grad_probs = mm(arriving, vb[j], NT)
            grad_scores = (probs * (grad_probs - delta)).astype(bf16)
            piece = slice(64 * k, 64 * k + 64)
            values = mm(incoming_t[piece, :], probs.astype(bf16))
            keys = mm(qt[p, piece, rows], grad_scores)
            keys_t[j] = before[0][j] + keys if before else keys
            values_t[j] = before[1][j] + values if before else values
            grad_queries.append(mm(grad_scores, kb[j]) * 0.125)
        out[:, to] = jnp.where(
            lane < 64, grad_queries[0], pltpu.roll(grad_queries[1], 64, 1)
        ).astype(bf16)


def back_kernel(groups, sc, qf, kb, vb, qt, *rest):
    count = len(groups)
    before, (keys_t, values_t) = rest[3 * count : -count - 2], rest[-2:]
    for k, (first, start, rows) in enumerate(groups):
        mixed32, logs, grad = rest[3 * k : 3 * k + 3]
        back_rows(
            sc,
            first,
            qf,
            kb,
            vb,
            qt,
            lambda part, p, grad=grad: grad[part, p * LANES : (p + 1) * LANES].astype(f32),
            mixed32,
            logs,
            pl.ds(start, rows),
            before,
            keys_t,
            values_t,
            rest[k - count - 2],
        )
        before = (keys_t, values_t)


def back_edge_kernel(
    late,
    sc,
    qf,
    kb,
    vb,
    qt,
    mixed32,
    logs,
    edge_here,
    edge_core,
    mixed32_sib,
    logs_sib,
    grad_sib,
    keys_in,
    values_in,
    dq_first,
    dq_own,
    dq_sib,
    own,
    sib,
    edge,
    out,
    stay,
    leave,
    keys_t,
    values_t,
    full,
    dq_late,
    dq_edge,
):
    x, c, dp = sc[2], sc[3], sc[4]
    local = own.shape[0]
    before = (keys_in, values_in)

    def from_sib(part, p):
        return grad_sib[part, p * LANES : (p + 1) * LANES].astype(f32)

    def from_edge(part, p):
        there, here = slice(p * LANES, (p + 1) * LANES), slice((p + 2) * LANES, (p + 3) * LANES)
        return jnp.where(
            x == c, edge_here[part, here].astype(f32), edge_core[part, there].astype(f32)
        )

    for first, part, operands, target in (
        (2 * local - late, pl.ds(local - late, late), (from_sib, mixed32_sib, logs_sib), dq_late),
        (2 * local, pl.ds(0, edge.shape[0]), (from_edge, mixed32, logs), dq_edge),
    ):
        back_rows(
            sc, first, qf, kb, vb, qt, *operands, part, before, keys_t, values_t, target
        )
        before = (keys_t, values_t)
    at = 0
    for piece in (dq_first, dq_own, dq_sib, dq_late, dq_edge):
        out[at : at + piece.shape[0], 0:256] = piece[...]
        at += piece.shape[0]
    for m, held in ((1, keys_t), (2, values_t)):
        for p in range(2):
            pair = jnp.concatenate([held[2 * p], held[2 * p + 1]], axis=0)
            to = slice(m * 256 + p * LANES, m * 256 + (p + 1) * LANES)
            out[:, to] = jnp.transpose(pair).astype(bf16)
    for m in range(3):
        to = slice(m * 256, (m + 1) * 256)
        total = 0.0
        for source, base in ((own, 0), (sib, local), (edge, 2 * local)):
            total += mm(source[...], out[base : base + source.shape[0], to], TN)
        full[:, to] = total.astype(bf16)
    for place, target in enumerate((stay, leave)):
        for sub in range(8):
            over_dp, over_x = owner(place * 8 + sub, c, QKV_ORDERS)
            row = pl.multiple_of((dp ^ over_dp) * UNIT, UNIT)
            for m in range(3):
                column = pl.multiple_of(m * 256 + (x ^ over_x) * LANES, LANES)
                target[sub, m] = full[pl.ds(row, UNIT), pl.ds(column, LANES)]


def norm_parts(rows):
    width = rows.shape[1]
    center = rows - jnp.sum(rows, axis=1, keepdims=True) * (1.0 / width)
    spread = jnp.sum(center * center, axis=1, keepdims=True) * (1.0 / width)
    scale = lax.rsqrt(spread + norm_epsilon)
    return center * scale, scale


def norm_back(normed, scale, gain, incoming):
    width = normed.shape[1]
    e = incoming * gain
    mean_e = jnp.sum(e, axis=1, keepdims=True) * (1.0 / width)
    mean_en = jnp.sum(e * normed, axis=1, keepdims=True) * (1.0 / width)
    return (e - mean_e - normed * mean_en) * scale


def middle_kernel(
    sc,
    embedded,
    state,
    cotangent,
    running,
    mix_own,
    mix_sib,
    edge_own,
    edge_sib,
    own_a,
    own_b,
    sib_a,
    sib_b,
    halt_offset,
    gain_one,
    shift_one,
    gain_two,
    shift_two,
    halt_vector,
    bias_out,
    bias_in,
    new_state,
    base,
    grad_own,
    grad_sib,
    grad_edge,
    mixed,
    first_low,
    active,
    grad_out_low,
    grad_inner,
    grad_branch,
    sums,
    w_out,
    w_in,
    w_back,
    slope,
):
    head, x, c, dp = sc[1], sc[2], sc[3], sc[4]
    hidden = w_in.shape[1]
    width = w_out.shape[0]
    hidden_block = hidden // 4
    units = 16

    def unit_place(unit, core):
        over_dp, over_x = owner(unit, core)
        rows = pl.ds(pl.multiple_of((dp ^ over_dp) * UNIT, UNIT), UNIT)
        block = (x ^ over_x) * 2 + core
        narrow = pl.ds(pl.multiple_of(block * LANES, LANES), LANES)
        wide = pl.ds(pl.multiple_of(block * hidden_block, hidden_block), hidden_block)
        return rows, narrow, wide

    for held, first_unit, core in (
        (own_a, 0, c),
        (own_b, 8, c),
        (sib_a, 0, 1 - c),
        (sib_b, 8, 1 - c),
    ):

        def place(unit, carry, held=held, first_unit=first_unit, core=core):
            rows, narrow, wide = unit_place(unit + first_unit, core)
            w_out[rows, narrow] = held[unit, :, 0:LANES]
            w_in[rows, wide] = held[unit, :, LANES : LANES + hidden_block]
            w_back[rows, wide] = held[unit, :, LANES + hidden_block :]
            return carry

        lax.fori_loop(0, units // 2, place, 0)
    rows_all = embedded.shape[0]
    edge_rows = edge_own.shape[0]
    at = pl.multiple_of(jnp.where(x == 0, rows_all - edge_rows, 0), 128)
    edge_at = pl.ds(at, edge_rows)
    token = lax.broadcasted_iota(jnp.int32, (edge_rows, LANES), 0) + at + head * rows_all
    elsewhere = jnp.where(token < sc[0], 0, 1) != x
    for p in range(2):
        part = slice(p * LANES, (p + 1) * LANES)
        for held, edge, core in ((mix_own, edge_own, c), (mix_sib, edge_sib, 1 - c)):
            lanes = pl.ds(pl.multiple_of((2 * p + core) * LANES, LANES), LANES)
            mixed[:, lanes] = held[:, part]
            mixed[edge_at, lanes] = jnp.where(elsewhere, edge[:, part], mixed[edge_at, lanes])

    diagonal = lax.broadcasted_iota(jnp.int32, (LANES, LANES), 0) == lanes_of((LANES, LANES))
    run_all = jnp.concatenate(
        [
            jnp.sum(
                jnp.where(diagonal, running[k : k + 1, :].astype(f32), 0.0), axis=1, keepdims=True
            )
            for k in range(running.shape[0])
        ],
        axis=0,
    )
    gains = tuple(
        g[...] for g in (gain_one, shift_one, gain_two, shift_two, halt_vector, bias_out)
    )
    tall = rows_all // 2
    for start in range(0, rows_all, tall):
        rows = slice(start, start + tall)

        def total(row, value, lanes=slice(None), start=start):
            value = jnp.sum(value, axis=0, keepdims=True)
            at_row = (slice(row, row + 1), lanes)
            sums[at_row] = value if start == 0 else sums[at_row] + value

        middle_rows(
            rows,
            total,
            run_all[rows, :],
            halt_offset[0],
            gains,
            bias_in,
            embedded,
            state,
            cotangent,
            new_state,
            base,
            grad_own,
            grad_sib,
            mixed,
            first_low,
            active,
            grad_out_low,
            grad_inner,
            grad_branch,
            w_out,
            w_in,
            w_back,
            slope,
            c,
        )
    sums[7:8, :] = jnp.zeros_like(sums[7:8, :])
    sums[12:, :] = jnp.zeros_like(sums[12:, :])
    grad_edge[:, 0 : 2 * LANES] = grad_sib[edge_at, :]
    grad_edge[:, 2 * LANES :] = grad_own[edge_at, :]


def middle_rows(
    rows,
    total,
    run,
    halt_offset,
    gains,
    bias_in,
    embedded,
    state,
    cotangent,
    new_state,
    base,
    grad_own,
    grad_sib,
    mixed,
    first_low,
    active,
    grad_out_low,
    grad_inner,
    grad_branch,
    w_out,
    w_in,
    w_back,
    slope,
    c,
):
    gain_one, shift_one, gain_two, shift_two, halt_vector, bias_out = gains
    width = w_out.shape[0]
    branch = mm(mixed[rows, :], w_out[...], NT)
    normed_one, scale_one = norm_parts(embedded[rows, :] + branch)
    first = normed_one * gain_one + shift_one
    low = first.astype(bf16)
    first_low[rows, :] = low
    chunk = 256
    steps = w_in.shape[1] // chunk
    k0 = math.sqrt(2.0 / math.pi)

    outward = first + bias_out
    for index in range(steps):
        cols = slice(index * chunk, (index + 1) * chunk)
        u = mm(low, w_in[:, cols]) + bias_in[:, cols]
        square = u * u
        t = jnp.tanh(k0 * u * (1.0 + 0.044715 * square))
        half = 0.5 * (1.0 + t)
        act = (u * half).astype(bf16)
        active[rows, cols] = act
        slope[rows, cols] = half + 0.5 * u * (1.0 - t * t) * (k0 * (1.0 + 3 * 0.044715 * square))
        outward = outward + mm(act, w_back[:, cols], NT)
    normed_two, scale_two = norm_parts(outward)
    second = normed_two * gain_two + shift_two
    halting = jax.nn.sigmoid(jnp.sum(second * halt_vector, axis=1, keepdims=True) + halt_offset)
    rows_in = state[rows, :].astype(f32)
    difference = second - rows_in
    share = run * halting
    new_state[rows, :] = (rows_in + share * difference).astype(bf16)
    g = cotangent[rows, :].astype(f32)
    carry_c = jnp.sum(g * difference, axis=1, keepdims=True)
    push = share * (1.0 - halting) * carry_c
    grad_second = share * g + push * halt_vector
    total(5, push * second)
    total(6, jnp.broadcast_to(push, second.shape))
    total(3, grad_second * normed_two)
    total(4, grad_second)
    grad_outward = norm_back(normed_two, scale_two, gain_two, grad_second)
    total(0, grad_outward)
    out_low = grad_outward.astype(bf16)
    grad_out_low[rows, :] = out_low

    grad_first = grad_outward
    for index in range(steps):
        cols = slice(index * chunk, (index + 1) * chunk)
        gi = (mm(out_low, w_back[:, cols]) * slope[rows, cols]).astype(bf16)
        grad_inner[rows, cols] = gi
        lane0 = (index * chunk) % width
        total(8 + (index * chunk) // width, gi.astype(f32), slice(lane0, lane0 + chunk))
        grad_first = grad_first + mm(gi, w_in[:, cols], NT)
    total(1, grad_first * normed_one)
    total(2, grad_first)
    grad_resid = norm_back(normed_one, scale_one, gain_one, grad_first)
    base[rows, :] = grad_resid + (1.0 - share) * g
    branch_low = grad_resid.astype(bf16)
    grad_branch[rows, :] = branch_low
    grad_mixed = mm(branch_low, w_out[...]).astype(bf16)
    for p in range(2):
        blocks = [grad_mixed[:, (2 * p + k) * LANES : (2 * p + k + 1) * LANES] for k in range(2)]
        to = slice(p * LANES, (p + 1) * LANES)
        grad_own[rows, to] = jnp.where(c == 0, blocks[0], blocks[1])
        grad_sib[rows, to] = jnp.where(c == 0, blocks[1], blocks[0])


def weight_kernel(
    sc, mixed, first_low, active, grad_out_low, grad_inner, grad_branch, sums, sum_own, sum_sib
):
    x, c, dp = sc[2], sc[3], sc[4]
    width = mixed.shape[1]
    hidden_block = active.shape[1] // 4
    units = 16
    turned_branch = jnp.transpose(grad_branch[...])
    turned_first = jnp.transpose(first_low[...])
    turned_out = jnp.transpose(grad_out_low[...])
    high = sums[...].astype(bf16)
    low = (sums[...] - high.astype(f32)).astype(bf16)
    for out, core in ((sum_sib, 1 - c), (sum_own, c)):
        for over_x in range(2):
            block = (x ^ over_x) * 2 + core
            narrow = pl.ds(pl.multiple_of(block * LANES, LANES), LANES)
            wide = pl.ds(pl.multiple_of(block * hidden_block, hidden_block), hidden_block)
            for turned, source, lanes, lane0 in (
                (turned_branch, mixed, narrow, 0),
                (turned_first, grad_inner, wide, LANES),
                (turned_out, active, wide, LANES + hidden_block),
            ):
                value = mm(turned, source[:, lanes]).astype(bf16)
                for k in range(width // UNIT):
                    unit = unit_of((dp ^ k) * 4 + over_x * X, core, SUM_ORDERS)
                    to = pl.ds(pl.multiple_of(unit * UNIT, UNIT), UNIT)
                    out[to, lane0 : lane0 + value.shape[1]] = value[k * UNIT : (k + 1) * UNIT, :]
        tail = slice(units * UNIT, units * UNIT + 16)
        out[tail, 0:width] = high
        out[tail, width : 2 * width] = low
        out[tail, 2 * width :] = jnp.zeros_like(out[tail, 2 * width :])


def hidden_back_kernel(sc, grads, weight, base, own, sib, edge):
    local = own.shape[0]
    for target, first, tall in ((sib, local, 320), (edge, 2 * local, 256), (own, 0, 320)):

        def rows(index, carry, target=target, first=first, tall=tall):
            start = pl.multiple_of(index * tall, 64)
            at = pl.ds(pl.multiple_of(first + index * tall, 64), tall)
            value = mm(grads[at, :], weight[...], NT)
            to = pl.ds(start, tall)
            if target is own:
                target[to, :] = value + base[to, :]
            else:
                target[to, :] = value.astype(bf16)
            return carry

        lax.fori_loop(0, target.shape[0] // tall, rows, 0)


def finish_kernel(sc, own, sib, edge_here, edge_core, out):
    out[...] = own[...] + sib[...].astype(f32)
    rows = edge_here.shape[0]
    at = pl.ds(pl.multiple_of(jnp.where(sc[2] == 0, out.shape[0] - rows, 0), 128), rows)
    edge = edge_here[...].astype(f32) + edge_core[...].astype(f32)
    out[at, :] += jnp.where(sc[2] == sc[3], 0.0, edge)


def split_tail(rows, width):
    return rows[:, :width].astype(f32) + rows[:, width : 2 * width].astype(f32)


def join_tail(leave, rows, value):
    width = value.shape[1]
    high = value.astype(bf16)
    low = (value - high.astype(f32)).astype(bf16)
    leave[rows, 0:width] = high
    leave[rows, width : 2 * width] = low
    leave[rows, 2 * width :] = jnp.zeros((16, leave.shape[1] - 2 * width), bf16)
    return high.astype(f32) + low.astype(f32)


def fold_kernel(stage, sc, own, arrived, sums_in, leave, stay, sums):
    width = sums.shape[1]
    half = stay.shape[0]
    stay[...] = (own[0:half, :].astype(f32) + arrived[0:half, :].astype(f32)).astype(bf16)
    leave[0:half, :] = (
        own[half : 2 * half, :].astype(f32) + arrived[half : 2 * half, :].astype(f32)
    ).astype(bf16)
    first, second = slice(half, half + 16), slice(half + 16, half + 32)
    near = split_tail(arrived[2 * half : 2 * half + 16, :], width)
    if stage == 0:
        sums[...] = join_tail(leave, first, split_tail(own[2 * half :, :], width) + near)
    elif stage == 1:
        sums[0:16, :] = join_tail(leave, first, sums_in[...])
        sums[16:32, :] = join_tail(leave, second, near)
    elif stage == 2:
        opposite = split_tail(arrived[2 * half + 16 :, :], width)
        total = (sums_in[0:16, :] + opposite) + (sums_in[16:32, :] + near)
        sums[...] = join_tail(leave, first, total)
    else:
        sums[...] = join_tail(leave, first, sums_in[...] + near)


def last_fold_kernel(sc, own, arrived, sums_in, *outs):
    out_part, in_part, back_part, bias_in, *vectors, offset = outs
    width = sums_in.shape[1]
    rows = own.shape[0]
    total = own[...].astype(f32) + arrived[0:rows, :].astype(f32)
    hidden_block = in_part.shape[1]
    out_part[...] = total[:, :LANES]
    in_part[...] = total[:, LANES : LANES + hidden_block]
    back_part[...] = total[:, LANES + hidden_block :]
    sums = sums_in[...] + split_tail(arrived[rows:, :], width)
    for k, vector in enumerate(vectors):
        vector[...] = sums[k : k + 1, :]
    offset[...] = sums[6:7, 0:1]
    for k in range(bias_in.shape[1] // width):
        bias_in[:, k * width : (k + 1) * width] = sums[8 + k : 9 + k, :]


def fold(stage, sc, own, arrived, sums, width):
    wide = own.shape[1]
    half = (own.shape[0] - (16 if stage == 0 else 0)) // 2
    tail = 32 if stage == 1 else 16
    return call(
        functools.partial(fold_kernel, stage),
        "fold",
        [((half + tail, wide), bf16), ((half, wide), bf16), ((tail, width), f32)],
        [sc, own, arrived, sums],
        limit=16,
    )


def qkv_fold_kernel(sc, own, arrived, leave, stay):
    half = stay.shape[0]
    total = own[...].astype(f32) + arrived[...].astype(f32)
    stay[...] = total[0:half].astype(bf16)
    leave[...] = total[half:].astype(bf16)


def qkv_spread_kernel(sc, own, arrived, here, over_z1, over_z0, over_both):
    total = own[...].astype(f32) + arrived[...].astype(f32)
    for k, out in enumerate((here, over_z1, over_z0, over_both)):
        out[...] = total[k].astype(out.dtype)


def qkv_fold(sc, own, arrived):
    half = ((own.shape[0] // 2, *own.shape[1:]), bf16)
    return call(
        qkv_fold_kernel, "qkv_fold", [half, half], [sc, own, arrived], limit=16
    )


def add(a, b):
    return a.astype(f32) + b.astype(f32)


def after(array, *others):
    return lax.optimization_barrier((array, *others))[0]


def body(
    state_in,
    qkv_weight,
    out_weight,
    ffn_in_weight,
    ffn_out_weight,
    ffn_in_bias,
    ffn_out_bias,
    norm1_gain,
    norm1_shift,
    norm2_gain,
    norm2_shift,
    halt_weight,
    halt_bias,
    seg_ids,
    halt_mask,
    cotangent,
):
    dp = lax.axis_index("dp")
    head = lax.axis_index("head")
    x, c = head // 2, head % 2
    local, width = state_in.shape
    window = 4 * local - SEQ_MIN
    edge = window - 2 * local
    hidden = ffn_in_bias.shape[0]
    unit_wide = LANES + 2 * (hidden // 4)
    ringed = qkv_weight.shape[1] == UNIT and lax.axis_size("dp") == 8

    ids = jnp.stack([0 * dp, head, x, c, dp if ringed else 0 * dp, 0 * dp + local])
    ids = ids.astype(jnp.int32)
    at = jnp.where(x == 0, local - edge, 0)
    hops, qkv_hops = list(zip(*ORDERS)), list(zip(*QKV_ORDERS))
    sum_hops = list(zip(*SUM_ORDERS))
    rest = jnp.concatenate([out_weight, ffn_in_weight, ffn_out_weight], axis=1)
    edge_rows = lax.dynamic_slice_in_dim(state_in, at, edge)
    edge_here = lax.ppermute(edge_rows, "head", ACROSS)
    if ringed:
        rest_own = rest[None]
        rest_far = send(rest_own, hops[0])
        qkv_far = send(qkv_weight[None], qkv_hops[0])
        held = jnp.concatenate([qkv_weight[None], after(qkv_far, rest_own, edge_rows)], axis=0)
        qkv_far = send(held, qkv_hops[1])
        edge_here = after(edge_here, held)
    edge_core = lax.ppermute(edge_here, "head", CORE)
    sc, embedded, hidden_own, hidden_edge = call(
        embed_kernel,
        "embed",
        [
            ((6,), jnp.int32),
            ((local, width), f32),
            ((local, width), bf16),
            ((edge, width), bf16),
        ],
        [ids, seg_ids, state_in, edge_here, edge_core],
        scratch=[(seg_ids.shape, jnp.int32), (state_in.shape, bf16)],
        flops=2 * MICROSECOND,
        limit=20,
        scalars_out=(0,),
        far=(1, 2),
        copies=2,
    )
    hidden_sib = lax.ppermute(hidden_own, "head", CORE)
    if ringed:
        held = jnp.concatenate([held, after(qkv_far, hidden_edge)], axis=0)
        qkv_far = send(held, qkv_hops[2])
        rest_own = jnp.concatenate([rest_own, after(rest_far, held)], axis=0)
        rest_far = send(rest_own, hops[1])
        held = jnp.concatenate([held, after(qkv_far, rest_own)], axis=0)
        qkv_units = [held, send(held, qkv_hops[3])]
        rest_own = jnp.concatenate([rest_own, after(rest_far, held)], axis=0)
        rest_far = send(rest_own, hops[2])
        hidden_front = after(hidden_own, rest_own)
    else:
        qkv_units, rest_whole = gather_whole(qkv_weight, rest, x, c)
        hidden_front = hidden_own

    wide = ((4, window, LANES), bf16)
    qf, kb, vb, qt, qkv_full, mixed32_edge, logs_edge, mix_edge = call(
        front_kernel,
        "front",
        [
            wide,
            wide,
            wide,
            ((2, LANES, window), bf16),
            ((width, 6 * LANES), bf16),
            ((edge, 2 * LANES), f32),
            ((edge, LANES), f32),
            ((edge, 2 * LANES), bf16),
        ],
        [sc, hidden_front, hidden_sib, hidden_edge, *qkv_units],
        flops=7 * MICROSECOND,
        limit=28,
    )
    edge_own = lax.ppermute(mix_edge, "head", ACROSS)
    if ringed:
        rest_a = jnp.concatenate([rest_own, after(rest_far, mix_edge)], axis=0)
        rest_b = send(rest_a, hops[3])
        qf_ready = after(qf, rest_a)
    else:
        rest_a, rest_b, qf_ready = rest_whole[:8], rest_whole[8:], qf
    sib_a = lax.ppermute(rest_a, "head", CORE)
    attend = lambda rows: [
        ((rows, 2 * LANES), f32),
        ((rows, LANES), f32),
        ((rows, 2 * LANES), bf16),
    ]
    mixed32_sib, logs_sib, mix_for_sib = call(
        functools.partial(attend_kernel, local),
        "attend_sib",
        attend(local),
        [sc, qf_ready, kb, vb],
        flops=7 * MICROSECOND,
        limit=20,
    )
    mix_sib = lax.ppermute(mix_for_sib, "head", CORE)
    edge_sib = lax.ppermute(after(edge_own, mix_for_sib), "head", CORE)
    mixed32_own, logs_own, mix_own = call(
        functools.partial(attend_kernel, 0),
        "attend_own",
        attend(local),
        [sc, after(qf_ready, mix_for_sib), kb, vb],
        flops=7 * MICROSECOND,
        limit=20,
    )
    sib_b = lax.ppermute(after(rest_b, mix_own, mix_sib, edge_sib), "head", CORE)
    (
        new_state,
        base,
        grad_own,
        grad_for_sib,
        edge_for_others,
        *low_rows,
    ) = call(
        middle_kernel,
        "middle",
        [
            ((local, width), bf16),
            ((local, width), f32),
            ((local, 2 * LANES), bf16),
            ((local, 2 * LANES), bf16),
            ((edge, width), bf16),
            ((local, width), bf16),
            ((local, width), bf16),
            ((local, hidden), bf16),
            ((local, width), bf16),
            ((local, hidden), bf16),
            ((local, width), bf16),
            ((16, width), f32),
        ],
        [
            sc,
            embedded,
            state_in,
            cotangent,
            halt_mask.reshape(local // LANES, LANES),
            mix_own,
            mix_sib,
            edge_own,
            edge_sib,
            rest_a,
            rest_b,
            sib_a,
            sib_b,
            halt_bias,
            norm1_gain[None],
            norm1_shift[None],
            norm2_gain[None],
            norm2_shift[None],
            halt_weight[None],
            ffn_out_bias[None],
            ffn_in_bias[None],
        ],
        scalars=(13,),
        scratch=[
            ((width, width), bf16),
            ((width, hidden), bf16),
            ((width, hidden), bf16),
            ((local, hidden), f32),
        ],
        flops=13 * MICROSECOND,
        limit=26,
    )
    grad_sib = lax.ppermute(grad_for_sib, "head", CORE)
    grad_here = lax.ppermute(edge_for_others, "head", ACROSS)
    sum_own, sum_sib = call(
        weight_kernel,
        "weights",
        [((16 * UNIT + 16, unit_wide), bf16)] * 2,
        [sc, *low_rows],
        flops=5 * MICROSECOND,
        limit=28,
    )
    heads_t = ((4, HEAD_SIZE, window), f32)
    shared = [sc, qf, kb, vb, qt]

    def back(groups, name, *others):
        return call(
            functools.partial(back_kernel, groups),
            name,
            [((rows, 2 * LANES), bf16) for _, _, rows in groups] + [heads_t, heads_t],
            [*shared, *others],
            flops=sum(rows for _, _, rows in groups) * MICROSECOND // 60,
            limit=30,
        )

    early, late = 256, 128
    if ringed:
        sum_arrived = lax.ppermute(after(sum_sib, grad_sib), "head", CORE)
    dq_first, keys_t, values_t = back(
        ((0, 0, early),), "back_first", mixed32_own, logs_own, grad_own
    )
    if ringed:
        empty = jnp.zeros((16, width), f32)
        leave, stay, sums = fold(0, sc, sum_own, after(sum_arrived, dq_first), empty, width)
        sum_arrived = send(leave, sum_hops[3])
        grad_own = after(grad_own, stay)
    dq_own, dq_sib, keys_t, values_t = back(
        ((early, early, local - early), (local, 0, local - late)),
        "back_most",
        mixed32_own,
        logs_own,
        grad_own,
        mixed32_sib,
        logs_sib,
        grad_sib,
        keys_t,
        values_t,
    )
    if ringed:
        leave, stay, sums = fold(1, sc, stay, after(sum_arrived, dq_sib), sums, width)
        sum_arrived = send(leave, sum_hops[2])
        qf_last = after(qf, stay)
    else:
        qf_last = qf
    grad_core = lax.ppermute(after(grad_here, dq_sib), "head", CORE)
    qkv_half = ((8, 3, UNIT, LANES), bf16)
    grad_projected, qkv_stay, qkv_leave = call(
        functools.partial(back_edge_kernel, late),
        "back_edge",
        [((window, 6 * LANES), bf16), qkv_half, qkv_half],
        [
            sc,
            qf_last,
            *shared[2:],
            mixed32_edge,
            logs_edge,
            grad_here,
            grad_core,
            mixed32_sib,
            logs_sib,
            grad_sib,
            keys_t,
            values_t,
            dq_first,
            dq_own,
            dq_sib,
            hidden_own,
            hidden_sib,
            hidden_edge,
        ],
        scratch=[
            heads_t,
            heads_t,
            ((width, 6 * LANES), bf16),
            ((late, 2 * LANES), bf16),
            ((edge, 2 * LANES), bf16),
        ],
        flops=9 * MICROSECOND,
        limit=32,
    )
    if ringed:
        qkv_far = send(qkv_leave, qkv_hops[3])
        leave, stay, sums = fold(2, sc, stay, after(sum_arrived, qkv_leave), sums, width)
        sum_arrived = send(leave, sum_hops[1])
        base = after(base, stay)
    state_own, state_sib, state_far = call(
        hidden_back_kernel,
        "hidden_back",
        [((local, width), f32), ((local, width), bf16), ((edge, width), bf16)],
        [sc, grad_projected, qkv_full, base],
        flops=3 * MICROSECOND,
        limit=20,
    )
    state_sib = lax.ppermute(state_sib, "head", CORE)
    if ringed:
        qkv_leave, qkv_stay = qkv_fold(sc, after(qkv_stay, state_own), qkv_far)
        qkv_far = send(qkv_leave, qkv_hops[2])
        leave, stay, sums = fold(3, sc, stay, after(sum_arrived, qkv_leave), sums, width)
        sum_arrived = send(leave, sum_hops[0])
        unit = qkv_leave.shape[1:]
        here, *away = call(
            qkv_spread_kernel,
            "qkv_spread",
            [(unit, f32)] + [(unit, bf16)] * 3,
            [sc, after(qkv_stay, stay), qkv_far],
            limit=16,
        )
        away = [send(a, (bit, bit)) for a, bit in zip(away, (Z1, Z0, Z0 | Z1))]
        sum_arrived, *away = lax.optimization_barrier((sum_arrived, *away))
        grad_qkv_weight = add(here, away[0]) + add(away[1], away[2])
    state_here = lax.ppermute(state_far, "head", ACROSS)
    quarter = hidden // 4
    if ringed:
        grad_out, grad_in, grad_back, bias_sum, *vectors = call(
            last_fold_kernel,
            "last_fold",
            [
                ((UNIT, LANES), f32),
                ((UNIT, quarter), f32),
                ((UNIT, quarter), f32),
                ((1, hidden), f32),
                *[((1, width), f32)] * 6,
                ((1, 1), f32),
            ],
            [sc, stay, sum_arrived, sums],
            limit=16,
        )
        bias_sum, *vectors = [v.reshape(-1) for v in (bias_sum, *vectors)]
    else:
        grad_qkv_weight, rest_grad, small = scatter_whole(
            [qkv_stay, qkv_leave], sum_own, sum_sib, width, x
        )
        grad_out = rest_grad[:, :LANES]
        grad_in = rest_grad[:, LANES : LANES + quarter]
        grad_back = rest_grad[:, LANES + quarter :]
        bias_sum = small[8 : 8 + hidden // width].reshape(hidden)
        vectors = [*[small[k] for k in range(6)], small[6, 0:1]]

    state_core = lax.ppermute(state_here, "head", CORE)
    (grad_state,) = call(
        finish_kernel,
        "finish",
        [((local, width), f32)],
        [sc, state_own, state_sib, state_here, state_core],
        limit=16,
    )
    return (
        new_state,
        grad_state,
        grad_qkv_weight,
        grad_out,
        grad_in,
        grad_back,
        bias_sum,
        *vectors,
    )


def unit_owners(orders):
    tables = []
    for order in orders:
        numbers = [
            sum(bit for place, bit in enumerate(order) if (unit >> place) & 1)
            for unit in range(16)
        ]
        tables.append([(number >> 2, (number >> 1) & 1) for number in numbers])
    return tables


def gather_whole(qkv_weight, rest, x, c):
    def both(array, axis):
        whole = lax.all_gather(array, "dp", axis=axis, tiled=True)
        other = lax.ppermute(whole, "head", ACROSS)
        return jnp.stack([whole, other])

    qkv, rest = both(qkv_weight, 1), both(rest, 0)
    width = rest.shape[1]
    qkv = qkv.reshape(2, 3, width // UNIT, UNIT, LANES)
    rest = rest.reshape(2, width // UNIT, UNIT, rest.shape[2])

    def units(array, orders):
        return jnp.where(
            c == 0, *(jnp.stack([array[ox, od] for od, ox in t]) for t in unit_owners(orders))
        )

    qkv = units(jnp.swapaxes(qkv, 1, 2), QKV_ORDERS)
    return [qkv[:8], qkv[8:]], units(rest, ORDERS)


def scatter_whole(qkv_sums, sum_own, sum_sib, width, x):
    c = lax.axis_index("head") % 2
    rows = 16 * UNIT
    rest = add(sum_own, lax.ppermute(sum_sib, "head", CORE))
    tail = rest[rows:]
    small = lax.psum(tail[:, :width] + tail[:, width : 2 * width], ("dp", "head")) * 0.5
    rest = rest[:rows].reshape(16, UNIT, rest.shape[1])
    qkv = jnp.concatenate(qkv_sums, axis=0).astype(f32)

    def order(orders, array):
        whole = []
        for table in unit_owners(orders):
            back = {owner_of: unit for unit, owner_of in enumerate(table)}
            whole.append(
                [jnp.stack([array[back[od, ox]] for od in range(8)]) for ox in range(2)]
            )
        return [jnp.where(c == 0, *pair) for pair in zip(*whole)]

    rest = [r.reshape(width, r.shape[2]) for r in order(SUM_ORDERS, rest)]
    qkv = [
        jnp.swapaxes(q, 0, 1).reshape(3, width, LANES) for q in order(QKV_ORDERS, qkv)
    ]
    rest = rest[0] + lax.ppermute(rest[1], "head", ACROSS)
    qkv = qkv[0] + lax.ppermute(qkv[1], "head", ACROSS)
    return (
        lax.psum_scatter(qkv, "dp", scatter_dimension=1, tiled=True),
        lax.psum_scatter(rest, "dp", scatter_dimension=0, tiled=True),
        small,
    )


def solution(mesh):
    tokens = P(("dp", "head"), None)
    weights = P("dp", "head")
    return jax.shard_map(
        body,
        mesh=mesh,
        in_specs=(
            tokens,
            P(None, "dp", "head"),
            weights,
            weights,
            weights,
            P(),
            P(),
            P(),
            P(),
            P(),
            P(),
            P(),
            P(),
            P("dp", None),
            P(("dp", "head")),
            tokens,
        ),
        out_specs=(
            tokens,
            tokens,
            P(None, "dp", "head"),
            weights,
            weights,
            weights,
            P(),
            P(),
            P(),
            P(),
            P(),
            P(),
            P(),
            P(),
        ),
        check_vma=False,
    )
```
